128 devices in a mesh: head: 2 (over core), inner: 8 (over y_hi, z), outer: 8 (over y_lo, x).
Axes of the slice: x: 4, y: 4 (y_hi: 2, y_lo: 2; y = y_hi * 2 + y_lo), z: 4, core: 2. Of those that a mesh axis runs over, the one named last changes fastest.
Arguments:
- query_vectors: bfloat16 [8192, 2048], P(('inner', 'outer'), 'head'), may hold values from -5 to 5
- window_keys: bfloat16 [16384, 256], P(('head', 'inner', 'outer')), may hold values from -6 to 6
- window_values: bfloat16 [16384, 256], P(('head', 'inner', 'outer')), may hold values from -6 to 6
- attention_output: bfloat16 [8192, 2048], P(('inner', 'outer'), 'head'), may hold values from -4 to 4
- output_gradient: bfloat16 [8192, 2048], P(('inner', 'outer'), 'head'), may hold values from -96 to 96
- query_blocks: int32 [64], replicated, may hold values from 0 to 63, as said below
- key_blocks: int32 [128], replicated, may hold values from 0 to 127, as said below
- kept_blocks: int32 [64, 64], replicated, may hold values from -1 to 127, as said below
Outputs:
- query_gradient: bfloat16 [8192, 2048], P(('inner', 'outer'), 'head')
- key_gradient: bfloat16 [16384, 256], P(('head', 'inner', 'outer'))
- value_gradient: bfloat16 [16384, 256], P(('head', 'inner', 'outer'))
The draws below stay inside these ranges and needn't reach their ends.
Inputs may be any that keep to these rules, and one draw needn't show every extreme that they name: `query_blocks`: stored query blocks 2m and 2m + 1 hold slab positions p and 63 - p; every position once. `key_blocks`: stored key blocks 2m and 2m + 1 hold window positions p and 127 - p; every position once. `kept_blocks`: row b holds distinct key block positions, none above 64 + b and always that one; unused entries are -1 and come after the used ones.
All inputs are finite; a program needn't handle non-finite values.
Results may differ from the reference program's by a relative error of at most 0.0049.
Values may be sent and summed in bfloat16 or wider, within the bound.
A program may use at most 64 MiB of HBM per device.

```python
import math
import jax
import jax.numpy as jnp
from jax import lax

HEAD_SIZE = 128
GROUP_HEADS = 8
KEY_VALUE_HEADS = 2
QUERY_HEADS = 16
BLOCK_TOKENS = 128
QUERY_TOKENS = 8192
KEY_TOKENS = 16384
QUERY_BLOCKS = 64
KEY_BLOCKS = 128
LIST_ENTRIES = 64


def mirrored_pairs(key, total_blocks):
    pair_order = jax.random.permutation(key, total_blocks // 2).astype(jnp.int32)
    slot_ids = jnp.arange(total_blocks, dtype=jnp.int32)
    paired = pair_order[slot_ids // 2]
    return jnp.where(slot_ids % 2 == 0, paired, total_blocks - 1 - paired).astype(jnp.int32)


def block_orders(key):
    return (mirrored_pairs(jax.random.fold_in(key, 11), QUERY_BLOCKS), mirrored_pairs(jax.random.fold_in(key, 12), KEY_BLOCKS))


def draw_query_blocks(key, part):
    return block_orders(key)[0]


def draw_key_blocks(key, part):
    return block_orders(key)[1]


def draw_kept_blocks(key, part):
    key = jax.random.fold_in(key, 5)
    key_rank, key_light, key_heavy, key_pick = jax.random.split(key, 4)
    positions = jnp.arange(QUERY_BLOCKS, dtype=jnp.int32)[:, None]
    candidates = jnp.arange(KEY_BLOCKS, dtype=jnp.int32)[None, :]
    diagonal = KEY_BLOCKS - QUERY_BLOCKS + positions
    ranking = jax.random.randint(key_rank, (QUERY_BLOCKS, KEY_BLOCKS), 0, 2 ** 16, dtype=jnp.int32) * KEY_BLOCKS + candidates
    ranking = jnp.where(candidates == diagonal, 2 ** 30, jnp.where(candidates < diagonal, ranking, -1))
    ranked_values, ranked_ids = lax.top_k(ranking, LIST_ENTRIES)
    light_counts = jax.random.randint(key_light, (QUERY_BLOCKS,), 1, max(LIST_ENTRIES // 8, 1) + 1, dtype=jnp.int32)
    heavy_counts = jax.random.randint(key_heavy, (QUERY_BLOCKS,), LIST_ENTRIES // 2, LIST_ENTRIES + 1, dtype=jnp.int32)
    heavy_rows = jax.random.randint(key_pick, (QUERY_BLOCKS,), 0, 8, dtype=jnp.int32) == 0
    counts = jnp.where(heavy_rows, heavy_counts, light_counts).at[0].set(LIST_ENTRIES)
    rank_ids = jnp.arange(LIST_ENTRIES, dtype=jnp.int32)[None, :]
    return jnp.where(rank_ids < counts[:, None], ranked_ids, -1).astype(jnp.int32)


def draw_query_vectors(key, part):
    self_key = jax.random.fold_in(key, 21)
    return jnp.clip(jax.random.normal(self_key, (QUERY_TOKENS, QUERY_HEADS * HEAD_SIZE), jnp.float32), -5.0, 5.0).astype(jnp.bfloat16)


def draw_window_keys(key, part):
    self_key = jax.random.fold_in(key, 22)
    return jnp.clip(jax.random.normal(self_key, (KEY_TOKENS, KEY_VALUE_HEADS * HEAD_SIZE), jnp.float32), -5.0, 5.0).astype(jnp.bfloat16)


def block_levels(own_key, shape, shards, least, high):
    def one(dim, shards_of):
        draws = jax.random.uniform(jax.random.fold_in(jax.random.fold_in(own_key, 6), dim), (shards_of,), jnp.float32, least / len(shards), high / len(shards))
        return jnp.repeat(jnp.exp(draws), shape[dim] // shards_of).reshape((-1,) + (1,) * (len(shape) - dim - 1))

    factor_of = one(*shards[0])
    for cut in shards[1:]:
        factor_of = factor_of * one(*cut)
    return factor_of


def centred(rng, shape, width, reach, cuts=(), kind=jnp.bfloat16):
    array = jax.random.normal(rng, shape, jnp.float32) * width
    if len(cuts) > 0:
        array = block_levels(rng, shape, cuts, -0.22, 0.18) * array
    return jnp.clip(array, min=-reach, max=reach).astype(kind)


def setup_inputs(seed: int = 0) -> dict:
    key_list = jax.random.split(jax.random.key(seed), 9)
    query_vectors = draw_query_vectors(jax.random.fold_in(key_list[8], 71), 0)
    window_keys = draw_window_keys(jax.random.fold_in(key_list[8], 71), 0)
    window_values = centred(key_list[2], (KEY_TOKENS, KEY_VALUE_HEADS * HEAD_SIZE), 1.0, 6.0, ((0, 128),))
    attention_output = centred(key_list[3], (QUERY_TOKENS, QUERY_HEADS * HEAD_SIZE), 0.25, 4.0, ((0, 64), (1, 2)))
    output_gradient = centred(key_list[4], (QUERY_TOKENS, QUERY_HEADS * HEAD_SIZE), 16.0, 96.0, ((0, 64), (1, 2)))
    query_blocks = draw_query_blocks(jax.random.fold_in(key_list[8], 71), 0)
    key_blocks = draw_key_blocks(jax.random.fold_in(key_list[8], 71), 0)
    kept_blocks = draw_kept_blocks(jax.random.fold_in(key_list[8], 71), 0)
    return {"query_vectors": query_vectors, "window_keys": window_keys, "window_values": window_values, "attention_output": attention_output, "output_gradient": output_gradient, "query_blocks": query_blocks, "key_blocks": key_blocks, "kept_blocks": kept_blocks}


NEG_FILL = -1e+30

def reference(query_vectors, window_keys, window_values, attention_output, output_gradient, query_blocks, key_blocks, kept_blocks):
    logit_scale = 1.0 / math.sqrt(HEAD_SIZE)
    first_key = KEY_BLOCKS - QUERY_BLOCKS
    inverse = jnp.zeros((KEY_BLOCKS,), jnp.int32).at[key_blocks].set(jnp.arange(KEY_BLOCKS, dtype=jnp.int32))
    key_pieces = window_keys.reshape(KEY_BLOCKS, BLOCK_TOKENS, KEY_VALUE_HEADS, HEAD_SIZE)
    value_pieces = window_values.reshape(KEY_BLOCKS, BLOCK_TOKENS, KEY_VALUE_HEADS, HEAD_SIZE)
    offsets = jnp.arange(BLOCK_TOKENS, dtype=jnp.int32)

    def per_block(carried, slot_id):
        key_gradient_total, value_gradient_total = carried
        row_offset = (slot_id * BLOCK_TOKENS).astype(jnp.int32)
        query_piece = lax.dynamic_slice_in_dim(query_vectors, row_offset, BLOCK_TOKENS, 0).reshape(BLOCK_TOKENS, KEY_VALUE_HEADS, GROUP_HEADS, HEAD_SIZE).astype(jnp.float32)
        gradient_piece = lax.dynamic_slice_in_dim(output_gradient, row_offset, BLOCK_TOKENS, 0).reshape(BLOCK_TOKENS, KEY_VALUE_HEADS, GROUP_HEADS, HEAD_SIZE).astype(jnp.float32)
        output_piece = lax.dynamic_slice_in_dim(attention_output, row_offset, BLOCK_TOKENS, 0).reshape(BLOCK_TOKENS, KEY_VALUE_HEADS, GROUP_HEADS, HEAD_SIZE).astype(jnp.float32)
        position = query_blocks[slot_id]
        listed = kept_blocks[position]
        present = listed >= 0
        key_pos = jnp.where(present, listed, 0).astype(jnp.int32)
        key_positions_list = inverse[key_pos]
        key_used_count = key_pieces[key_positions_list].reshape(LIST_ENTRIES * BLOCK_TOKENS, KEY_VALUE_HEADS, HEAD_SIZE).astype(jnp.float32)
        value_used_count = value_pieces[key_positions_list].reshape(LIST_ENTRIES * BLOCK_TOKENS, KEY_VALUE_HEADS, HEAD_SIZE).astype(jnp.float32)
        query_tok = (first_key + position) * BLOCK_TOKENS + offsets
        key_tok = (key_pos[:, None] * BLOCK_TOKENS + offsets[None, :]).reshape(-1)
        visible = jnp.repeat(present, BLOCK_TOKENS)[None, :] & (key_tok[None, :] <= query_tok[:, None])
        scores = jnp.einsum('qhgd,khd->hgqk', query_piece, key_used_count) * logit_scale
        row_max = lax.optimization_barrier(jnp.max(jnp.where(visible, scores, NEG_FILL), axis=3))
        row_total = lax.optimization_barrier(jnp.sum(jnp.exp(jnp.where(visible, scores - row_max[..., None], NEG_FILL)), axis=3))
        log_total = row_max + jnp.log(row_total)
        attn_probs = jnp.exp(jnp.where(visible, scores - log_total[..., None], NEG_FILL))
        probability_reduced = lax.optimization_barrier(attn_probs.astype(jnp.bfloat16)).astype(jnp.float32)
        row_delta = jnp.einsum('qhgd,qhgd->hgq', gradient_piece, output_piece)
        grad_probs = jnp.einsum('qhgd,khd->hgqk', gradient_piece, value_used_count)
        score_gradient = attn_probs * (grad_probs - row_delta[..., None])
        score_gradient = lax.optimization_barrier(score_gradient.astype(jnp.bfloat16)).astype(jnp.float32)
        query_gradient = jnp.einsum('hgqk,khd->qhgd', score_gradient, key_used_count) * logit_scale
        query_gradient = query_gradient.reshape(BLOCK_TOKENS, KEY_VALUE_HEADS * GROUP_HEADS * HEAD_SIZE).astype(jnp.bfloat16)
        key_gradient = (jnp.einsum('fsrw,rfsx->wfx', score_gradient, query_piece) * logit_scale).reshape(LIST_ENTRIES, BLOCK_TOKENS, KEY_VALUE_HEADS, HEAD_SIZE)
        value_gradient = jnp.einsum('fsrw,rfsx->wfx', probability_reduced, gradient_piece).reshape(LIST_ENTRIES, BLOCK_TOKENS, KEY_VALUE_HEADS, HEAD_SIZE)
        keep_rows = present[:, None, None, None]
        key_gradient_total = key_gradient_total.at[key_positions_list].add(jnp.where(keep_rows, key_gradient, 0.0))
        value_gradient_total = value_gradient_total.at[key_positions_list].add(jnp.where(keep_rows, value_gradient, 0.0))
        return ((key_gradient_total, value_gradient_total), query_gradient)
    empty_pieces = jnp.zeros((KEY_BLOCKS, BLOCK_TOKENS, KEY_VALUE_HEADS, HEAD_SIZE), jnp.float32)
    (key_gradient_total, value_gradient_total), gradient_rows = lax.scan(per_block, (empty_pieces, empty_pieces), jnp.arange(QUERY_BLOCKS, dtype=jnp.int32))
    query_gradient = gradient_rows.reshape(QUERY_TOKENS, KEY_VALUE_HEADS * GROUP_HEADS * HEAD_SIZE)
    key_gradient = key_gradient_total.reshape(KEY_TOKENS, KEY_VALUE_HEADS * HEAD_SIZE).astype(jnp.bfloat16)
    value_gradient = value_gradient_total.reshape(KEY_TOKENS, KEY_VALUE_HEADS * HEAD_SIZE).astype(jnp.bfloat16)
    return (query_gradient, key_gradient, value_gradient)
```

```python
import math

import jax
import jax.numpy as jnp
from jax import lax
from jax.experimental import pallas as pl
from jax.experimental.pallas import tpu as pltpu
from jax.sharding import PartitionSpec as P

HEADS = 8
D = 128
B = 128
RING = 4
LOCAL_KEYS = 32
ENTRIES = 64
FIRST_KEY = 64
SCALE = 1.0 / math.sqrt(D)
LOG2E = math.log2(math.e)
C2 = SCALE * LOG2E
NEG = -1e30
MASKED = -2e30
MESH = pl.DeviceIdType.MESH
ANY = pl.BlockSpec(memory_space=pl.ANY)
VMEM = pl.BlockSpec(memory_space=pltpu.VMEM)
SMEM = pl.BlockSpec(memory_space=pltpu.SMEM)
BF = jnp.bfloat16
F32 = jnp.float32


class Place:
    def __init__(self):
        self.h = lax.axis_index("head")
        inner, outer = lax.axis_index("inner"), lax.axis_index("outer")
        self.x, self.z = lax.rem(outer, 4), lax.rem(inner, 4)
        self.y = (inner // 4) * 2 + outer // 4

    def device(self, x=None, y=None, z=None, h=None):
        x, y, z, h = (
            own if new is None else new
            for own, new in ((self.x, x), (self.y, y), (self.z, z), (self.h, h))
        )
        return (h, (y // 2) * 4 + z, lax.rem(y, 2) * 4 + x)

    def along(self, axis, step):
        at = lax.rem(getattr(self, axis) + step + RING, RING)
        return self.device(**{axis: at})

    def partner(self):
        return self.device(h=1 - self.h)


def ring_at(me, step):
    return lax.rem(me + step + RING, RING)


def greet(devices):
    barrier = pltpu.get_barrier_semaphore()
    for device in devices:
        pl.semaphore_signal(barrier, inc=1, device_id=device, device_id_type=MESH)
    pl.semaphore_wait(barrier, len(devices))


class Gather:
    def __init__(self, place, axis, part, own, send, recv):
        self.me = getattr(place, axis)
        self.to = (place.along(axis, 1), place.along(axis, -1))
        self.part, self.own, self.send, self.recv = part, own, send, recv

    def copy(self, src, dst, way, k):
        return pltpu.make_async_remote_copy(
            src_ref=src,
            dst_ref=dst,
            send_sem=self.send.at[way * 3 + k],
            recv_sem=self.recv.at[way * 3 + k],
            device_id=self.to[way],
            device_id_type=MESH,
        )

    def start(self):
        for k in range(2):
            for way in range(2):
                for src, dst in self.own(k ^ way):
                    self.copy(src, dst, way, k).start()

    def whole(self, at, half, way, k):
        ref = self.part(at, half)
        return self.copy(ref, ref, way, k)

    def arrived(self, way, k):
        step = (-1 if way == 0 else 1) * (2 if k == 2 else 1)
        half = way if k == 2 else k ^ way
        self.whole(ring_at(self.me, step), half, way, k).wait_recv()

    def forward(self):
        for way in range(2):
            self.arrived(way, 0)
            step = -1 if way == 0 else 1
            self.whole(ring_at(self.me, step), way, way, 2).start()

    def finish(self):
        for way in range(2):
            self.arrived(way, 1)
        for way in range(2):
            self.arrived(way, 2)

    def sent(self):
        for way in range(2):
            for k in range(3):
                self.whole(self.me, k ^ way if k < 2 else way, way, k).wait_send()


def gather_kernel(
    q_ref, g_ref, k_ref, v_ref, qd_ref, kv_ref, local, swap_send, swap_recv, zs, zr, cs, cr
):
    place = Place()
    h, x, y, z = place.h, place.x, place.y, place.z
    greet(
        [place.along(a, s) for a in ("x", "y", "z") for s in (1, -1)] + [place.partner()]
    )
    partner = place.partner()
    theirs = pl.ds(pl.multiple_of((1 - h) * D, D), D)
    ours = pl.ds(pl.multiple_of(h * D, D), D)

    def swaps():
        return [
            pltpu.make_async_remote_copy(
                src_ref=source.at[:, theirs],
                dst_ref=kv_ref.at[1, x, y, n],
                send_sem=swap_send.at[n],
                recv_sem=swap_recv.at[n],
                device_id=partner,
                device_id_type=MESH,
            )
            for n, source in enumerate((k_ref, v_ref))
        ]

    for copy in swaps():
        copy.start()

    def own_qd(half):
        source = (q_ref, g_ref)[half]
        return [
            (source.at[:, a * D : (a + 1) * D], qd_ref.at[z, half, a]) for a in range(HEADS)
        ]

    gz = Gather(place, "z", lambda at, half: qd_ref.at[at, half], own_qd, zs, zr)
    gz.start()
    gx0 = Gather(
        place,
        "x",
        lambda at, half: kv_ref.at[0, y, at, half],
        lambda half: [((k_ref, v_ref)[half].at[:, ours], kv_ref.at[0, y, x, half])],
        cs.at[0],
        cr.at[0],
    )
    gx0.start()

    def own_copies():
        for n, source in enumerate((k_ref, v_ref)):
            yield pltpu.make_async_copy(source.at[:, ours], kv_ref.at[0, y, x, n], local.at[n])
        for half in range(2):
            for n, (src, dst) in enumerate(own_qd(half)):
                yield pltpu.make_async_copy(src, dst, local.at[2 + half * HEADS + n])

    own = list(own_copies())
    for copy in own:
        copy.start()

    def slab(n, line):
        return (
            lambda at, half: kv_ref.at[n, at, 2 * half : 2 * half + 2],
            lambda half: [
                (kv_ref.at[n, line, 2 * half : 2 * half + 2],) * 2
            ],
        )

    for copy in swaps():
        copy.wait_recv()
    gy1 = Gather(
        place,
        "y",
        lambda at, half: kv_ref.at[1, x, at, half],
        lambda half: [(kv_ref.at[1, x, y, half],) * 2],
        cs.at[1],
        cr.at[1],
    )
    gy1.start()
    gx0.forward()
    gy1.forward()
    gx0.finish()
    own[0].wait()
    own[1].wait()
    gy0 = Gather(place, "y", *slab(0, y), cs.at[2], cr.at[2])
    gy0.start()
    gy1.finish()
    gx1 = Gather(place, "x", *slab(1, x), cs.at[3], cr.at[3])
    gx1.start()
    gz.forward()
    gy0.forward()
    gx1.forward()
    gy0.finish()
    gx1.finish()
    gz.finish()
    for copy in own[2:]:
        copy.wait()
    for copy in swaps():
        copy.wait_send()
    for ring in (gz, gx0, gy1, gy0, gx1):
        ring.sent()


def gather(q, g, k, v):
    return pl.pallas_call(
        gather_kernel,
        out_shape=(
            jax.ShapeDtypeStruct((RING, 2, HEADS, B, D), BF),
            jax.ShapeDtypeStruct((2, RING, RING, 2, B, D), BF),
        ),
        in_specs=[ANY] * 4,
        out_specs=(ANY, ANY),
        scratch_shapes=[
            pltpu.SemaphoreType.DMA((2 + 2 * HEADS,)),
            pltpu.SemaphoreType.DMA((2,)),
            pltpu.SemaphoreType.DMA((2,)),
            pltpu.SemaphoreType.DMA((6,)),
            pltpu.SemaphoreType.DMA((6,)),
            pltpu.SemaphoreType.DMA((4, 6)),
            pltpu.SemaphoreType.DMA((4, 6)),
        ],
        compiler_params=pltpu.CompilerParams(collective_id=0, has_side_effects=True),
        name="gather",
    )(q, g, k, v)


def across(a, b):
    return lax.dot_general(a, b, (((1,), (1,)), ((), ())), preferred_element_type=F32)


def pick(list_ref, i, n):
    first = list_ref[i, 2 * n]
    second = list_ref[i, 2 * n + 1]
    return [(lax.rem(e, 64), (e // 64) * B - B) for e in (first, second)]


def allowed_of(gap, past):
    return gap <= past


def stats_kernel(
    qb_ref, kb_ref, kept_ref, qd_hbm, kv_hbm, o_hbm, st_ref, delta_ref, list_ref,
    q_vmem, k_vmem, g_vmem, o_vmem, m_ref, l_ref, place_ref, sems,
):
    place = Place()
    z = place.z
    loads = [
        pltpu.make_async_copy(qd_hbm.at[:, 0], q_vmem, sems.at[0]),
        pltpu.make_async_copy(kv_hbm.at[:, 0], k_vmem, sems.at[1]),
        pltpu.make_async_copy(qd_hbm.at[z, 1], g_vmem, sems.at[2]),
        pltpu.make_async_copy(o_hbm, o_vmem, sems.at[3]),
    ]
    for load in loads:
        load.start()

    def clear(n, _):
        place_ref[n] = -1
        return 0

    lax.fori_loop(0, 128, clear, 0, unroll=16)

    def enter(j, _):
        first, a, b = j // 16, lax.rem(j // 4, 4), lax.rem(j, 4)
        own = first == 0
        yy, xx = jnp.where(own, a, b), jnp.where(own, b, a)
        owner = jnp.where(own, place.h, 1 - place.h)
        slot = owner * 64 + (yy // 2) * 32 + z * 8 + lax.rem(yy, 2) * 4 + xx
        place_ref[kb_ref[slot]] = j
        return 0

    lax.fori_loop(0, LOCAL_KEYS, enter, 0, unroll=4)
    for i in range(RING):
        slot = (place.y // 2) * 32 + i * 8 + lax.rem(place.y, 2) * 4 + place.x
        position = qb_ref[slot]

        def more(state):
            e, _ = state
            return jnp.logical_and(e < ENTRIES, kept_ref[position, jnp.minimum(e, ENTRIES - 1)] >= 0)

        def step(state):
            e, count = state
            block = kept_ref[position, e]
            j = place_ref[block]
            list_ref[i, count] = j + jnp.where(block == FIRST_KEY + position, 64, 128)
            return e + 1, count + (j >= 0).astype(jnp.int32)

        _, count = lax.while_loop(more, step, (jnp.int32(0), jnp.int32(0)))
        list_ref[i, count] = 0
        list_ref[i, 34] = (count + 1) // 2

    for load in loads:
        load.wait()

    for a in range(HEADS):
        product = g_vmem[a].astype(F32) * o_vmem[:, a * D : (a + 1) * D].astype(F32)
        delta_ref[a : a + 1, :] = jnp.sum(jnp.transpose(product), axis=0, keepdims=True)

    gap = lax.broadcasted_iota(jnp.int32, (B, 2 * B), 0) - lax.rem(
        lax.broadcasted_iota(jnp.int32, (B, 2 * B), 1), B
    )
    m_ref[...] = jnp.full_like(m_ref, NEG)
    l_ref[...] = jnp.zeros_like(l_ref)
    for i in range(RING):

        def pair(n, _):
            (j0, past0), (j1, past1) = pick(list_ref, i, n)
            keys = jnp.concatenate([k_vmem[j0], k_vmem[j1]], axis=0)
            for c in range(HEADS // 2):
                queries = q_vmem[i, 2 * c : 2 * c + 2].reshape(2 * B, D)
                s = across(keys, queries)
                s = jnp.concatenate(
                    [
                        jnp.where(allowed_of(gap, past0), s[:B], MASKED),
                        jnp.where(allowed_of(gap, past1), s[B:], MASKED),
                    ],
                    axis=0,
                ).reshape(2 * B // 8, 8, 2 * B)
                old = m_ref[i, c]
                new = jnp.maximum(old, jnp.max(s, axis=0))
                m_ref[i, c] = new
                total = jnp.sum(jnp.exp2(s * C2 - (new * C2)[None]), axis=0)
                l_ref[i, c] = l_ref[i, c] * jnp.exp2((old - new) * C2) + total
            return 0

        lax.fori_loop(0, list_ref[i, 34], pair, 0)
    for i in range(RING):
        for c in range(HEADS // 2):
            m8 = m_ref[i, c]
            m = jnp.max(m8, axis=0, keepdims=True)
            l = jnp.sum(l_ref[i, c] * jnp.exp2((m8 - m) * C2), axis=0, keepdims=True)
            for t in range(2):
                row = pl.ds(2 * c + t, 1)
                st_ref[0, i, row, :] = m[:, t * B : (t + 1) * B]
                st_ref[1, i, row, :] = l[:, t * B : (t + 1) * B]


def statistics(qb, kb, kept, qd, kv, o):
    return pl.pallas_call(
        stats_kernel,
        out_shape=(
            jax.ShapeDtypeStruct((2, RING, HEADS, B), F32),
            jax.ShapeDtypeStruct((HEADS, B), F32),
            jax.ShapeDtypeStruct((RING, 40), jnp.int32),
        ),
        in_specs=[SMEM, SMEM, SMEM, ANY, ANY, ANY],
        out_specs=(VMEM, VMEM, SMEM),
        scratch_shapes=[
            pltpu.VMEM((RING, HEADS, B, D), BF),
            pltpu.VMEM((LOCAL_KEYS, B, D), BF),
            pltpu.VMEM((HEADS, B, D), BF),
            pltpu.VMEM((B, HEADS * D), BF),
            pltpu.VMEM((RING, HEADS // 2, 8, 2 * B), F32),
            pltpu.VMEM((RING, HEADS // 2, 8, 2 * B), F32),
            pltpu.SMEM((128,), jnp.int32),
            pltpu.SemaphoreType.DMA((4,)),
        ],
        compiler_params=pltpu.CompilerParams(vmem_limit_bytes=32 * 2**20),
        name="statistics",
    )(qb, kb, kept, qd, kv.reshape(LOCAL_KEYS, 2, B, D), o)


def exchange_kernel(st_ref, delta_ref, total_ref, all_delta_ref, sts, deltas, send, recv):
    place = Place()
    z = place.z
    greet([place.along("z", s) for s in (1, 2, 3)])

    def copies(step):
        to = place.along("z", step)
        for n, (src, dst) in enumerate(((st_ref, sts.at[step - 1]), (delta_ref, deltas.at[step - 1]))):
            yield pltpu.make_async_remote_copy(
                src_ref=src,
                dst_ref=dst,
                send_sem=send.at[step - 1, n],
                recv_sem=recv.at[step - 1, n],
                device_id=to,
                device_id_type=MESH,
            )

    for step in (2, 1, 3):
        for copy in copies(step):
            copy.start()
    for step in (1, 3, 2):
        for copy in copies(step):
            copy.wait()
    top = st_ref[0]
    for n in range(3):
        top = jnp.maximum(top, sts[n, 0])
    total = st_ref[1] * jnp.exp2((st_ref[0] - top) * C2)
    for n in range(3):
        total = total + sts[n, 1] * jnp.exp2((sts[n, 0] - top) * C2)
    total_ref[...] = top * C2 + jnp.log2(total)
    all_delta_ref[z] = delta_ref[...]
    for n in range(3):
        all_delta_ref[ring_at(z, -(n + 1))] = deltas[n]


def exchange(st, delta):
    return pl.pallas_call(
        exchange_kernel,
        out_shape=(
            jax.ShapeDtypeStruct((RING, HEADS, B), F32),
            jax.ShapeDtypeStruct((RING, HEADS, B), F32),
        ),
        in_specs=[VMEM, VMEM],
        out_specs=(VMEM, VMEM),
        scratch_shapes=[
            pltpu.VMEM((3, 2, RING, HEADS, B), F32),
            pltpu.VMEM((3, HEADS, B), F32),
            pltpu.SemaphoreType.DMA((3, 2)),
            pltpu.SemaphoreType.DMA((3, 2)),
        ],
        compiler_params=pltpu.CompilerParams(collective_id=1, has_side_effects=True),
        name="exchange",
    )(st, delta)


def grads_kernel(
    list_ref, qd_hbm, kv_hbm, total_ref, delta_ref, dq_ref, dkv_ref,
    qd_vmem, kv_vmem, dq_acc, dk_acc, dv_acc, sems,
):
    loads = [
        pltpu.make_async_copy(qd_hbm, qd_vmem, sems.at[0]),
        pltpu.make_async_copy(kv_hbm, kv_vmem, sems.at[1]),
    ]
    for load in loads:
        load.start()
    dk_acc[...] = jnp.zeros_like(dk_acc)
    dv_acc[...] = jnp.zeros_like(dv_acc)
    for load in loads:
        load.wait()
    gap = lax.broadcasted_iota(jnp.int32, (B, 2 * B), 0) - lax.rem(
        lax.broadcasted_iota(jnp.int32, (B, 2 * B), 1), B
    )
    for i in range(RING):
        dq_acc[...] = jnp.zeros_like(dq_acc)

        def pair(n, _):
            (j0, past0), (j1, past1) = pick(list_ref, i, n)
            keys = jnp.concatenate([kv_vmem[j0, 0], kv_vmem[j1, 0]], axis=0)
            values = jnp.concatenate([kv_vmem[j0, 1], kv_vmem[j1, 1]], axis=0)
            keys_t = jnp.transpose(keys)
            dk = jnp.zeros((2 * B, D), F32)
            dv = jnp.zeros((2 * B, D), F32)
            for c in range(HEADS // 2):
                queries = qd_vmem[i, 0, 2 * c : 2 * c + 2].reshape(2 * B, D)
                cotangents = qd_vmem[i, 1, 2 * c : 2 * c + 2].reshape(2 * B, D)
                total = jnp.concatenate(
                    [total_ref[i, 2 * c : 2 * c + 1, :], total_ref[i, 2 * c + 1 : 2 * c + 2, :]],
                    axis=1,
                )
                delta = jnp.concatenate(
                    [delta_ref[i, 2 * c : 2 * c + 1, :], delta_ref[i, 2 * c + 1 : 2 * c + 2, :]],
                    axis=1,
                )
                s = across(keys, queries)
                s = jnp.concatenate(
                    [
                        jnp.where(allowed_of(gap, past0), s[:B], MASKED),
                        jnp.where(allowed_of(gap, past1), s[B:], MASKED),
                    ],
                    axis=0,
                )
                p = jnp.exp2(s * C2 - total)
                ds = (p * (across(values, cotangents) - delta)).astype(BF)
                dv = dv + jnp.dot(p.astype(BF), cotangents, preferred_element_type=F32)
                dk = dk + jnp.dot(ds, queries, preferred_element_type=F32)
                cols = slice(2 * c * B, 2 * (c + 1) * B)
                dq_acc[:, cols] += jnp.dot(keys_t, ds, preferred_element_type=F32)
            dk_acc[j0] += dk[:B]
            dk_acc[j1] += dk[B:]
            dv_acc[j0] += dv[:B]
            dv_acc[j1] += dv[B:]
            return 0

        lax.fori_loop(0, list_ref[i, 34], pair, 0)
        dq_ref[i] = (dq_acc[...] * SCALE).astype(BF)
    for j in range(LOCAL_KEYS):
        dkv_ref[j, 0] = (dk_acc[j] * SCALE).astype(BF)
        dkv_ref[j, 1] = dv_acc[j].astype(BF)


def grads(lists, qd, kv, total, delta):
    return pl.pallas_call(
        grads_kernel,
        out_shape=(
            jax.ShapeDtypeStruct((RING, D, HEADS * B), BF),
            jax.ShapeDtypeStruct((LOCAL_KEYS, 2, B, D), BF),
        ),
        in_specs=[SMEM, ANY, ANY, VMEM, VMEM],
        out_specs=(VMEM, VMEM),
        scratch_shapes=[
            pltpu.VMEM((RING, 2, HEADS, B, D), BF),
            pltpu.VMEM((LOCAL_KEYS, 2, B, D), BF),
            pltpu.VMEM((D, HEADS * B), F32),
            pltpu.VMEM((LOCAL_KEYS, B, D), F32),
            pltpu.VMEM((LOCAL_KEYS, B, D), F32),
            pltpu.SemaphoreType.DMA((2,)),
        ],
        compiler_params=pltpu.CompilerParams(vmem_limit_bytes=48 * 2**20),
        name="grads",
    )(lists, qd, kv.reshape(LOCAL_KEYS, 2, B, D), total, delta)


class Scatter:
    def __init__(self, place, axis, part, near, far, mid, send, recv):
        self.me = getattr(place, axis)
        self.to = (place.along(axis, 1), place.along(axis, -1))
        self.part, self.near, self.far, self.mid = part, near, far, mid
        self.send, self.recv = send, recv

    def copy(self, src, dst, way, k):
        return pltpu.make_async_remote_copy(
            src_ref=src,
            dst_ref=dst,
            send_sem=self.send.at[way * 3 + k],
            recv_sem=self.recv.at[way * 3 + k],
            device_id=self.to[way],
            device_id_type=MESH,
        )

    def far_copy(self, way):
        return self.copy(self.part(ring_at(self.me, 2), way), self.far.at[way], way, 0)

    def plain_copy(self, way):
        step = 1 if way == 0 else -1
        return self.copy(self.part(ring_at(self.me, step), 1 - way), self.near(way, 1 - way), way, 1)

    def mid_copy(self, way):
        return self.copy(self.mid.at[way], self.near(way, way), way, 2)

    def start(self):
        for way in range(2):
            self.far_copy(way).start()
        for way in range(2):
            self.plain_copy(way).start()

    def forward(self):
        for way in range(2):
            step = 1 if way == 0 else -1
            self.far_copy(way).wait_recv()
            own = self.part(ring_at(self.me, step), way)[...].astype(F32)
            self.mid[way] = (self.far[way].astype(F32) + own).astype(BF)
            self.mid_copy(way).start()

    def finish(self):
        for way in range(2):
            self.plain_copy(way).wait_recv()
        for way in range(2):
            self.mid_copy(way).wait_recv()

    def half(self, half):
        total = self.part(self.me, half)[...].astype(F32)
        return total + self.near(0, half)[...].astype(F32) + self.near(1, half)[...].astype(F32)

    def sent(self):
        for way in range(2):
            self.far_copy(way).wait_send()
            self.plain_copy(way).wait_send()
            self.mid_copy(way).wait_send()


def scatter_kernel(
    dq_ref, dkv_ref, qg_ref, kg_ref, vg_ref,
    zn, zf, zm, n1, f1, m1, s1, n2, f2, m2, fin, qout, zs, zr, cs, cr, swap_send, swap_recv, local,
):
    place = Place()
    h, x, y, z = place.h, place.x, place.y, place.z
    greet(
        [place.along(a, s) for a in ("x", "y", "z") for s in (1, -1)] + [place.partner()]
    )
    width = HEADS * B // 2

    rz = Scatter(
        place,
        "z",
        lambda at, half: dq_ref.at[at, :, half * width : (half + 1) * width],
        lambda way, half: zn.at[way, half],
        zf, zm, zs, zr,
    )

    def first(n, axis):
        return Scatter(
            place,
            axis,
            lambda at, half: dkv_ref.at[n, at, 2 * half : 2 * half + 2],
            lambda way, half: n1.at[n, way, half],
            f1.at[n], m1.at[n], cs.at[n], cr.at[n],
        )

    def second(n, axis):
        return Scatter(
            place,
            axis,
            lambda at, half: s1.at[n, at, half],
            lambda way, half: n2.at[n, way, half],
            f2.at[n], m2.at[n], cs.at[2 + n], cr.at[2 + n],
        )

    ry0, rx1 = first(0, "y"), first(1, "x")
    rx0, ry1 = second(0, "x"), second(1, "y")
    ry0.start()
    rx1.start()
    rz.start()
    ry0.forward()
    rx1.forward()
    rz.forward()
    for n, (one, two) in enumerate(((ry0, rx0), (rx1, ry1))):
        one.finish()
        for half in range(2):
            s1[n, 2 * half : 2 * half + 2] = one.half(half).astype(BF)
        two.start()
    rx0.forward()
    ry1.forward()
    rz.finish()
    for half in range(2):
        total = rz.half(half)
        for a in range(HEADS // 2):
            head = half * (HEADS // 2) + a
            qout[:, head * D : (head + 1) * D] = jnp.transpose(
                total[:, a * B : (a + 1) * B]
            ).astype(BF)
    q_copy = pltpu.make_async_copy(qout, qg_ref, local.at[0])
    q_copy.start()
    ours = pl.ds(pl.multiple_of(h * D, D), D)
    ry1.finish()
    for half in range(2):
        fin[1, half] = ry1.half(half).astype(BF)
    swaps = [
        pltpu.make_async_remote_copy(
            src_ref=fin.at[1, n],
            dst_ref=target.at[:, ours],
            send_sem=swap_send.at[n],
            recv_sem=swap_recv.at[n],
            device_id=place.partner(),
            device_id_type=MESH,
        )
        for n, target in enumerate((kg_ref, vg_ref))
    ]
    for copy in swaps:
        copy.start()
    rx0.finish()
    for half in range(2):
        fin[0, half] = rx0.half(half).astype(BF)
    outs = [
        pltpu.make_async_copy(fin.at[0, n], target.at[:, ours], local.at[1 + n])
        for n, target in enumerate((kg_ref, vg_ref))
    ]
    for copy in outs:
        copy.start()
    for copy in outs:
        copy.wait()
    q_copy.wait()
    for copy in swaps:
        copy.wait()
    for ring in (rz, ry0, rx1, rx0, ry1):
        ring.sent()


def scatter(dq, dkv):
    half_block = (2, 2, B, D)
    return pl.pallas_call(
        scatter_kernel,
        out_shape=(
            jax.ShapeDtypeStruct((B, HEADS * D), BF),
            jax.ShapeDtypeStruct((B, 2 * D), BF),
            jax.ShapeDtypeStruct((B, 2 * D), BF),
        ),
        in_specs=[VMEM, VMEM],
        out_specs=(ANY, ANY, ANY),
        scratch_shapes=[
            pltpu.VMEM((2, 2, D, HEADS * B // 2), BF),
            pltpu.VMEM((2, D, HEADS * B // 2), BF),
            pltpu.VMEM((2, D, HEADS * B // 2), BF),
            pltpu.VMEM((2, 2, 2) + half_block, BF),
            pltpu.VMEM((2, 2) + half_block, BF),
            pltpu.VMEM((2, 2) + half_block, BF),
            pltpu.VMEM((2, RING, 2, B, D), BF),
            pltpu.VMEM((2, 2, 2, B, D), BF),
            pltpu.VMEM((2, 2, B, D), BF),
            pltpu.VMEM((2, 2, B, D), BF),
            pltpu.VMEM((2, 2, B, D), BF),
            pltpu.VMEM((B, HEADS * D), BF),
            pltpu.SemaphoreType.DMA((6,)),
            pltpu.SemaphoreType.DMA((6,)),
            pltpu.SemaphoreType.DMA((4, 6)),
            pltpu.SemaphoreType.DMA((4, 6)),
            pltpu.SemaphoreType.DMA((2,)),
            pltpu.SemaphoreType.DMA((2,)),
            pltpu.SemaphoreType.DMA((3,)),
        ],
        compiler_params=pltpu.CompilerParams(
            collective_id=2, has_side_effects=True, vmem_limit_bytes=32 * 2**20
        ),
        name="scatter",
    )(dq, dkv.reshape(2, RING, RING, 2, B, D))


def body(q, k, v, o, g, query_blocks, key_blocks, kept_blocks):
    qd, kv = gather(q, g, k, v)
    st, delta, lists = statistics(query_blocks, key_blocks, kept_blocks, qd, kv, o)
    total, all_delta = exchange(st, delta)
    dq, dkv = grads(lists, qd, kv, total, all_delta)
    return scatter(dq, dkv)


def solution(mesh):
    rows, stored = P(("inner", "outer"), "head"), P(("head", "inner", "outer"), None)
    return jax.shard_map(
        body,
        mesh=mesh,
        in_specs=(rows, stored, stored, rows, rows, P(), P(), P()),
        out_specs=(rows, stored, stored),
        check_vma=False,
    )
```

```python
import math

import jax
import jax.numpy as jnp
from jax import lax
from jax.experimental import pallas as pl
from jax.experimental.pallas import tpu as pltpu
from jax.sharding import PartitionSpec as P

HEADS = 8
D = 128
B = 128
RING = 4
QUARTERS = 4
PART = 2
COLS = PART * B
LOCAL_ROWS = 16
LOCAL_KEYS = 32
ENTRIES = 64
GROUP = 8
TASKS = 272
FIRST_KEY = 64
SCALE = 1.0 / math.sqrt(D)
LOG2E = math.log2(math.e)
C2 = SCALE * LOG2E
NEG = -1e30
MASKED = -2e30
MESH = pl.DeviceIdType.MESH
ANY = pl.BlockSpec(memory_space=pl.ANY)
HBM = pl.BlockSpec(memory_space=pltpu.HBM)
VMEM = pl.BlockSpec(memory_space=pltpu.VMEM)
SMEM = pl.BlockSpec(memory_space=pltpu.SMEM)
BF = jnp.bfloat16
F32 = jnp.float32


class Place:
    def __init__(self):
        self.h = lax.axis_index("head")
        inner, outer = lax.axis_index("inner"), lax.axis_index("outer")
        self.x, self.z = lax.rem(outer, 4), lax.rem(inner, 4)
        self.y = (inner // 4) * 2 + outer // 4

    def device(self, x=None, y=None, z=None, h=None):
        x, y, z, h = (
            own if new is None else new
            for own, new in ((self.x, x), (self.y, y), (self.z, z), (self.h, h))
        )
        return (h, (y // 2) * 4 + z, lax.rem(y, 2) * 4 + x)

    def along(self, axis, step):
        at = lax.rem(getattr(self, axis) + step + RING, RING)
        return self.device(**{axis: at})

    def partner(self):
        return self.device(h=1 - self.h)

    def quarter(self, r):
        b, a = lax.rem(self.y, 2), lax.rem(self.x, 2)
        b, a = (1 - b if r & 2 else b), (1 - a if r & 1 else a)
        return 2 * b + a

    def square(self, r):
        b, a = lax.rem(self.y, 2), lax.rem(self.x, 2)
        y = self.y + 1 - 2 * b if r & 2 else self.y
        x = self.x + 1 - 2 * a if r & 1 else self.x
        return self.device(x=x, y=y)

    def around(self):
        near = [self.along(a, s) for a in ("x", "y", "z") for s in (1, -1)]
        return near + [self.partner(), self.square(3)]


def ring_at(me, step):
    return lax.rem(me + step + RING, RING)


def greet(devices):
    barrier = pltpu.get_barrier_semaphore()
    for device in devices:
        pl.semaphore_signal(barrier, inc=1, device_id=device, device_id_type=MESH)
    pl.semaphore_wait(barrier, len(devices))


class Gather:
    def __init__(self, place, axis, part, own, six, send, recv):
        self.me = getattr(place, axis)
        self.to = (place.along(axis, 1), place.along(axis, -1))
        self.part, self.own, self.six, self.send, self.recv = part, own, six, send, recv

    def copy(self, src, dst, way, k):
        return pltpu.make_async_remote_copy(
            src_ref=src,
            dst_ref=dst,
            send_sem=self.send,
            recv_sem=self.recv.at[way * 3 + k],
            device_id=self.to[way],
            device_id_type=MESH,
        )

    def start(self):
        for k in range(2):
            for way in range(2):
                for src, dst in self.own(k ^ way):
                    self.copy(src, dst, way, k).start()

    def whole(self, at, half, way, k):
        ref = self.part(at, half)
        return self.copy(ref, ref, way, k)

    def arrived(self, way, k):
        step = (-1 if way == 0 else 1) * (2 if k == 2 else 1)
        half = way if k == 2 else k ^ way
        self.whole(ring_at(self.me, step), half, way, k).wait_recv()

    def forward(self):
        for way in range(2):
            self.arrived(way, 0)
            step = -1 if way == 0 else 1
            self.whole(ring_at(self.me, step), way, way, 2).start()

    def finish(self):
        for way in range(2):
            self.arrived(way, 1)
        for way in range(2):
            self.arrived(way, 2)

    def sent(self):
        self.copy(self.six, self.six, 0, 0).wait_send()


def key_slot(place, j):
    n, a, b = j // 16, lax.rem(j // 4, 4), lax.rem(j, 4)
    owner = jnp.where(n == 0, place.h, 1 - place.h)
    yy, xx = jnp.where(n == 0, a, b), jnp.where(n == 0, b, a)
    return owner * 64 + (yy // 2) * 32 + place.z * 8 + lax.rem(yy, 2) * 4 + xx


def row_slot(place, i):
    zz, b, a = i // 4, lax.rem(i // 2, 2), lax.rem(i, 2)
    return (place.y // 2) * 32 + zz * 8 + b * 4 + (place.x // 2) * 2 + a


def tile_lists(place, qb_ref, kb_ref, kept):
    lanes = lax.broadcasted_iota(jnp.int32, (1, 128), 1)
    subs = lax.broadcasted_iota(jnp.int32, (LOCAL_ROWS, 1), 0)

    def key_step(j, row):
        return jnp.where(lanes == j, kb_ref[key_slot(place, j)], row)

    def row_step(i, column):
        return jnp.where(subs == i, qb_ref[row_slot(place, i)], column)

    key_pos = lax.fori_loop(0, LOCAL_KEYS, key_step, jnp.full((1, 128), -7, jnp.int32))
    row_pos = lax.fori_loop(0, LOCAL_ROWS, row_step, jnp.zeros((LOCAL_ROWS, 1), jnp.int32))
    wide = lax.broadcasted_iota(jnp.int32, (64, 128), 1)
    listed = jnp.zeros((64, 128), F32)
    for e in range(ENTRIES):
        listed = jnp.where(kept[:, e : e + 1] == wide, 1.0, listed)
    rows_of = (row_pos == lax.broadcasted_iota(jnp.int32, (LOCAL_ROWS, 64), 1)).astype(F32)
    keys_of = (key_pos == lax.broadcasted_iota(jnp.int32, (128, 128), 0)).astype(F32)
    mine = jnp.dot(
        jnp.dot(rows_of.astype(BF), listed.astype(BF), preferred_element_type=F32).astype(BF),
        keys_of.astype(BF),
        preferred_element_type=F32,
    )
    lane16 = lax.broadcasted_iota(jnp.int32, (LOCAL_ROWS, 128), 1)
    weight = lax.shift_left(jnp.ones_like(lane16), lax.rem(lane16, 16)).astype(F32)
    low = jnp.sum(jnp.where(lane16 < 16, mine * weight, 0.0), axis=1, keepdims=True)
    high = jnp.sum(
        jnp.where((lane16 >= 16) & (lane16 < 32), mine * weight, 0.0), axis=1, keepdims=True
    )
    bits = low.astype(jnp.int32) + lax.shift_left(
        high.astype(jnp.int32), jnp.full((LOCAL_ROWS, 1), 16, jnp.int32)
    )
    on = (key_pos == row_pos + FIRST_KEY).astype(F32)
    diagonal = jnp.sum(on * (lane16 - 99).astype(F32), axis=1, keepdims=True) + 99.0
    return jnp.where(lane16 == 0, bits, diagonal.astype(jnp.int32))


def gather_kernel(
    qb_hbm, kb_hbm, kept_hbm, q_ref, k_ref, v_ref, o_ref, g_ref,
    rows_out, keys_out, delta_ref, meta_ref,
    qb, kb, kept, o_vmem, g_vmem, parts,
    load, local, swap_send, swap_recv, s_send, s_recv, d_send, d_recv, zs, zr, cs, cr,
):
    place = Place()
    h, x, y, z = place.h, place.x, place.y, place.z
    pairs = ((o_ref, o_vmem), (g_ref, g_vmem), (kept_hbm, kept), (qb_hbm, qb), (kb_hbm, kb))
    loads = [pltpu.make_async_copy(src, dst, load.at[n]) for n, (src, dst) in enumerate(pairs)]
    for copy in loads:
        copy.start()
    greet(place.around())
    ours = pl.ds(pl.multiple_of(h * D, D), D)
    theirs = pl.ds(pl.multiple_of((1 - h) * D, D), D)

    swaps = [
        pltpu.make_async_remote_copy(
            src_ref=source.at[:, theirs],
            dst_ref=keys_out.at[1, x, y, n],
            send_sem=swap_send.at[n],
            recv_sem=swap_recv.at[n],
            device_id=place.partner(),
            device_id_type=MESH,
        )
        for n, source in enumerate((k_ref, v_ref))
    ]
    for copy in swaps:
        copy.start()

    def head(half, quarter, k):
        source = (q_ref, g_ref)[half]
        return source.at[:, pl.ds(pl.multiple_of((quarter * PART + k) * D, D), D)]

    def rows_copies(half):
        mine = place.quarter(0)
        return [(head(half, mine, k), rows_out.at[z, mine, half, k]) for k in range(PART)]

    def row_ring(r):
        part = lambda at, half: rows_out.at[at, place.quarter(r), half]
        own = rows_copies if r == 0 else lambda half: [(part(z, half),) * 2]
        return Gather(place, "z", part, own, rows_out.at[0, 0:3], zs.at[r], zr.at[r])

    gz = [row_ring(r) for r in range(QUARTERS)]

    def row_swaps(r):
        return [
            pltpu.make_async_remote_copy(
                src_ref=head(half, place.quarter(r), k),
                dst_ref=rows_out.at[z, place.quarter(0), half, k],
                send_sem=s_send.at[r],
                recv_sem=s_recv.at[r],
                device_id=place.square(r),
                device_id_type=MESH,
            )
            for half in range(2)
            for k in range(PART)
        ]

    def swapped(r):
        ref = rows_out.at[z, place.quarter(r)]
        return pltpu.make_async_remote_copy(
            src_ref=ref,
            dst_ref=ref,
            send_sem=s_send.at[r],
            recv_sem=s_recv.at[r],
            device_id=place.square(r),
            device_id_type=MESH,
        )

    def pass_rows(r):
        swapped(r).wait_recv()
        gz[r].start()

    def line(n):
        at_line = y if n == 0 else x
        part = lambda at, half: keys_out.at[n, at_line, at, half]
        if n == 0:
            own = lambda half: [((k_ref, v_ref)[half].at[:, ours], part(x, half))]
        else:
            own = lambda half: [(part(y, half),) * 2]
        return Gather(place, "xy"[n], part, own, keys_out.at[n, 0, 0:3], cs.at[n, 0], cr.at[n, 0])

    def cross(n, step):
        at_line, spot = (y, x) if n == 0 else (x, y)
        spot = ring_at(spot, step)
        part = lambda at, half: keys_out.at[n, at, spot, half]
        if n == 0 and step == 0:
            own = lambda half: [((k_ref, v_ref)[half].at[:, ours], part(y, half))]
        else:
            own = lambda half: [(part(at_line, half),) * 2]
        k = 1 + step % RING
        return Gather(place, "yx"[n], part, own, keys_out.at[n, 0, 0:3], cs.at[n, k], cr.at[n, k])

    lines = [line(n) for n in range(2)]
    crosses = [[cross(n, step) for step in (0, -1, 1, 2)] for n in range(2)]

    gz[0].start()
    for r in (2, 1):
        for copy in row_swaps(r):
            copy.start()
    lines[0].start()
    crosses[0][0].start()
    for copy in row_swaps(3):
        copy.start()
    for src, dst in rows_copies(0) + rows_copies(1):
        pltpu.make_async_copy(src, dst, local.at[0]).start()
    for n, source in enumerate((k_ref, v_ref)):
        pltpu.make_async_copy(source.at[:, ours], keys_out.at[0, y, x, n], local.at[1]).start()
    for copy in swaps:
        copy.wait_recv()
    lines[1].start()
    crosses[1][0].start()

    for copy in loads:
        copy.wait()
    for quarter in range(QUARTERS):
        for k in range(PART):
            cols = slice((quarter * PART + k) * D, (quarter * PART + k + 1) * D)
            product = g_vmem[:, cols].astype(F32) * o_vmem[:, cols].astype(F32)
            parts[quarter, :, k * B : (k + 1) * B] = jnp.sum(
                jnp.transpose(product), axis=0, keepdims=True
            )

    def delta_copy(r):
        return pltpu.make_async_remote_copy(
            src_ref=parts.at[place.quarter(r)],
            dst_ref=delta_ref.at[place.quarter(0)],
            send_sem=d_send.at[r],
            recv_sem=d_recv.at[r],
            device_id=place.square(r),
            device_id_type=MESH,
        )

    for r in (1, 2, 3):
        delta_copy(r).start()
    delta_ref[place.quarter(0)] = parts[place.quarter(0)]
    pass_rows(2)
    pass_rows(1)
    gz[0].forward()
    for n in range(2):
        lines[n].forward()
    for n in range(2):
        lines[n].arrived(0, 1)
        crosses[n][1].start()
        lines[n].arrived(1, 1)
        crosses[n][2].start()
    pass_rows(3)
    for n in range(2):
        crosses[n][0].forward()
    for n in range(2):
        lines[n].arrived(0, 2)
        lines[n].arrived(1, 2)
        crosses[n][3].start()
    gz[2].forward()
    gz[1].forward()
    for n in range(2):
        crosses[n][1].forward()
        crosses[n][2].forward()
    gz[3].forward()
    for n in range(2):
        crosses[n][3].forward()

    meta_ref[...] = tile_lists(place, qb, kb, kept)

    for n in range(2):
        for ring in crosses[n]:
            ring.finish()
    for ring in gz:
        ring.finish()
    for n, ref in enumerate((rows_out.at[z, place.quarter(0)], keys_out.at[0, y, x])):
        pltpu.make_async_copy(ref, ref, local.at[n]).wait()
    for copy in swaps:
        copy.wait_send()
    for r in (1, 2, 3):
        swapped(r).wait_send()
        delta_copy(r).wait_send()
        ref = delta_ref.at[place.quarter(r)]
        pltpu.make_async_remote_copy(
            src_ref=ref,
            dst_ref=ref,
            send_sem=d_send.at[r],
            recv_sem=d_recv.at[r],
            device_id=place.square(r),
            device_id_type=MESH,
        ).wait_recv()
    for ring in gz + lines + crosses[0] + crosses[1]:
        ring.sent()


def in_hbm(*arrays):
    return [pltpu.with_memory_space_constraint(a, pltpu.HBM) for a in arrays]


def gather(qb, kb, kept, q, k, v, o, g):
    return pl.pallas_call(
        gather_kernel,
        out_shape=(
            pltpu.VMEM((RING, QUARTERS, 2, PART, B, D), BF),
            pltpu.VMEM((2, RING, RING, 2, B, D), BF),
            pltpu.VMEM((QUARTERS, 1, COLS), F32),
            pltpu.VMEM((LOCAL_ROWS, 128), jnp.int32),
        ),
        in_specs=[HBM] * 8,
        out_specs=(ANY, ANY, VMEM, VMEM),
        scratch_shapes=[
            pltpu.SMEM((64,), jnp.int32),
            pltpu.SMEM((128,), jnp.int32),
            pltpu.VMEM((64, 64), jnp.int32),
            pltpu.VMEM((B, HEADS * D), BF),
            pltpu.VMEM((B, HEADS * D), BF),
            pltpu.VMEM((QUARTERS, 1, COLS), F32),
            pltpu.SemaphoreType.DMA((5,)),
            pltpu.SemaphoreType.DMA((2,)),
            pltpu.SemaphoreType.DMA((2,)),
            pltpu.SemaphoreType.DMA((2,)),
            pltpu.SemaphoreType.DMA((QUARTERS,)),
            pltpu.SemaphoreType.DMA((QUARTERS,)),
            pltpu.SemaphoreType.DMA((QUARTERS,)),
            pltpu.SemaphoreType.DMA((QUARTERS,)),
            pltpu.SemaphoreType.DMA((QUARTERS,)),
            pltpu.SemaphoreType.DMA((QUARTERS, 6)),
            pltpu.SemaphoreType.DMA((2, 1 + RING)),
            pltpu.SemaphoreType.DMA((2, 1 + RING, 6)),
        ],
        compiler_params=pltpu.CompilerParams(
            collective_id=0, has_side_effects=True, vmem_limit_bytes=8 * 2**20
        ),
        name="gather",
    )(*in_hbm(qb, kb, kept, q, k, v, o, g))


def across(a, b):
    return lax.dot_general(a, b, (((1,), (1,)), ((), ())), preferred_element_type=F32)


def fill_bias(bias_ref):
    keys = lax.broadcasted_iota(jnp.int32, (B, COLS), 0)
    rows = lax.rem(lax.broadcasted_iota(jnp.int32, (B, COLS), 1), B)
    bias_ref[0] = jnp.full((B, COLS), MASKED, F32)
    bias_ref[1] = jnp.where(keys <= rows, 0.0, MASKED)
    bias_ref[2] = jnp.zeros((B, COLS), F32)


def pop(bits, diagonal):
    j = (31 - lax.clz(bits)) & 31
    kind = jnp.where(bits == 0, 0, jnp.where(j == diagonal, 1, 2))
    return j, bits & ~lax.shift_left(jnp.int32(1), j), kind


def list_tasks(meta_ref, task_ref):
    def row(i, count):
        diagonal = meta_ref[i, 1]

        def more(state):
            return state[0] != 0

        def step(state):
            bits, count = state
            j0, bits, kind0 = pop(bits, diagonal)
            j1, bits, kind1 = pop(bits, diagonal)
            task_ref[count] = i + j0 * 16 + j1 * 512 + kind0 * 16384 + kind1 * 65536
            return bits, count + 1

        return lax.while_loop(more, step, (meta_ref[i, 0], count))[1]

    count = lax.fori_loop(0, LOCAL_ROWS, row, jnp.int32(0))
    for n in range(GROUP - 1):
        task_ref[count + n] = 0
    task_ref[TASKS - 1] = (count + GROUP - 1) // GROUP


def read_task(task_ref, n):
    e = task_ref[n]
    return (
        e & 15,
        (e // 16) & 31,
        (e // 512) & 31,
        (e // 16384) & 3,
        (e // 65536) & 3,
    )


def stats_kernel(meta_ref, rows_ref, keys_ref, st_ref, task_ref, m_ref, l_ref, bias_ref):
    list_tasks(meta_ref, task_ref)
    fill_bias(bias_ref)
    m_ref[...] = jnp.full_like(m_ref, NEG)
    l_ref[...] = jnp.zeros_like(l_ref)

    def group(n, _):
        results = []
        for t in range(GROUP):
            i, j0, j1, kind0, kind1 = read_task(task_ref, GROUP * n + t)
            queries = rows_ref[i, 0].reshape(COLS, D)
            keys = jnp.concatenate([keys_ref[j0, 0], keys_ref[j1, 0]], axis=0)
            s = across(keys, queries) * C2
            s = jnp.concatenate([s[:B] + bias_ref[kind0], s[B:] + bias_ref[kind1]], axis=0)
            s = s.reshape(2 * B // 8, 8, COLS)
            m = jnp.max(s, axis=0)
            results.append((i, m, jnp.sum(jnp.exp2(s - m[None]), axis=0)))
        for i, m, l in results:
            old = m_ref[i]
            new = jnp.maximum(old, m)
            m_ref[i] = new
            l_ref[i] = l_ref[i] * jnp.exp2(old - new) + l * jnp.exp2(m - new)
        return 0

    lax.fori_loop(0, task_ref[TASKS - 1], group, 0)
    m8 = m_ref[...]
    m = jnp.max(m8, axis=1, keepdims=True)
    st_ref[0] = m
    st_ref[1] = jnp.sum(l_ref[...] * jnp.exp2(m8 - m), axis=1, keepdims=True)


def statistics(meta, rows, keys):
    return pl.pallas_call(
        stats_kernel,
        out_shape=(
            pltpu.VMEM((2, LOCAL_ROWS, 1, COLS), F32),
            jax.ShapeDtypeStruct((TASKS,), jnp.int32),
        ),
        in_specs=[SMEM, VMEM, VMEM],
        out_specs=(VMEM, SMEM),
        scratch_shapes=[
            pltpu.VMEM((LOCAL_ROWS, 8, COLS), F32),
            pltpu.VMEM((LOCAL_ROWS, 8, COLS), F32),
            pltpu.VMEM((3, B, COLS), F32),
        ],
        compiler_params=pltpu.CompilerParams(vmem_limit_bytes=24 * 2**20),
        name="statistics",
    )(meta, rows, keys)


def exchange_kernel(
    st_ref, delta_ref, total_ref, all_delta_ref, sts, st_send, st_recv
):
    place = Place()
    z = place.z
    greet([place.along("z", step) for step in (1, 2, 3)])

    def copies(step):
        to = place.along("z", step)
        pairs = ((st_ref, sts.at[step - 1]), (delta_ref, all_delta_ref.at[z]))
        for n, (src, dst) in enumerate(pairs):
            yield pltpu.make_async_remote_copy(
                src_ref=src,
                dst_ref=dst,
                send_sem=st_send.at[step - 1, n],
                recv_sem=st_recv.at[step - 1, n],
                device_id=to,
                device_id_type=MESH,
            )

    for step in (2, 1, 3):
        for copy in copies(step):
            copy.start()
    all_delta_ref[z] = delta_ref[...]
    for step in (1, 3, 2):
        st_copy, delta_copy = copies(step)
        st_copy.wait()
        delta_copy.wait_send()
        ref = all_delta_ref.at[ring_at(z, -step)]
        pltpu.make_async_remote_copy(
            src_ref=ref,
            dst_ref=ref,
            send_sem=st_send.at[step - 1, 1],
            recv_sem=st_recv.at[step - 1, 1],
            device_id=place.along("z", step),
            device_id_type=MESH,
        ).wait_recv()
    top = st_ref[0]
    for n in range(3):
        top = jnp.maximum(top, sts[n, 0])
    total = st_ref[1] * jnp.exp2(st_ref[0] - top)
    for n in range(3):
        total = total + sts[n, 1] * jnp.exp2(sts[n, 0] - top)
    total_ref[...] = top + jnp.log2(total)


def exchange(st, delta):
    return pl.pallas_call(
        exchange_kernel,
        out_shape=(
            pltpu.VMEM((LOCAL_ROWS, 1, COLS), F32),
            pltpu.VMEM((RING, QUARTERS, 1, COLS), F32),
        ),
        in_specs=[VMEM, VMEM],
        out_specs=(VMEM, VMEM),
        scratch_shapes=[
            pltpu.VMEM((3, 2, LOCAL_ROWS, 1, COLS), F32),
            pltpu.SemaphoreType.DMA((3, 2)),
            pltpu.SemaphoreType.DMA((3, 2)),
        ],
        compiler_params=pltpu.CompilerParams(
            collective_id=1, has_side_effects=True, vmem_limit_bytes=8 * 2**20
        ),
        name="exchange",
    )(st, delta)


def grads_kernel(
    task_ref, rows_ref, keys_ref, total_ref, delta_ref, dq_ref, dkv_ref,
    dq_acc, dk_acc, dv_acc, bias_ref, p_ref, ds_ref,
):
    fill_bias(bias_ref)
    dq_acc[...] = jnp.zeros_like(dq_acc)
    dk_acc[...] = jnp.zeros_like(dk_acc)
    dv_acc[...] = jnp.zeros_like(dv_acc)

    def group(n, _):
        tasks = [read_task(task_ref, GROUP * n + t) for t in range(GROUP)]
        for t, (i, j0, j1, kind0, kind1) in enumerate(tasks):
            keys = jnp.concatenate([keys_ref[j0, 0], keys_ref[j1, 0]], axis=0)
            values = jnp.concatenate([keys_ref[j0, 1], keys_ref[j1, 1]], axis=0)
            s = across(keys, rows_ref[i, 0].reshape(COLS, D)) * C2 - total_ref[i]
            s = jnp.concatenate([s[:B] + bias_ref[kind0], s[B:] + bias_ref[kind1]], axis=0)
            p = jnp.exp2(s)
            p_ref[t] = p.astype(BF)
            dp = across(values, rows_ref[i, 1].reshape(COLS, D))
            ds_ref[t] = (p * (dp - delta_ref[i])).astype(BF)
        for t, (i, j0, j1, _, _) in enumerate(tasks):
            keys = jnp.concatenate([keys_ref[j0, 0], keys_ref[j1, 0]], axis=0)
            ds = ds_ref[t]
            dv = jnp.dot(p_ref[t], rows_ref[i, 1].reshape(COLS, D), preferred_element_type=F32)
            dk = jnp.dot(ds, rows_ref[i, 0].reshape(COLS, D), preferred_element_type=F32)
            dq_acc[i] += jnp.dot(jnp.transpose(keys), ds, preferred_element_type=F32)
            dk_acc[j0] += dk[:B]
            dk_acc[j1] += dk[B:]
            dv_acc[j0] += dv[:B]
            dv_acc[j1] += dv[B:]
        return 0

    lax.fori_loop(0, task_ref[TASKS - 1], group, 0)

    def write(j, _):
        dkv_ref[j, 0] = (dk_acc[j] * SCALE).astype(BF)
        dkv_ref[j, 1] = dv_acc[j].astype(BF)
        return 0

    lax.fori_loop(0, LOCAL_KEYS, write, 0, unroll=8)

    def write_rows(i, _):
        for k in range(PART):
            dq_ref[i, k] = (dq_acc[i, :, k * B : (k + 1) * B] * SCALE).astype(BF)
        return 0

    lax.fori_loop(0, LOCAL_ROWS, write_rows, 0, unroll=8)


def grads(tasks, rows, keys, total, delta):
    return pl.pallas_call(
        grads_kernel,
        out_shape=(
            pltpu.VMEM((LOCAL_ROWS, PART, D, B), BF),
            pltpu.VMEM((LOCAL_KEYS, 2, B, D), BF),
        ),
        in_specs=[SMEM] + [VMEM] * 4,
        out_specs=(VMEM, VMEM),
        scratch_shapes=[
            pltpu.VMEM((LOCAL_ROWS, D, COLS), F32),
            pltpu.VMEM((LOCAL_KEYS, B, D), F32),
            pltpu.VMEM((LOCAL_KEYS, B, D), F32),
            pltpu.VMEM((3, B, COLS), F32),
            pltpu.VMEM((GROUP, 2 * B, COLS), BF),
            pltpu.VMEM((GROUP, 2 * B, COLS), BF),
        ],
        compiler_params=pltpu.CompilerParams(vmem_limit_bytes=32 * 2**20),
        name="grads",
    )(tasks, rows, keys, total, delta)


class Scatter:
    def __init__(self, place, axis, part, near, far, mid, six, send, recv):
        self.me = getattr(place, axis)
        self.to = (place.along(axis, 1), place.along(axis, -1))
        self.part, self.near, self.far, self.mid, self.six = part, near, far, mid, six
        self.send, self.recv = send, recv

    def copy(self, src, dst, way, k):
        return pltpu.make_async_remote_copy(
            src_ref=src,
            dst_ref=dst,
            send_sem=self.send,
            recv_sem=self.recv.at[way * 3 + k],
            device_id=self.to[way],
            device_id_type=MESH,
        )

    def far_copy(self, way):
        return self.copy(self.part(ring_at(self.me, 2), way), self.far.at[way], way, 0)

    def plain_copy(self, way):
        step = 1 if way == 0 else -1
        return self.copy(
            self.part(ring_at(self.me, step), 1 - way), self.near.at[way, 1 - way], way, 1
        )

    def mid_copy(self, way):
        return self.copy(self.mid.at[way], self.near.at[way, way], way, 2)

    def start_far(self):
        for way in range(2):
            self.far_copy(way).start()

    def start_plain(self, way):
        self.plain_copy(way).start()

    def forward(self):
        for way in range(2):
            step = 1 if way == 0 else -1
            self.far_copy(way).wait_recv()
            own = self.part(ring_at(self.me, step), way)[...].astype(F32)
            self.mid[way] = (self.far[way].astype(F32) + own).astype(BF)
            self.mid_copy(way).start()

    def finish(self):
        for way in range(2):
            self.plain_copy(way).wait_recv()
        for way in range(2):
            self.mid_copy(way).wait_recv()

    def total(self, half, own=None):
        own = self.part(self.me, half)[...].astype(F32) if own is None else own
        return own + self.near[0, half].astype(F32) + self.near[1, half].astype(F32)

    def sent(self):
        self.copy(self.six, self.six, 0, 0).wait_send()


STEPS = (2, -1, 1, 0)
MEMBERS = (3, 2, 1, 0)


def scatter_kernel(
    dq_ref, dkv_ref, qg_ref, kg_ref, vg_ref,
    zn, zf, zm, cn, cf, cm, ln, lf, lm, sums, own_sum, fin, qout,
    zs, zr, cs, cr, ls, lr, swap_send, swap_recv, q_send, q_recv, local,
):
    place = Place()
    h, x, y, z = place.h, place.x, place.y, place.z
    greet(place.around())

    def row_ring(k):
        number = place.quarter(MEMBERS[k])
        part = lambda at, half: dq_ref.at[at, number, half]
        return Scatter(place, "z", part, zn.at[k], zf.at[k], zm.at[k], dq_ref.at[0, 0:3], zs.at[k], zr.at[k])

    def cross(n, k):
        spot = ring_at((x, y)[n], STEPS[k])
        part = lambda at, half: dkv_ref.at[n, at, spot, half]
        return Scatter(
            place, "yx"[n], part, cn.at[n, k], cf.at[n, k], cm.at[n, k], dkv_ref.at[n, 0, 0:3],
            cs.at[n, k], cr.at[n, k],
        )

    def line(n):
        part = lambda at, half: sums.at[n, at, half]
        return Scatter(place, "xy"[n], part, ln.at[n], lf.at[n], lm.at[n], sums.at[n, 0:3], ls.at[n], lr.at[n])

    rows = [row_ring(k) for k in range(RING)]
    crosses = [[cross(n, k) for k in range(RING)] for n in range(2)]
    lines = [line(n) for n in range(2)]
    waves = [(crosses[0][k], crosses[1][k], rows[k]) for k in range(RING)]
    for wave in waves:
        for ring in wave:
            ring.start_far()
    for wave in waves:
        for ring in wave:
            for way in range(2):
                ring.start_plain(way)
    for wave in waves:
        for ring in wave:
            ring.forward()

    part_cols = pl.ds(pl.multiple_of(place.quarter(0) * COLS, COLS), COLS)

    def q_copy(k):
        r = MEMBERS[k]
        return pltpu.make_async_remote_copy(
            src_ref=qout.at[k],
            dst_ref=qg_ref.at[:, part_cols],
            send_sem=q_send.at[r],
            recv_sem=q_recv.at[r],
            device_id=place.square(r),
            device_id_type=MESH,
        )

    q_own = pltpu.make_async_copy(qout.at[RING - 1], qg_ref.at[:, part_cols], local.at[0])
    for k in range(RING):
        for n in range(2):
            ring = crosses[n][k]
            ring.finish()
            for half in range(2):
                total = ring.total(half)
                if STEPS[k] == 0:
                    own_sum[n, half] = total
                else:
                    sums[n, ring_at((x, y)[n], STEPS[k]), half] = total.astype(BF)
            if STEPS[k] == 2:
                lines[n].start_far()
            elif STEPS[k] != 0:
                lines[n].start_plain(0 if STEPS[k] == 1 else 1)
        if k == 2:
            for n in range(2):
                lines[n].forward()
        rows[k].finish()
        for half in range(PART):
            qout[k, :, half * D : (half + 1) * D] = jnp.transpose(rows[k].total(half)).astype(BF)
        if MEMBERS[k]:
            q_copy(k).start()
        else:
            q_own.start()

    ours = pl.ds(pl.multiple_of(h * D, D), D)
    theirs = pl.ds(pl.multiple_of((1 - h) * D, D), D)
    swaps = [
        pltpu.make_async_remote_copy(
            src_ref=fin.at[1, n],
            dst_ref=target.at[:, ours],
            send_sem=swap_send.at[n],
            recv_sem=swap_recv.at[n],
            device_id=place.partner(),
            device_id_type=MESH,
        )
        for n, target in enumerate((kg_ref, vg_ref))
    ]
    outs = [
        pltpu.make_async_copy(fin.at[0, n], target.at[:, ours], local.at[1 + n])
        for n, target in enumerate((kg_ref, vg_ref))
    ]
    for n, copies in ((1, swaps), (0, outs)):
        lines[n].finish()
        for half in range(2):
            fin[n, half] = lines[n].total(half, own_sum[n, half]).astype(BF)
        for copy in copies:
            copy.start()
    for copy in outs:
        copy.wait()
    q_own.wait()
    for n, target in enumerate((kg_ref, vg_ref)):
        swaps[n].wait_send()
        ref = target.at[:, theirs]
        pltpu.make_async_remote_copy(
            src_ref=ref,
            dst_ref=ref,
            send_sem=swap_send.at[n],
            recv_sem=swap_recv.at[n],
            device_id=place.partner(),
            device_id_type=MESH,
        ).wait_recv()
    for k in range(RING - 1):
        q_copy(k).wait_send()
        r = MEMBERS[k]
        ref = qg_ref.at[:, pl.ds(pl.multiple_of(place.quarter(r) * COLS, COLS), COLS)]
        pltpu.make_async_remote_copy(
            src_ref=ref,
            dst_ref=ref,
            send_sem=q_send.at[r],
            recv_sem=q_recv.at[r],
            device_id=place.square(r),
            device_id_type=MESH,
        ).wait_recv()
    for ring in rows + crosses[0] + crosses[1] + lines:
        ring.sent()


def scatter(dq, dkv):
    def ring_scratch(*rings):
        return [
            pltpu.VMEM(rings + (2, 2, B, D), BF),
            pltpu.VMEM(rings + (2, B, D), BF),
            pltpu.VMEM(rings + (2, B, D), BF),
        ]

    def ring_semaphores(*rings):
        return [pltpu.SemaphoreType.DMA(rings), pltpu.SemaphoreType.DMA(rings + (6,))]

    return pl.pallas_call(
        scatter_kernel,
        out_shape=(
            pltpu.VMEM((B, HEADS * D), BF),
            pltpu.VMEM((B, 2 * D), BF),
            pltpu.VMEM((B, 2 * D), BF),
        ),
        in_specs=[VMEM, VMEM],
        out_specs=(VMEM, VMEM, VMEM),
        scratch_shapes=ring_scratch(RING)
        + ring_scratch(2, RING)
        + ring_scratch(2)
        + [
            pltpu.VMEM((2, RING, 2, B, D), BF),
            pltpu.VMEM((2, 2, B, D), F32),
            pltpu.VMEM((2, 2, B, D), BF),
            pltpu.VMEM((QUARTERS, B, COLS), BF),
        ]
        + ring_semaphores(RING)
        + ring_semaphores(2, RING)
        + ring_semaphores(2)
        + [
            pltpu.SemaphoreType.DMA((2,)),
            pltpu.SemaphoreType.DMA((2,)),
            pltpu.SemaphoreType.DMA((QUARTERS,)),
            pltpu.SemaphoreType.DMA((QUARTERS,)),
            pltpu.SemaphoreType.DMA((3,)),
        ],
        compiler_params=pltpu.CompilerParams(
            collective_id=2, has_side_effects=True, vmem_limit_bytes=24 * 2**20
        ),
        name="scatter",
    )(dq.reshape(RING, QUARTERS, PART, D, B), dkv.reshape(2, RING, RING, 2, B, D))


def store_kernel(q_ref, k_ref, v_ref, qg_ref, kg_ref, vg_ref, sems):
    copies = [
        pltpu.make_async_copy(src, dst, sems.at[n])
        for n, (src, dst) in enumerate(((q_ref, qg_ref), (k_ref, kg_ref), (v_ref, vg_ref)))
    ]
    for copy in copies:
        copy.start()
    for copy in copies:
        copy.wait()


def store(*results):
    return pl.pallas_call(
        store_kernel,
        out_shape=tuple(pltpu.HBM(r.shape, r.dtype) for r in results),
        in_specs=[VMEM] * 3,
        out_specs=(HBM,) * 3,
        scratch_shapes=[pltpu.SemaphoreType.DMA((3,))],
        compiler_params=pltpu.CompilerParams(vmem_limit_bytes=4 * 2**20),
        name="store",
    )(*results)


def body(q, k, v, o, g, query_blocks, key_blocks, kept_blocks):
    rows, keys, delta, meta = gather(query_blocks, key_blocks, kept_blocks, q, k, v, o, g)
    rows = rows.reshape(LOCAL_ROWS, 2, PART, B, D)
    keys = keys.reshape(LOCAL_KEYS, 2, B, D)
    st, tasks = statistics(meta, rows, keys)
    total, all_delta = exchange(st, delta)
    dq, dkv = grads(tasks, rows, keys, total, all_delta.reshape(LOCAL_ROWS, 1, COLS))
    return store(*scatter(dq, dkv))


def solution(mesh):
    rows, stored = P(("inner", "outer"), "head"), P(("head", "inner", "outer"), None)
    return jax.shard_map(
        body,
        mesh=mesh,
        in_specs=(rows, stored, stored, rows, rows, P(), P(), P()),
        out_specs=(rows, stored, stored),
        check_vma=False,
    )
```

```python
import math

import jax
import jax.numpy as jnp
from jax import lax
from jax.experimental import pallas as pl
from jax.experimental.pallas import tpu as pltpu
from jax.sharding import PartitionSpec as P

HEADS = 8
D = 128
B = 128
RING = 4
QUARTERS = 4
PART = 2
COLS = PART * B
LOCAL_ROWS = 16
LOCAL_KEYS = 32
ENTRIES = 64
GROUP = 8
TASKS = 272
EARLY = 120
FIRST_KEY = 64
SCALE = 1.0 / math.sqrt(D)
LOG2E = math.log2(math.e)
C2 = SCALE * LOG2E
NEG = -1e30
MASKED = -2e30
MESH = pl.DeviceIdType.MESH
ANY = pl.BlockSpec(memory_space=pl.ANY)
HBM = pl.BlockSpec(memory_space=pltpu.HBM)
VMEM = pl.BlockSpec(memory_space=pltpu.VMEM)
SMEM = pl.BlockSpec(memory_space=pltpu.SMEM)
BF = jnp.bfloat16
F32 = jnp.float32


class Place:
    def __init__(self):
        self.h = lax.axis_index("head")
        inner, outer = lax.axis_index("inner"), lax.axis_index("outer")
        self.x, self.z = lax.rem(outer, 4), lax.rem(inner, 4)
        self.y = (inner // 4) * 2 + outer // 4

    def device(self, x=None, y=None, z=None, h=None):
        x, y, z, h = (
            own if new is None else new
            for own, new in ((self.x, x), (self.y, y), (self.z, z), (self.h, h))
        )
        return (h, (y // 2) * 4 + z, lax.rem(y, 2) * 4 + x)

    def along(self, axis, step):
        at = lax.rem(getattr(self, axis) + step + RING, RING)
        return self.device(**{axis: at})

    def partner(self):
        return self.device(h=1 - self.h)

    def quarter(self, r):
        b, a = lax.rem(self.y, 2), lax.rem(self.x, 2)
        b, a = (1 - b if r & 2 else b), (1 - a if r & 1 else a)
        return 2 * b + a

    def square(self, r):
        b, a = lax.rem(self.y, 2), lax.rem(self.x, 2)
        y = self.y + 1 - 2 * b if r & 2 else self.y
        x = self.x + 1 - 2 * a if r & 1 else self.x
        return self.device(x=x, y=y)

    def around(self):
        near = [self.along(a, s) for a in ("x", "y", "z") for s in (1, -1)]
        return near + [self.partner(), self.square(3)]


def ring_at(me, step):
    return lax.rem(me + step + RING, RING)


def greet(devices):
    barrier = pltpu.get_barrier_semaphore()
    for device in devices:
        pl.semaphore_signal(barrier, inc=1, device_id=device, device_id_type=MESH)
    pl.semaphore_wait(barrier, len(devices))


class Gather:
    def __init__(self, place, axis, part, own, six, send, recv):
        self.me = getattr(place, axis)
        self.to = (place.along(axis, 1), place.along(axis, -1))
        self.part, self.own, self.six, self.send, self.recv = part, own, six, send, recv

    def copy(self, src, dst, way, k):
        return pltpu.make_async_remote_copy(
            src_ref=src,
            dst_ref=dst,
            send_sem=self.send,
            recv_sem=self.recv.at[way * 3 + k],
            device_id=self.to[way],
            device_id_type=MESH,
        )

    def start(self):
        for k in range(2):
            for way in range(2):
                for src, dst in self.own(k ^ way):
                    self.copy(src, dst, way, k).start()

    def whole(self, at, half, way, k):
        ref = self.part(at, half)
        return self.copy(ref, ref, way, k)

    def arrived(self, way, k):
        step = (-1 if way == 0 else 1) * (2 if k == 2 else 1)
        half = way if k == 2 else k ^ way
        self.whole(ring_at(self.me, step), half, way, k).wait_recv()

    def forward(self):
        for way in range(2):
            self.arrived(way, 0)
            step = -1 if way == 0 else 1
            self.whole(ring_at(self.me, step), way, way, 2).start()

    def finish(self):
        for way in range(2):
            self.arrived(way, 1)
        for way in range(2):
            self.arrived(way, 2)

    def sent(self):
        self.copy(self.six, self.six, 0, 0).wait_send()


def key_slot(place, j):
    n, a, b = j // 16, lax.rem(j // 4, 4), lax.rem(j, 4)
    owner = jnp.where(n == 0, place.h, 1 - place.h)
    yy, xx = jnp.where(n == 0, a, b), jnp.where(n == 0, b, a)
    return owner * 64 + (yy // 2) * 32 + place.z * 8 + lax.rem(yy, 2) * 4 + xx


def row_slot(place, i):
    zz, b, a = i // 4, lax.rem(i // 2, 2), lax.rem(i, 2)
    return (place.y // 2) * 32 + zz * 8 + b * 4 + (place.x // 2) * 2 + a


def tile_lists(place, qb_ref, kb_ref, kept):
    lanes = lax.broadcasted_iota(jnp.int32, (1, 128), 1)
    subs = lax.broadcasted_iota(jnp.int32, (LOCAL_ROWS, 1), 0)

    def key_step(j, row):
        return jnp.where(lanes == j, kb_ref[key_slot(place, j)], row)

    def row_step(i, column):
        return jnp.where(subs == i, qb_ref[row_slot(place, i)], column)

    key_pos = lax.fori_loop(0, LOCAL_KEYS, key_step, jnp.full((1, 128), -7, jnp.int32))
    row_pos = lax.fori_loop(0, LOCAL_ROWS, row_step, jnp.zeros((LOCAL_ROWS, 1), jnp.int32))
    wide = lax.broadcasted_iota(jnp.int32, (64, 128), 1)
    listed = jnp.zeros((64, 128), F32)
    for e in range(ENTRIES):
        listed = jnp.where(kept[:, e : e + 1] == wide, 1.0, listed)
    rows_of = (row_pos == lax.broadcasted_iota(jnp.int32, (LOCAL_ROWS, 64), 1)).astype(F32)
    keys_of = (key_pos == lax.broadcasted_iota(jnp.int32, (128, 128), 0)).astype(F32)
    mine = jnp.dot(
        jnp.dot(rows_of.astype(BF), listed.astype(BF), preferred_element_type=F32).astype(BF),
        keys_of.astype(BF),
        preferred_element_type=F32,
    )
    lane16 = lax.broadcasted_iota(jnp.int32, (LOCAL_ROWS, 128), 1)
    weight = lax.shift_left(jnp.ones_like(lane16), lax.rem(lane16, 16)).astype(F32)
    low = jnp.sum(jnp.where(lane16 < 16, mine * weight, 0.0), axis=1, keepdims=True)
    high = jnp.sum(
        jnp.where((lane16 >= 16) & (lane16 < 32), mine * weight, 0.0), axis=1, keepdims=True
    )
    bits = low.astype(jnp.int32) + lax.shift_left(
        high.astype(jnp.int32), jnp.full((LOCAL_ROWS, 1), 16, jnp.int32)
    )
    on = (key_pos == row_pos + FIRST_KEY).astype(F32)
    diagonal = jnp.sum(on * (lane16 - 99).astype(F32), axis=1, keepdims=True) + 99.0
    meta = jnp.where(lane16 == 0, bits, diagonal.astype(jnp.int32))
    return meta, mine, diagonal


def halves_up(count):
    return lax.shift_right_logical(
        count.astype(jnp.int32) + 1, jnp.ones(count.shape, jnp.int32)
    ).astype(F32)


def exact(a, b, dims=(((1,), (0,)), ((), ()))):
    return lax.dot_general(a.astype(BF), b.astype(BF), dims, preferred_element_type=F32)


def early_tasks(mine, diagonal):
    sub = lax.broadcasted_iota(jnp.int32, (LOCAL_ROWS, 128), 0)
    lane = lax.broadcasted_iota(jnp.int32, (LOCAL_ROWS, 128), 1)
    count = jnp.broadcast_to(jnp.sum(mine, axis=1, keepdims=True), (LOCAL_ROWS, 128))
    tasks = halves_up(count)
    before = (
        lax.broadcasted_iota(jnp.int32, (LOCAL_ROWS, LOCAL_ROWS), 1)
        < lax.broadcasted_iota(jnp.int32, (LOCAL_ROWS, LOCAL_ROWS), 0)
    ).astype(F32)
    start = exact(before, tasks)
    at = lane.astype(F32)
    chosen = ((start <= at) & (at < start + tasks)).astype(F32)

    def of_row(column):
        return jnp.sum(chosen * column, axis=0, keepdims=True)

    row, first, diag = of_row(sub.astype(F32)), of_row(start), of_row(diagonal)
    lower = (
        lax.broadcasted_iota(jnp.int32, (128, 128), 0)
        < lax.broadcasted_iota(jnp.int32, (128, 128), 1)
    ).astype(F32)
    rank = exact(mine, lower)
    down = (((0,), (0,)), ((), ()))
    mine_t, rank_t = exact(mine, chosen, down), exact(rank, chosen, down)
    block = lax.broadcasted_iota(jnp.int32, (128, 128), 0).astype(F32)
    code = row
    for k in range(2):
        here = mine_t * (rank_t == 2.0 * (at[:1] - first) + k).astype(F32)
        j = jnp.sum(here * block, axis=0, keepdims=True)
        valid = jnp.sum(here, axis=0, keepdims=True)
        kind = valid * jnp.where(j == diag, 1.0, 2.0)
        code = code + j * (16.0, 512.0)[k] + kind * (16384.0, 65536.0)[k]
    return code, jnp.sum(tasks, axis=0, keepdims=True)


def gather_kernel(
    qb_hbm, kb_hbm, kept_hbm, q_ref, k_ref, v_ref, o_ref, g_ref,
    rows_out, keys_out, delta_ref, meta_ref, list_ref,
    qb, kb, kept, o_vmem, g_vmem, parts,
    load, local, swap_send, swap_recv, s_send, s_recv, d_send, d_recv, dz_send, dz_recv, zs, zr, cs, cr,
):
    place = Place()
    h, x, y, z = place.h, place.x, place.y, place.z
    pairs = ((o_ref, o_vmem), (g_ref, g_vmem), (kept_hbm, kept), (qb_hbm, qb), (kb_hbm, kb))
    loads = [pltpu.make_async_copy(src, dst, load.at[n]) for n, (src, dst) in enumerate(pairs)]
    for copy in loads:
        copy.start()
    greet(place.around() + [place.along("z", 2)])
    ours = pl.ds(pl.multiple_of(h * D, D), D)
    theirs = pl.ds(pl.multiple_of((1 - h) * D, D), D)

    swaps = [
        pltpu.make_async_remote_copy(
            src_ref=source.at[:, theirs],
            dst_ref=keys_out.at[1, x, y, n],
            send_sem=swap_send.at[n],
            recv_sem=swap_recv.at[n],
            device_id=place.partner(),
            device_id_type=MESH,
        )
        for n, source in enumerate((k_ref, v_ref))
    ]
    for copy in swaps:
        copy.start()

    def head(half, quarter, k):
        source = (q_ref, g_ref)[half]
        return source.at[:, pl.ds(pl.multiple_of((quarter * PART + k) * D, D), D)]

    def rows_copies(half):
        mine = place.quarter(0)
        return [(head(half, mine, k), rows_out.at[z, mine, half, k]) for k in range(PART)]

    def row_ring(r):
        part = lambda at, half: rows_out.at[at, place.quarter(r), half]
        own = rows_copies if r == 0 else lambda half: [(part(z, half),) * 2]
        return Gather(place, "z", part, own, rows_out.at[0, 0:3], zs.at[r], zr.at[r])

    gz = [row_ring(r) for r in range(QUARTERS)]

    def row_swaps(r):
        return [
            pltpu.make_async_remote_copy(
                src_ref=head(half, place.quarter(r), k),
                dst_ref=rows_out.at[z, place.quarter(0), half, k],
                send_sem=s_send.at[r],
                recv_sem=s_recv.at[r],
                device_id=place.square(r),
                device_id_type=MESH,
            )
            for half in range(2)
            for k in range(PART)
        ]

    def swapped(r):
        ref = rows_out.at[z, place.quarter(r)]
        return pltpu.make_async_remote_copy(
            src_ref=ref,
            dst_ref=ref,
            send_sem=s_send.at[r],
            recv_sem=s_recv.at[r],
            device_id=place.square(r),
            device_id_type=MESH,
        )

    def pass_rows(r):
        swapped(r).wait_recv()
        gz[r].start()

    def line(n):
        at_line = y if n == 0 else x
        part = lambda at, half: keys_out.at[n, at_line, at, half]
        if n == 0:
            own = lambda half: [((k_ref, v_ref)[half].at[:, ours], part(x, half))]
        else:
            own = lambda half: [(part(y, half),) * 2]
        return Gather(place, "xy"[n], part, own, keys_out.at[n, 0, 0:3], cs.at[n, 0], cr.at[n, 0])

    def cross(n, step):
        at_line, spot = (y, x) if n == 0 else (x, y)
        spot = ring_at(spot, step)
        part = lambda at, half: keys_out.at[n, at, spot, half]
        if n == 0 and step == 0:
            own = lambda half: [((k_ref, v_ref)[half].at[:, ours], part(y, half))]
        else:
            own = lambda half: [(part(at_line, half),) * 2]
        k = 1 + step % RING
        return Gather(place, "yx"[n], part, own, keys_out.at[n, 0, 0:3], cs.at[n, k], cr.at[n, k])

    lines = [line(n) for n in range(2)]
    crosses = [[cross(n, step) for step in (0, -1, 1, 2)] for n in range(2)]

    def send_rows(r):
        for copy in row_swaps(r):
            copy.start()

    def start_cross(n, way):
        lines[n].arrived(way, 1)
        crosses[n][1 + way].start()

    def start_far(n):
        for way in range(2):
            lines[n].arrived(way, 2)
        crosses[n][3].start()

    def start_keys(n):
        lines[n].start()
        crosses[n][0].start()

    gz[0].start()
    send_rows(2)
    send_rows(1)
    start_keys(0)
    send_rows(3)
    for src, dst in rows_copies(0) + rows_copies(1):
        pltpu.make_async_copy(src, dst, local.at[0]).start()
    for n, source in enumerate((k_ref, v_ref)):
        pltpu.make_async_copy(source.at[:, ours], keys_out.at[0, y, x, n], local.at[1]).start()
    for copy in swaps:
        copy.wait_recv()
    start_keys(1)

    for copy in loads:
        copy.wait()
    for quarter in range(QUARTERS):
        for k in range(PART):
            cols = slice((quarter * PART + k) * D, (quarter * PART + k + 1) * D)
            product = g_vmem[:, cols].astype(F32) * o_vmem[:, cols].astype(F32)
            parts[quarter, :, k * B : (k + 1) * B] = jnp.sum(
                jnp.transpose(product), axis=0, keepdims=True
            )

    def delta_copy(r):
        return pltpu.make_async_remote_copy(
            src_ref=parts.at[place.quarter(r)],
            dst_ref=delta_ref.at[z, place.quarter(0)],
            send_sem=d_send.at[r],
            recv_sem=d_recv.at[r],
            device_id=place.square(r),
            device_id_type=MESH,
        )

    def swapped_delta(r):
        ref = delta_ref.at[z, place.quarter(r)]
        return pltpu.make_async_remote_copy(
            src_ref=ref,
            dst_ref=ref,
            send_sem=d_send.at[r],
            recv_sem=d_recv.at[r],
            device_id=place.square(r),
            device_id_type=MESH,
        )

    def delta_line(step, at):
        return pltpu.make_async_remote_copy(
            src_ref=delta_ref.at[at],
            dst_ref=delta_ref.at[at],
            send_sem=dz_send.at[step - 1],
            recv_sem=dz_recv.at[step - 1],
            device_id=place.along("z", step),
            device_id_type=MESH,
        )

    for r in (1, 2, 3):
        delta_copy(r).start()
    delta_ref[z, place.quarter(0)] = parts[place.quarter(0)]
    pass_rows(2)
    pass_rows(1)
    gz[0].forward()
    lines[0].forward()
    start_cross(0, 0)
    start_cross(0, 1)

    meta, mine, diagonal = tile_lists(place, qb, kb, kept)
    meta_ref[...] = meta
    code, count = early_tasks(mine, diagonal)
    sub = lax.broadcasted_iota(jnp.int32, (8, 128), 0)
    list_ref[...] = jnp.where(sub == 0, code, count).astype(jnp.int32)

    lines[1].forward()
    start_cross(1, 0)
    start_cross(1, 1)
    pass_rows(3)
    for n in range(2):
        crosses[n][0].forward()
    for n in range(2):
        start_far(n)
    gz[2].forward()
    gz[1].forward()
    for n in range(2):
        crosses[n][1].forward()
        crosses[n][2].forward()
    gz[3].forward()
    for n in range(2):
        crosses[n][3].forward()
    for r in (1, 2, 3):
        swapped_delta(r).wait_recv()
    for step in (1, 2, 3):
        delta_line(step, z).start()

    for n in range(2):
        for ring in crosses[n]:
            ring.finish()
    for ring in gz:
        ring.finish()
    for n, ref in enumerate((rows_out.at[z, place.quarter(0)], keys_out.at[0, y, x])):
        pltpu.make_async_copy(ref, ref, local.at[n]).wait()
    for copy in swaps:
        copy.wait_send()
    for r in (1, 2, 3):
        swapped(r).wait_send()
        swapped_delta(r).wait_send()
    for step in (1, 2, 3):
        delta_line(step, z).wait_send()
        delta_line(step, ring_at(z, -step)).wait_recv()
    for ring in gz + lines + crosses[0] + crosses[1]:
        ring.sent()


def in_hbm(*arrays):
    return [pltpu.with_memory_space_constraint(a, pltpu.HBM) for a in arrays]


def gather(qb, kb, kept, q, k, v, o, g):
    return pl.pallas_call(
        gather_kernel,
        out_shape=(
            pltpu.VMEM((RING, QUARTERS, 2, PART, B, D), BF),
            pltpu.VMEM((2, RING, RING, 2, B, D), BF),
            pltpu.VMEM((RING, QUARTERS, 1, COLS), F32),
            pltpu.VMEM((LOCAL_ROWS, 128), jnp.int32),
            pltpu.VMEM((8, 128), jnp.int32),
        ),
        in_specs=[HBM] * 8,
        out_specs=(ANY, ANY, VMEM, VMEM, VMEM),
        scratch_shapes=[
            pltpu.SMEM((64,), jnp.int32),
            pltpu.SMEM((128,), jnp.int32),
            pltpu.VMEM((64, 64), jnp.int32),
            pltpu.VMEM((B, HEADS * D), BF),
            pltpu.VMEM((B, HEADS * D), BF),
            pltpu.VMEM((QUARTERS, 1, COLS), F32),
            pltpu.SemaphoreType.DMA((5,)),
            pltpu.SemaphoreType.DMA((2,)),
            pltpu.SemaphoreType.DMA((2,)),
            pltpu.SemaphoreType.DMA((2,)),
            pltpu.SemaphoreType.DMA((QUARTERS,)),
            pltpu.SemaphoreType.DMA((QUARTERS,)),
            pltpu.SemaphoreType.DMA((QUARTERS,)),
            pltpu.SemaphoreType.DMA((QUARTERS,)),
            pltpu.SemaphoreType.DMA((3,)),
            pltpu.SemaphoreType.DMA((3,)),
            pltpu.SemaphoreType.DMA((QUARTERS,)),
            pltpu.SemaphoreType.DMA((QUARTERS, 6)),
            pltpu.SemaphoreType.DMA((2, 1 + RING)),
            pltpu.SemaphoreType.DMA((2, 1 + RING, 6)),
        ],
        compiler_params=pltpu.CompilerParams(
            collective_id=0, has_side_effects=True, vmem_limit_bytes=8 * 2**20
        ),
        name="gather",
    )(*in_hbm(qb, kb, kept, q, k, v, o, g))


def across(a, b):
    return lax.dot_general(a, b, (((1,), (1,)), ((), ())), preferred_element_type=F32)


def fill_bias(bias_ref):
    keys = lax.broadcasted_iota(jnp.int32, (B, COLS), 0)
    rows = lax.rem(lax.broadcasted_iota(jnp.int32, (B, COLS), 1), B)
    bias_ref[0] = jnp.full((B, COLS), MASKED, F32)
    bias_ref[1] = jnp.where(keys <= rows, 0.0, MASKED)
    bias_ref[2] = jnp.zeros((B, COLS), F32)


def pop(bits, diagonal):
    j = (31 - lax.clz(bits)) & 31
    kind = jnp.where(bits == 0, 0, jnp.where(j == diagonal, 1, 2))
    return j, bits & ~lax.shift_left(jnp.int32(1), j), kind


def list_tasks(meta_ref, task_ref):
    def row(i, count):
        diagonal = meta_ref[i, 1]

        def more(state):
            return state[0] != 0

        def step(state):
            bits, count = state
            j0, bits, kind0 = pop(bits, diagonal)
            j1, bits, kind1 = pop(bits, diagonal)
            task_ref[count] = i + j0 * 16 + j1 * 512 + kind0 * 16384 + kind1 * 65536
            return bits, count + 1

        return lax.while_loop(more, step, (meta_ref[i, 0], count))[1]

    count = lax.fori_loop(0, LOCAL_ROWS, row, jnp.int32(0))
    for n in range(GROUP - 1):
        task_ref[count + n] = 0
    task_ref[TASKS - 1] = (count + GROUP - 1) // GROUP


def read_task(task_ref, n):
    e = task_ref[n]
    return (
        e & 15,
        (e // 16) & 31,
        (e // 512) & 31,
        (e // 16384) & 3,
        (e // 65536) & 3,
    )


def take_tasks(meta_ref, list_ref, task_ref):
    count = list_ref[1, 0]

    @pl.when(count <= EARLY)
    def _():
        for n in range(EARLY):
            task_ref[n] = list_ref[0, n]
        task_ref[TASKS - 1] = (count + GROUP - 1) // GROUP

    @pl.when(count > EARLY)
    def _():
        list_tasks(meta_ref, task_ref)


def stats_kernel(meta_ref, list_ref, rows_ref, keys_ref, st_ref, task_ref, m_ref, l_ref, bias_ref):
    take_tasks(meta_ref, list_ref, task_ref)
    fill_bias(bias_ref)
    m_ref[...] = jnp.full_like(m_ref, NEG)
    l_ref[...] = jnp.zeros_like(l_ref)

    def group(n, _):
        results = []
        for t in range(GROUP):
            i, j0, j1, kind0, kind1 = read_task(task_ref, GROUP * n + t)
            queries = rows_ref[i, 0].reshape(COLS, D)
            keys = jnp.concatenate([keys_ref[j0, 0], keys_ref[j1, 0]], axis=0)
            s = across(keys, queries) * C2
            s = jnp.concatenate([s[:B] + bias_ref[kind0], s[B:] + bias_ref[kind1]], axis=0)
            s = s.reshape(2 * B // 8, 8, COLS)
            m = jnp.max(s, axis=0)
            results.append((i, m, jnp.sum(jnp.exp2(s - m[None]), axis=0)))
        for i, m, l in results:
            old = m_ref[i]
            new = jnp.maximum(old, m)
            m_ref[i] = new
            l_ref[i] = l_ref[i] * jnp.exp2(old - new) + l * jnp.exp2(m - new)
        return 0

    lax.fori_loop(0, task_ref[TASKS - 1], group, 0)
    m8 = m_ref[...]
    m = jnp.max(m8, axis=1, keepdims=True)
    st_ref[0] = m
    st_ref[1] = jnp.sum(l_ref[...] * jnp.exp2(m8 - m), axis=1, keepdims=True)


def statistics(meta, lists, rows, keys):
    return pl.pallas_call(
        stats_kernel,
        out_shape=pltpu.VMEM((2, LOCAL_ROWS, 1, COLS), F32),
        in_specs=[SMEM, SMEM, VMEM, VMEM],
        out_specs=VMEM,
        scratch_shapes=[
            pltpu.SMEM((TASKS,), jnp.int32),
            pltpu.VMEM((LOCAL_ROWS, 8, COLS), F32),
            pltpu.VMEM((LOCAL_ROWS, 8, COLS), F32),
            pltpu.VMEM((3, B, COLS), F32),
        ],
        compiler_params=pltpu.CompilerParams(vmem_limit_bytes=24 * 2**20),
        name="statistics",
    )(meta, lists, rows, keys)


def merge_statistics(st, sts, total_ref):
    top = st[0]
    for n in range(3):
        top = jnp.maximum(top, sts[n, 0])
    total = st[1] * jnp.exp2(st[0] - top)
    for n in range(3):
        total = total + sts[n, 1] * jnp.exp2(sts[n, 0] - top)
    total_ref[...] = top + jnp.log2(total)


def exchange_kernel(st_ref, total_ref, sts, st_send, st_recv):
    place = Place()
    greet([place.along("z", step) for step in (1, 2, 3)])
    copies = [
        pltpu.make_async_remote_copy(
            src_ref=st_ref,
            dst_ref=sts.at[step - 1],
            send_sem=st_send.at[step - 1],
            recv_sem=st_recv.at[step - 1],
            device_id=place.along("z", step),
            device_id_type=MESH,
        )
        for step in (1, 2, 3)
    ]
    for copy in copies:
        copy.start()
    for copy in copies:
        copy.wait()
    merge_statistics(st_ref, sts, total_ref)


def exchange(st):
    return pl.pallas_call(
        exchange_kernel,
        out_shape=pltpu.VMEM((LOCAL_ROWS, 1, COLS), F32),
        in_specs=[VMEM],
        out_specs=VMEM,
        scratch_shapes=[
            pltpu.VMEM((3, 2, LOCAL_ROWS, 1, COLS), F32),
            pltpu.SemaphoreType.DMA((3,)),
            pltpu.SemaphoreType.DMA((3,)),
        ],
        compiler_params=pltpu.CompilerParams(
            collective_id=1, has_side_effects=True, vmem_limit_bytes=8 * 2**20
        ),
        name="exchange",
    )(st)


def grads_kernel(
    meta_ref, list_ref, rows_ref, keys_ref, total_ref, delta_ref, dq_ref, dkv_ref,
    task_ref, dq_acc, dk_acc, dv_acc, bias_ref, p_ref, ds_ref,
):
    take_tasks(meta_ref, list_ref, task_ref)
    fill_bias(bias_ref)
    dq_acc[...] = jnp.zeros_like(dq_acc)
    dk_acc[...] = jnp.zeros_like(dk_acc)
    dv_acc[...] = jnp.zeros_like(dv_acc)

    def group(n, _):
        tasks = [read_task(task_ref, GROUP * n + t) for t in range(GROUP)]
        for t, (i, j0, j1, kind0, kind1) in enumerate(tasks):
            keys = jnp.concatenate([keys_ref[j0, 0], keys_ref[j1, 0]], axis=0)
            values = jnp.concatenate([keys_ref[j0, 1], keys_ref[j1, 1]], axis=0)
            s = across(keys, rows_ref[i, 0].reshape(COLS, D)) * C2 - total_ref[i]
            s = jnp.concatenate([s[:B] + bias_ref[kind0], s[B:] + bias_ref[kind1]], axis=0)
            p = jnp.exp2(s)
            p_ref[t] = p.astype(BF)
            dp = across(values, rows_ref[i, 1].reshape(COLS, D))
            ds_ref[t] = (p * (dp - delta_ref[i])).astype(BF)
        for t, (i, j0, j1, _, _) in enumerate(tasks):
            keys = jnp.concatenate([keys_ref[j0, 0], keys_ref[j1, 0]], axis=0)
            ds = ds_ref[t]
            dv = jnp.dot(p_ref[t], rows_ref[i, 1].reshape(COLS, D), preferred_element_type=F32)
            dk = jnp.dot(ds, rows_ref[i, 0].reshape(COLS, D), preferred_element_type=F32)
            dq_acc[i] += jnp.dot(jnp.transpose(keys), ds, preferred_element_type=F32)
            dk_acc[j0] += dk[:B]
            dk_acc[j1] += dk[B:]
            dv_acc[j0] += dv[:B]
            dv_acc[j1] += dv[B:]
        return 0

    lax.fori_loop(0, task_ref[TASKS - 1], group, 0)

    def write(j, _):
        dkv_ref[j, 0] = (dk_acc[j] * SCALE).astype(BF)
        dkv_ref[j, 1] = dv_acc[j].astype(BF)
        return 0

    lax.fori_loop(0, LOCAL_KEYS, write, 0, unroll=8)

    def write_rows(i, _):
        for k in range(PART):
            dq_ref[i, k] = (dq_acc[i, :, k * B : (k + 1) * B] * SCALE).astype(BF)
        return 0

    lax.fori_loop(0, LOCAL_ROWS, write_rows, 0, unroll=8)


def grads(meta, lists, rows, keys, total, delta):
    return pl.pallas_call(
        grads_kernel,
        out_shape=(
            pltpu.VMEM((LOCAL_ROWS, PART, D, B), BF),
            pltpu.VMEM((LOCAL_KEYS, 2, B, D), BF),
        ),
        in_specs=[SMEM, SMEM] + [VMEM] * 4,
        out_specs=(VMEM, VMEM),
        scratch_shapes=[
            pltpu.SMEM((TASKS,), jnp.int32),
            pltpu.VMEM((LOCAL_ROWS, D, COLS), F32),
            pltpu.VMEM((LOCAL_KEYS, B, D), F32),
            pltpu.VMEM((LOCAL_KEYS, B, D), F32),
            pltpu.VMEM((3, B, COLS), F32),
            pltpu.VMEM((GROUP, 2 * B, COLS), BF),
            pltpu.VMEM((GROUP, 2 * B, COLS), BF),
        ],
        compiler_params=pltpu.CompilerParams(vmem_limit_bytes=32 * 2**20),
        name="grads",
    )(meta, lists, rows, keys, total, delta)


class Scatter:
    def __init__(self, place, axis, part, near, far, mid, six, send, recv):
        self.me = getattr(place, axis)
        self.to = (place.along(axis, 1), place.along(axis, -1))
        self.part, self.near, self.far, self.mid, self.six = part, near, far, mid, six
        self.send, self.recv = send, recv

    def copy(self, src, dst, way, k):
        return pltpu.make_async_remote_copy(
            src_ref=src,
            dst_ref=dst,
            send_sem=self.send,
            recv_sem=self.recv.at[way * 3 + k],
            device_id=self.to[way],
            device_id_type=MESH,
        )

    def far_copy(self, way):
        return self.copy(self.part(ring_at(self.me, 2), way), self.far.at[way], way, 0)

    def plain_copy(self, way):
        step = 1 if way == 0 else -1
        return self.copy(
            self.part(ring_at(self.me, step), 1 - way), self.near.at[way, 1 - way], way, 1
        )

    def mid_copy(self, way):
        return self.copy(self.mid.at[way], self.near.at[way, way], way, 2)

    def start_far(self):
        for way in range(2):
            self.far_copy(way).start()

    def start_plain(self, way):
        self.plain_copy(way).start()

    def forward(self):
        for way in range(2):
            step = 1 if way == 0 else -1
            self.far_copy(way).wait_recv()
            own = self.part(ring_at(self.me, step), way)[...].astype(F32)
            self.mid[way] = (self.far[way].astype(F32) + own).astype(BF)
            self.mid_copy(way).start()

    def finish(self):
        for way in range(2):
            self.plain_copy(way).wait_recv()
        for way in range(2):
            self.mid_copy(way).wait_recv()

    def total(self, half, own=None):
        own = self.part(self.me, half)[...].astype(F32) if own is None else own
        return own + self.near[0, half].astype(F32) + self.near[1, half].astype(F32)

    def sent(self):
        self.copy(self.six, self.six, 0, 0).wait_send()


STEPS = (2, -1, 1, 0)
MEMBERS = (3, 2, 1, 0)
ORDER = (
    "c10P0", "c00F", "c01P1", "c10F", "r0F", "c12F", "r3P1", "r1P0", "c11F",
    "c01F", "r1P1", "r0P1", "r3F", "c00P0", "c11P0", "c10P1", "c00P1", "c03F",
    "c12P1", "c02F", "r0P0", "c00W", "c10W", "r3P0", "r2F", "c02P0", "c01P0",
    "c12P0", "c11P1", "c12W", "c13P1", "c11W", "r0W", "r2P0", "r1F", "r2P1",
    "c01W", "c10E", "l1F", "c13F", "r2W", "c02W", "c00E", "l0F", "c02P1",
    "c03W", "r0E", "c03P1", "r3W", "c01E", "l0P1", "c12E", "r1W", "l1P0",
    "c11E", "l1W", "c13W", "c13P0", "c02E", "l0P0", "c03P0", "l0W", "l1P1",
    "r1E", "r2E", "c13E", "l1E", "r3E", "c03E", "l0E",
)


def scatter_kernel(
    dq_ref, dkv_ref, qg_ref, kg_ref, vg_ref,
    zn, zf, zm, cn, cf, cm, ln, lf, lm, sums, own_sum, fin, qout,
    zs, zr, cs, cr, ls, lr, swap_send, swap_recv, q_send, q_recv, local,
):
    place = Place()
    h, x, y, z = place.h, place.x, place.y, place.z
    greet(place.around())

    def row_ring(k):
        number = place.quarter(MEMBERS[k])
        part = lambda at, half: dq_ref.at[at, number, half]
        return Scatter(place, "z", part, zn.at[k], zf.at[k], zm.at[k], dq_ref.at[0, 0:3], zs.at[k], zr.at[k])

    def cross(n, k):
        spot = ring_at((x, y)[n], STEPS[k])
        part = lambda at, half: dkv_ref.at[n, at, spot, half]
        return Scatter(
            place, "yx"[n], part, cn.at[n, k], cf.at[n, k], cm.at[n, k], dkv_ref.at[n, 0, 0:3],
            cs.at[n, k], cr.at[n, k],
        )

    def line(n):
        part = lambda at, half: sums.at[n, at, half]
        return Scatter(place, "xy"[n], part, ln.at[n], lf.at[n], lm.at[n], sums.at[n, 0:3], ls.at[n], lr.at[n])

    rows = [row_ring(k) for k in range(RING)]
    crosses = [[cross(n, k) for k in range(RING)] for n in range(2)]
    lines = [line(n) for n in range(2)]
    part_cols = pl.ds(pl.multiple_of(place.quarter(0) * COLS, COLS), COLS)

    def q_copy(k):
        r = MEMBERS[k]
        return pltpu.make_async_remote_copy(
            src_ref=qout.at[k],
            dst_ref=qg_ref.at[:, part_cols],
            send_sem=q_send.at[r],
            recv_sem=q_recv.at[r],
            device_id=place.square(r),
            device_id_type=MESH,
        )

    q_own = pltpu.make_async_copy(qout.at[RING - 1], qg_ref.at[:, part_cols], local.at[0])
    ours = pl.ds(pl.multiple_of(h * D, D), D)
    theirs = pl.ds(pl.multiple_of((1 - h) * D, D), D)
    swaps = [
        pltpu.make_async_remote_copy(
            src_ref=fin.at[1, n],
            dst_ref=target.at[:, ours],
            send_sem=swap_send.at[n],
            recv_sem=swap_recv.at[n],
            device_id=place.partner(),
            device_id_type=MESH,
        )
        for n, target in enumerate((kg_ref, vg_ref))
    ]
    outs = [
        pltpu.make_async_copy(fin.at[0, n], target.at[:, ours], local.at[1 + n])
        for n, target in enumerate((kg_ref, vg_ref))
    ]
    def end_rows(k):
        rows[k].finish()
        for half in range(PART):
            qout[k, :, half * D : (half + 1) * D] = jnp.transpose(rows[k].total(half)).astype(BF)
        if MEMBERS[k]:
            q_copy(k).start()
        else:
            q_own.start()

    def end_cross(n, k):
        ring = crosses[n][k]
        ring.finish()
        for half in range(2):
            total = ring.total(half)
            if STEPS[k] == 0:
                own_sum[n, half] = total
            else:
                sums[n, ring_at((x, y)[n], STEPS[k]), half] = total.astype(BF)

    def end_line(n):
        lines[n].finish()
        for half in range(2):
            fin[n, half] = lines[n].total(half, own_sum[n, half]).astype(BF)
        for copy in (outs, swaps)[n]:
            copy.start()

    for step in ORDER:
        at = [int(c) for c in step if c.isdigit()]
        kind, action = step[0], next(c for c in step if c in "FPWE")
        ring = {"r": lambda: rows[at[0]], "c": lambda: crosses[at[0]][at[1]], "l": lambda: lines[at[0]]}[kind]()
        if action == "F":
            ring.start_far()
        elif action == "P":
            ring.start_plain(at[-1])
        elif action == "W":
            ring.forward()
        else:
            {"r": end_rows, "c": end_cross, "l": end_line}[kind](*at)
    for copy in outs:
        copy.wait()
    q_own.wait()
    for n, target in enumerate((kg_ref, vg_ref)):
        swaps[n].wait_send()
        ref = target.at[:, theirs]
        pltpu.make_async_remote_copy(
            src_ref=ref,
            dst_ref=ref,
            send_sem=swap_send.at[n],
            recv_sem=swap_recv.at[n],
            device_id=place.partner(),
            device_id_type=MESH,
        ).wait_recv()
    for k in range(RING - 1):
        q_copy(k).wait_send()
        r = MEMBERS[k]
        ref = qg_ref.at[:, pl.ds(pl.multiple_of(place.quarter(r) * COLS, COLS), COLS)]
        pltpu.make_async_remote_copy(
            src_ref=ref,
            dst_ref=ref,
            send_sem=q_send.at[r],
            recv_sem=q_recv.at[r],
            device_id=place.square(r),
            device_id_type=MESH,
        ).wait_recv()
    for ring in rows + crosses[0] + crosses[1] + lines:
        ring.sent()


def scatter(dq, dkv):
    def ring_scratch(*rings):
        return [
            pltpu.VMEM(rings + (2, 2, B, D), BF),
            pltpu.VMEM(rings + (2, B, D), BF),
            pltpu.VMEM(rings + (2, B, D), BF),
        ]

    def ring_semaphores(*rings):
        return [pltpu.SemaphoreType.DMA(rings), pltpu.SemaphoreType.DMA(rings + (6,))]

    return pl.pallas_call(
        scatter_kernel,
        out_shape=(
            pltpu.VMEM((B, HEADS * D), BF),
            pltpu.VMEM((B, 2 * D), BF),
            pltpu.VMEM((B, 2 * D), BF),
        ),
        in_specs=[VMEM, VMEM],
        out_specs=(VMEM, VMEM, VMEM),
        scratch_shapes=ring_scratch(RING)
        + ring_scratch(2, RING)
        + ring_scratch(2)
        + [
            pltpu.VMEM((2, RING, 2, B, D), BF),
            pltpu.VMEM((2, 2, B, D), F32),
            pltpu.VMEM((2, 2, B, D), BF),
            pltpu.VMEM((QUARTERS, B, COLS), BF),
        ]
        + ring_semaphores(RING)
        + ring_semaphores(2, RING)
        + ring_semaphores(2)
        + [
            pltpu.SemaphoreType.DMA((2,)),
            pltpu.SemaphoreType.DMA((2,)),
            pltpu.SemaphoreType.DMA((QUARTERS,)),
            pltpu.SemaphoreType.DMA((QUARTERS,)),
            pltpu.SemaphoreType.DMA((3,)),
        ],
        compiler_params=pltpu.CompilerParams(
            collective_id=2, has_side_effects=True, vmem_limit_bytes=24 * 2**20
        ),
        name="scatter",
    )(dq.reshape(RING, QUARTERS, PART, D, B), dkv.reshape(2, RING, RING, 2, B, D))


def store_kernel(q_ref, k_ref, v_ref, qg_ref, kg_ref, vg_ref, sems):
    copies = [
        pltpu.make_async_copy(src, dst, sems.at[n])
        for n, (src, dst) in enumerate(((q_ref, qg_ref), (k_ref, kg_ref), (v_ref, vg_ref)))
    ]
    for copy in copies:
        copy.start()
    for copy in copies:
        copy.wait()


def store(*results):
    return pl.pallas_call(
        store_kernel,
        out_shape=tuple(pltpu.HBM(r.shape, r.dtype) for r in results),
        in_specs=[VMEM] * 3,
        out_specs=(HBM,) * 3,
        scratch_shapes=[pltpu.SemaphoreType.DMA((3,))],
        compiler_params=pltpu.CompilerParams(vmem_limit_bytes=4 * 2**20),
        name="store",
    )(*results)


def body(q, k, v, o, g, query_blocks, key_blocks, kept_blocks):
    rows, keys, delta, meta, lists = gather(query_blocks, key_blocks, kept_blocks, q, k, v, o, g)
    rows = rows.reshape(LOCAL_ROWS, 2, PART, B, D)
    keys = keys.reshape(LOCAL_KEYS, 2, B, D)
    total = exchange(statistics(meta, lists, rows, keys))
    dq, dkv = grads(meta, lists, rows, keys, total, delta.reshape(LOCAL_ROWS, 1, COLS))
    return store(*scatter(dq, dkv))


def solution(mesh):
    rows, stored = P(("inner", "outer"), "head"), P(("head", "inner", "outer"), None)
    return jax.shard_map(
        body,
        mesh=mesh,
        in_specs=(rows, stored, stored, rows, rows, P(), P(), P()),
        out_specs=(rows, stored, stored),
        check_vma=False,
    )
```

```python
import math

import jax
import jax.numpy as jnp
from jax import lax
from jax.experimental import pallas as pl
from jax.experimental.pallas import tpu as pltpu
from jax.sharding import PartitionSpec as P

HEADS = 8
D = 128
B = 128
RING = 4
QUARTERS = 4
PART = 2
COLS = PART * B
LOCAL_ROWS = 16
LOCAL_KEYS = 32
ENTRIES = 64
GROUP = 8
TASKS = 272
EARLY = 64
FIRST_KEY = 64
SCALE = 1.0 / math.sqrt(D)
LOG2E = math.log2(math.e)
C2 = SCALE * LOG2E
NEG = -1e30
MASKED = -2e30
MESH = pl.DeviceIdType.MESH
ANY = pl.BlockSpec(memory_space=pl.ANY)
HBM = pl.BlockSpec(memory_space=pltpu.HBM)
VMEM = pl.BlockSpec(memory_space=pltpu.VMEM)
SMEM = pl.BlockSpec(memory_space=pltpu.SMEM)
BF = jnp.bfloat16
F32 = jnp.float32


class Place:
    def __init__(self):
        self.h = lax.axis_index("head")
        inner, outer = lax.axis_index("inner"), lax.axis_index("outer")
        self.x, self.z = lax.rem(outer, 4), lax.rem(inner, 4)
        self.y = (inner // 4) * 2 + outer // 4

    def device(self, x=None, y=None, z=None, h=None):
        x, y, z, h = (
            own if new is None else new
            for own, new in ((self.x, x), (self.y, y), (self.z, z), (self.h, h))
        )
        return (h, (y // 2) * 4 + z, lax.rem(y, 2) * 4 + x)

    def along(self, axis, step):
        at = lax.rem(getattr(self, axis) + step + RING, RING)
        return self.device(**{axis: at})

    def partner(self):
        return self.device(h=1 - self.h)

    def quarter(self, r):
        b, a = lax.rem(self.y, 2), lax.rem(self.x, 2)
        b, a = (1 - b if r & 2 else b), (1 - a if r & 1 else a)
        return 2 * b + a

    def square(self, r):
        b, a = lax.rem(self.y, 2), lax.rem(self.x, 2)
        y = self.y + 1 - 2 * b if r & 2 else self.y
        x = self.x + 1 - 2 * a if r & 1 else self.x
        return self.device(x=x, y=y)

    def around(self):
        near = [self.along(a, s) for a in ("x", "y", "z") for s in (1, -1)]
        return near + [self.partner(), self.square(3)]


def ring_at(me, step):
    return lax.rem(me + step + RING, RING)


def greet(devices):
    barrier = pltpu.get_barrier_semaphore()
    for device in devices:
        pl.semaphore_signal(barrier, inc=1, device_id=device, device_id_type=MESH)
    pl.semaphore_wait(barrier, len(devices))


class Gather:
    def __init__(self, place, axis, part, own, six, send, recv):
        self.me = getattr(place, axis)
        self.to = (place.along(axis, 1), place.along(axis, -1))
        self.part, self.own, self.six, self.send, self.recv = part, own, six, send, recv

    def copy(self, src, dst, way, k):
        return pltpu.make_async_remote_copy(
            src_ref=src,
            dst_ref=dst,
            send_sem=self.send,
            recv_sem=self.recv.at[way * 3 + k],
            device_id=self.to[way],
            device_id_type=MESH,
        )

    def start(self):
        for k in range(2):
            for way in range(2):
                for src, dst in self.own(k ^ way):
                    self.copy(src, dst, way, k).start()

    def whole(self, at, half, way, k):
        ref = self.part(at, half)
        return self.copy(ref, ref, way, k)

    def arrived(self, way, k):
        step = (-1 if way == 0 else 1) * (2 if k == 2 else 1)
        half = way if k == 2 else k ^ way
        self.whole(ring_at(self.me, step), half, way, k).wait_recv()

    def forward(self):
        for way in range(2):
            self.arrived(way, 0)
            step = -1 if way == 0 else 1
            self.whole(ring_at(self.me, step), way, way, 2).start()

    def finish(self):
        for way in range(2):
            self.arrived(way, 1)
        for way in range(2):
            self.arrived(way, 2)

    def sent(self):
        self.copy(self.six, self.six, 0, 0).wait_send()


def key_slot(place, j):
    n, a, b = j // 16, lax.rem(j // 4, 4), lax.rem(j, 4)
    owner = jnp.where(n == 0, place.h, 1 - place.h)
    yy, xx = jnp.where(n == 0, a, b), jnp.where(n == 0, b, a)
    return owner * 64 + (yy // 2) * 32 + place.z * 8 + lax.rem(yy, 2) * 4 + xx


def row_slot(place, i):
    zz, b, a = i // 4, lax.rem(i // 2, 2), lax.rem(i, 2)
    return (place.y // 2) * 32 + zz * 8 + b * 4 + (place.x // 2) * 2 + a


def tile_lists(place, qb_ref, kb_ref, kept):
    lanes = lax.broadcasted_iota(jnp.int32, (1, 128), 1)
    subs = lax.broadcasted_iota(jnp.int32, (LOCAL_ROWS, 1), 0)

    def key_step(j, row):
        return jnp.where(lanes == j, kb_ref[key_slot(place, j)], row)

    def row_step(i, column):
        return jnp.where(subs == i, qb_ref[row_slot(place, i)], column)

    key_pos = lax.fori_loop(0, LOCAL_KEYS, key_step, jnp.full((1, 128), -7, jnp.int32))
    row_pos = lax.fori_loop(0, LOCAL_ROWS, row_step, jnp.zeros((LOCAL_ROWS, 1), jnp.int32))
    wide = lax.broadcasted_iota(jnp.int32, (64, 128), 1)
    listed = jnp.zeros((64, 128), F32)
    for e in range(ENTRIES):
        listed = jnp.where(kept[:, e : e + 1] == wide, 1.0, listed)
    rows_of = (row_pos == lax.broadcasted_iota(jnp.int32, (LOCAL_ROWS, 64), 1)).astype(F32)
    keys_of = (key_pos == lax.broadcasted_iota(jnp.int32, (128, 128), 0)).astype(F32)
    mine = jnp.dot(
        jnp.dot(rows_of.astype(BF), listed.astype(BF), preferred_element_type=F32).astype(BF),
        keys_of.astype(BF),
        preferred_element_type=F32,
    )
    lane16 = lax.broadcasted_iota(jnp.int32, (LOCAL_ROWS, 128), 1)
    weight = lax.shift_left(jnp.ones_like(lane16), lax.rem(lane16, 16)).astype(F32)
    low = jnp.sum(jnp.where(lane16 < 16, mine * weight, 0.0), axis=1, keepdims=True)
    high = jnp.sum(
        jnp.where((lane16 >= 16) & (lane16 < 32), mine * weight, 0.0), axis=1, keepdims=True
    )
    bits = low.astype(jnp.int32) + lax.shift_left(
        high.astype(jnp.int32), jnp.full((LOCAL_ROWS, 1), 16, jnp.int32)
    )
    on = (key_pos == row_pos + FIRST_KEY).astype(F32)
    diagonal = jnp.sum(on * (lane16 - 99).astype(F32), axis=1, keepdims=True) + 99.0
    meta = jnp.where(lane16 == 0, bits, diagonal.astype(jnp.int32))
    return meta, mine, diagonal


def halves_up(count):
    return lax.shift_right_logical(
        count.astype(jnp.int32) + 1, jnp.ones(count.shape, jnp.int32)
    ).astype(F32)


def exact(a, b, dims=(((1,), (0,)), ((), ()))):
    return lax.dot_general(a.astype(BF), b.astype(BF), dims, preferred_element_type=F32)


def early_tasks(mine, diagonal):
    sub = lax.broadcasted_iota(jnp.int32, (LOCAL_ROWS, 128), 0)
    lane = lax.broadcasted_iota(jnp.int32, (LOCAL_ROWS, 128), 1)
    count = jnp.broadcast_to(jnp.sum(mine, axis=1, keepdims=True), (LOCAL_ROWS, 128))
    tasks = halves_up(count)
    before = (
        lax.broadcasted_iota(jnp.int32, (LOCAL_ROWS, LOCAL_ROWS), 1)
        < lax.broadcasted_iota(jnp.int32, (LOCAL_ROWS, LOCAL_ROWS), 0)
    ).astype(F32)
    start = exact(before, tasks)
    at = lane.astype(F32)
    chosen = ((start <= at) & (at < start + tasks)).astype(F32)

    def of_row(column):
        return jnp.sum(chosen * column, axis=0, keepdims=True)

    row, first, diag = of_row(sub.astype(F32)), of_row(start), of_row(diagonal)
    lower = (
        lax.broadcasted_iota(jnp.int32, (128, 128), 0)
        < lax.broadcasted_iota(jnp.int32, (128, 128), 1)
    ).astype(F32)
    rank = exact(mine, lower)
    down = (((0,), (0,)), ((), ()))
    mine_t, rank_t = exact(mine, chosen, down), exact(rank, chosen, down)
    block = lax.broadcasted_iota(jnp.int32, (128, 128), 0).astype(F32)
    code = row
    for k in range(2):
        here = mine_t * (rank_t == 2.0 * (at[:1] - first) + k).astype(F32)
        j = jnp.sum(here * block, axis=0, keepdims=True)
        valid = jnp.sum(here, axis=0, keepdims=True)
        kind = valid * jnp.where(j == diag, 1.0, 2.0)
        code = code + j * (16.0, 512.0)[k] + kind * (16384.0, 65536.0)[k]
    return code, jnp.sum(tasks, axis=0, keepdims=True)


def gather_kernel(
    qb_hbm, kb_hbm, kept_hbm, q_ref, k_ref, v_ref, o_ref, g_ref,
    rows_out, keys_out, delta_ref, meta_ref, list_ref,
    qb, kb, kept, o_vmem, g_vmem, parts,
    load, local, swap_send, swap_recv, s_send, s_recv, d_send, d_recv, dz_send, dz_recv, zs, zr, cs, cr,
):
    place = Place()
    h, x, y, z = place.h, place.x, place.y, place.z
    pairs = ((o_ref, o_vmem), (g_ref, g_vmem), (kept_hbm, kept), (qb_hbm, qb), (kb_hbm, kb))
    loads = [pltpu.make_async_copy(src, dst, load.at[n]) for n, (src, dst) in enumerate(pairs)]
    for copy in loads:
        copy.start()
    greet(place.around() + [place.along("z", 2)])
    ours = pl.ds(pl.multiple_of(h * D, D), D)
    theirs = pl.ds(pl.multiple_of((1 - h) * D, D), D)

    swaps = [
        pltpu.make_async_remote_copy(
            src_ref=source.at[:, theirs],
            dst_ref=keys_out.at[1, x, y, n],
            send_sem=swap_send.at[n],
            recv_sem=swap_recv.at[n],
            device_id=place.partner(),
            device_id_type=MESH,
        )
        for n, source in enumerate((k_ref, v_ref))
    ]
    for copy in swaps:
        copy.start()

    def head(half, quarter, k):
        source = (q_ref, g_ref)[half]
        return source.at[:, pl.ds(pl.multiple_of((quarter * PART + k) * D, D), D)]

    def rows_copies(half):
        mine = place.quarter(0)
        return [(head(half, mine, k), rows_out.at[z, mine, half, k]) for k in range(PART)]

    def row_ring(r):
        part = lambda at, half: rows_out.at[at, place.quarter(r), half]
        own = rows_copies if r == 0 else lambda half: [(part(z, half),) * 2]
        return Gather(place, "z", part, own, rows_out.at[0, 0:3], zs.at[r], zr.at[r])

    gz = [row_ring(r) for r in range(QUARTERS)]

    def row_swaps(r):
        return [
            pltpu.make_async_remote_copy(
                src_ref=head(half, place.quarter(r), k),
                dst_ref=rows_out.at[z, place.quarter(0), half, k],
                send_sem=s_send.at[r],
                recv_sem=s_recv.at[r],
                device_id=place.square(r),
                device_id_type=MESH,
            )
            for half in range(2)
            for k in range(PART)
        ]

    def swapped(r):
        ref = rows_out.at[z, place.quarter(r)]
        return pltpu.make_async_remote_copy(
            src_ref=ref,
            dst_ref=ref,
            send_sem=s_send.at[r],
            recv_sem=s_recv.at[r],
            device_id=place.square(r),
            device_id_type=MESH,
        )

    def pass_rows(r):
        swapped(r).wait_recv()
        gz[r].start()

    def line(n):
        at_line = y if n == 0 else x
        part = lambda at, half: keys_out.at[n, at_line, at, half]
        if n == 0:
            own = lambda half: [((k_ref, v_ref)[half].at[:, ours], part(x, half))]
        else:
            own = lambda half: [(part(y, half),) * 2]
        return Gather(place, "xy"[n], part, own, keys_out.at[n, 0, 0:3], cs.at[n, 0], cr.at[n, 0])

    def cross(n, step):
        at_line, spot = (y, x) if n == 0 else (x, y)
        spot = ring_at(spot, step)
        part = lambda at, half: keys_out.at[n, at, spot, half]
        if n == 0 and step == 0:
            own = lambda half: [((k_ref, v_ref)[half].at[:, ours], part(y, half))]
        else:
            own = lambda half: [(part(at_line, half),) * 2]
        k = 1 + step % RING
        return Gather(place, "yx"[n], part, own, keys_out.at[n, 0, 0:3], cs.at[n, k], cr.at[n, k])

    lines = [line(n) for n in range(2)]
    crosses = [[cross(n, step) for step in (0, -1, 1, 2)] for n in range(2)]

    def send_rows(r):
        for copy in row_swaps(r):
            copy.start()

    def start_cross(n, way):
        lines[n].arrived(way, 1)
        crosses[n][1 + way].start()

    def start_far(n):
        for way in range(2):
            lines[n].arrived(way, 2)
        crosses[n][3].start()

    def start_keys(n):
        lines[n].start()
        crosses[n][0].start()

    gz[0].start()
    send_rows(2)
    send_rows(1)
    start_keys(0)
    send_rows(3)
    for src, dst in rows_copies(0) + rows_copies(1):
        pltpu.make_async_copy(src, dst, local.at[0]).start()
    for n, source in enumerate((k_ref, v_ref)):
        pltpu.make_async_copy(source.at[:, ours], keys_out.at[0, y, x, n], local.at[1]).start()
    for copy in swaps:
        copy.wait_recv()
    start_keys(1)

    for copy in loads:
        copy.wait()
    for quarter in range(QUARTERS):
        for k in range(PART):
            cols = slice((quarter * PART + k) * D, (quarter * PART + k + 1) * D)
            product = g_vmem[:, cols].astype(F32) * o_vmem[:, cols].astype(F32)
            parts[quarter, :, k * B : (k + 1) * B] = jnp.sum(
                jnp.transpose(product), axis=0, keepdims=True
            )

    def delta_copy(r):
        return pltpu.make_async_remote_copy(
            src_ref=parts.at[place.quarter(r)],
            dst_ref=delta_ref.at[z, place.quarter(0)],
            send_sem=d_send.at[r],
            recv_sem=d_recv.at[r],
            device_id=place.square(r),
            device_id_type=MESH,
        )

    def swapped_delta(r):
        ref = delta_ref.at[z, place.quarter(r)]
        return pltpu.make_async_remote_copy(
            src_ref=ref,
            dst_ref=ref,
            send_sem=d_send.at[r],
            recv_sem=d_recv.at[r],
            device_id=place.square(r),
            device_id_type=MESH,
        )

    def delta_line(step, at):
        return pltpu.make_async_remote_copy(
            src_ref=delta_ref.at[at],
            dst_ref=delta_ref.at[at],
            send_sem=dz_send.at[step - 1],
            recv_sem=dz_recv.at[step - 1],
            device_id=place.along("z", step),
            device_id_type=MESH,
        )

    for r in (1, 2, 3):
        delta_copy(r).start()
    delta_ref[z, place.quarter(0)] = parts[place.quarter(0)]
    pass_rows(2)
    pass_rows(1)
    gz[0].forward()
    lines[0].forward()
    start_cross(0, 0)
    start_cross(0, 1)

    meta, mine, diagonal = tile_lists(place, qb, kb, kept)
    meta_ref[...] = meta
    code, count = early_tasks(mine, diagonal)
    sub = lax.broadcasted_iota(jnp.int32, (8, 128), 0)
    list_ref[...] = jnp.where(sub == 0, code, count).astype(jnp.int32)

    lines[1].forward()
    start_cross(1, 0)
    start_cross(1, 1)
    pass_rows(3)
    for n in range(2):
        crosses[n][0].forward()
    for n in range(2):
        start_far(n)
    gz[2].forward()
    gz[1].forward()
    for n in range(2):
        crosses[n][1].forward()
        crosses[n][2].forward()
    gz[3].forward()
    for n in range(2):
        crosses[n][3].forward()
    for r in (1, 2, 3):
        swapped_delta(r).wait_recv()
    for step in (1, 2, 3):
        delta_line(step, z).start()

    for n in range(2):
        for ring in crosses[n]:
            ring.finish()
    for ring in gz:
        ring.finish()
    for n, ref in enumerate((rows_out.at[z, place.quarter(0)], keys_out.at[0, y, x])):
        pltpu.make_async_copy(ref, ref, local.at[n]).wait()
    for copy in swaps:
        copy.wait_send()
    for r in (1, 2, 3):
        swapped(r).wait_send()
        swapped_delta(r).wait_send()
    for step in (1, 2, 3):
        delta_line(step, z).wait_send()
        delta_line(step, ring_at(z, -step)).wait_recv()
    for ring in gz + lines + crosses[0] + crosses[1]:
        ring.sent()


def in_hbm(*arrays):
    return [pltpu.with_memory_space_constraint(a, pltpu.HBM) for a in arrays]


def gather(qb, kb, kept, q, k, v, o, g):
    return pl.pallas_call(
        gather_kernel,
        out_shape=(
            pltpu.VMEM((RING, QUARTERS, 2, PART, B, D), BF),
            pltpu.VMEM((2, RING, RING, 2, B, D), BF),
            pltpu.VMEM((RING, QUARTERS, 1, COLS), F32),
            pltpu.VMEM((LOCAL_ROWS, 128), jnp.int32),
            pltpu.VMEM((8, 128), jnp.int32),
        ),
        in_specs=[HBM] * 8,
        out_specs=(ANY, ANY, VMEM, VMEM, VMEM),
        scratch_shapes=[
            pltpu.SMEM((64,), jnp.int32),
            pltpu.SMEM((128,), jnp.int32),
            pltpu.VMEM((64, 64), jnp.int32),
            pltpu.VMEM((B, HEADS * D), BF),
            pltpu.VMEM((B, HEADS * D), BF),
            pltpu.VMEM((QUARTERS, 1, COLS), F32),
            pltpu.SemaphoreType.DMA((5,)),
            pltpu.SemaphoreType.DMA((2,)),
            pltpu.SemaphoreType.DMA((2,)),
            pltpu.SemaphoreType.DMA((2,)),
            pltpu.SemaphoreType.DMA((QUARTERS,)),
            pltpu.SemaphoreType.DMA((QUARTERS,)),
            pltpu.SemaphoreType.DMA((QUARTERS,)),
            pltpu.SemaphoreType.DMA((QUARTERS,)),
            pltpu.SemaphoreType.DMA((3,)),
            pltpu.SemaphoreType.DMA((3,)),
            pltpu.SemaphoreType.DMA((QUARTERS,)),
            pltpu.SemaphoreType.DMA((QUARTERS, 6)),
            pltpu.SemaphoreType.DMA((2, 1 + RING)),
            pltpu.SemaphoreType.DMA((2, 1 + RING, 6)),
        ],
        compiler_params=pltpu.CompilerParams(
            collective_id=0, has_side_effects=True, vmem_limit_bytes=8 * 2**20
        ),
        name="gather",
    )(*in_hbm(qb, kb, kept, q, k, v, o, g))


def across(a, b):
    return lax.dot_general(a, b, (((1,), (1,)), ((), ())), preferred_element_type=F32)


def fill_bias(bias_ref):
    keys = lax.broadcasted_iota(jnp.int32, (B, COLS), 0)
    rows = lax.rem(lax.broadcasted_iota(jnp.int32, (B, COLS), 1), B)
    bias_ref[0] = jnp.full((B, COLS), MASKED, F32)
    bias_ref[1] = jnp.where(keys <= rows, 0.0, MASKED)
    bias_ref[2] = jnp.zeros((B, COLS), F32)


def pop(bits, diagonal):
    j = (31 - lax.clz(bits)) & 31
    kind = jnp.where(bits == 0, 0, jnp.where(j == diagonal, 1, 2))
    return j, bits & ~lax.shift_left(jnp.int32(1), j), kind


def list_tasks(meta_ref, task_ref):
    def row(i, count):
        diagonal = meta_ref[i, 1]

        def more(state):
            return state[0] != 0

        def step(state):
            bits, count = state
            j0, bits, kind0 = pop(bits, diagonal)
            j1, bits, kind1 = pop(bits, diagonal)
            task_ref[count] = i + j0 * 16 + j1 * 512 + kind0 * 16384 + kind1 * 65536
            return bits, count + 1

        return lax.while_loop(more, step, (meta_ref[i, 0], count))[1]

    count = lax.fori_loop(0, LOCAL_ROWS, row, jnp.int32(0))
    for n in range(GROUP - 1):
        task_ref[count + n] = 0
    task_ref[TASKS - 1] = (count + GROUP - 1) // GROUP


def read_task(task_ref, n):
    e = task_ref[n]
    return (
        e & 15,
        (e // 16) & 31,
        (e // 512) & 31,
        (e // 16384) & 3,
        (e // 65536) & 3,
    )


def take_tasks(meta_hbm, list_ref, task_ref, meta_ref, meta_sem):
    count = list_ref[1, 0]

    @pl.when(count <= EARLY)
    def _():
        for n in range(EARLY):
            task_ref[n] = list_ref[0, n]
        task_ref[TASKS - 1] = (count + GROUP - 1) // GROUP

    @pl.when(count > EARLY)
    def _():
        copy = pltpu.make_async_copy(meta_hbm, meta_ref, meta_sem)
        copy.start()
        copy.wait()
        list_tasks(meta_ref, task_ref)


def stats_kernel(
    meta_hbm, list_ref, rows_ref, keys_ref, st_ref, task_ref, meta_ref, meta_sem, m_ref, l_ref, bias_ref
):
    take_tasks(meta_hbm, list_ref, task_ref, meta_ref, meta_sem)
    fill_bias(bias_ref)
    m_ref[...] = jnp.full_like(m_ref, NEG)
    l_ref[...] = jnp.zeros_like(l_ref)

    def group(n, _):
        results = []
        for t in range(GROUP):
            i, j0, j1, kind0, kind1 = read_task(task_ref, GROUP * n + t)
            queries = rows_ref[i, 0].reshape(COLS, D)
            keys = jnp.concatenate([keys_ref[j0, 0], keys_ref[j1, 0]], axis=0)
            s = across(keys, queries) * C2
            s = jnp.concatenate([s[:B] + bias_ref[kind0], s[B:] + bias_ref[kind1]], axis=0)
            s = s.reshape(2 * B // 8, 8, COLS)
            m = jnp.max(s, axis=0)
            results.append((i, m, jnp.sum(jnp.exp2(s - m[None]), axis=0)))
        for i, m, l in results:
            old = m_ref[i]
            new = jnp.maximum(old, m)
            m_ref[i] = new
            l_ref[i] = l_ref[i] * jnp.exp2(old - new) + l * jnp.exp2(m - new)
        return 0

    lax.fori_loop(0, task_ref[TASKS - 1], group, 0)
    m8 = m_ref[...]
    m = jnp.max(m8, axis=1, keepdims=True)
    l = jnp.sum(l_ref[...] * jnp.exp2(m8 - m), axis=1, keepdims=True)
    st_ref[...] = jnp.where(l > 0.0, m + jnp.log2(l), NEG)


def statistics(meta, lists, rows, keys):
    return pl.pallas_call(
        stats_kernel,
        out_shape=pltpu.VMEM((LOCAL_ROWS, 1, COLS), F32),
        in_specs=[ANY, SMEM, VMEM, VMEM],
        out_specs=VMEM,
        scratch_shapes=[
            pltpu.SMEM((TASKS,), jnp.int32),
            pltpu.SMEM((LOCAL_ROWS, 128), jnp.int32),
            pltpu.SemaphoreType.DMA,
            pltpu.VMEM((LOCAL_ROWS, 8, COLS), F32),
            pltpu.VMEM((LOCAL_ROWS, 8, COLS), F32),
            pltpu.VMEM((3, B, COLS), F32),
        ],
        compiler_params=pltpu.CompilerParams(vmem_limit_bytes=24 * 2**20),
        name="statistics",
    )(meta, lists, rows, keys)


def exchange_kernel(st_ref, total_ref, sts, st_send, st_recv):
    place = Place()
    greet([place.along("z", step) for step in (1, 2, 3)])
    copies = [
        pltpu.make_async_remote_copy(
            src_ref=st_ref,
            dst_ref=sts.at[step - 1],
            send_sem=st_send.at[step - 1],
            recv_sem=st_recv.at[step - 1],
            device_id=place.along("z", step),
            device_id_type=MESH,
        )
        for step in (1, 2, 3)
    ]
    for copy in copies:
        copy.start()
    for copy in copies:
        copy.wait()
    logs = [st_ref[...]] + [sts[n] for n in range(3)]
    top = jnp.maximum(jnp.maximum(logs[0], logs[1]), jnp.maximum(logs[2], logs[3]))
    total_ref[...] = top + jnp.log2(sum(jnp.exp2(log - top) for log in logs))


def exchange(st):
    return pl.pallas_call(
        exchange_kernel,
        out_shape=pltpu.VMEM((LOCAL_ROWS, 1, COLS), F32),
        in_specs=[VMEM],
        out_specs=VMEM,
        scratch_shapes=[
            pltpu.VMEM((3, LOCAL_ROWS, 1, COLS), F32),
            pltpu.SemaphoreType.DMA((3,)),
            pltpu.SemaphoreType.DMA((3,)),
        ],
        compiler_params=pltpu.CompilerParams(
            collective_id=1, has_side_effects=True, vmem_limit_bytes=8 * 2**20
        ),
        name="exchange",
    )(st)


def grads_kernel(
    meta_hbm, list_ref, rows_ref, keys_ref, total_ref, delta_ref, dq_ref, dkv_ref,
    task_ref, meta_ref, meta_sem, dq_acc, dk_acc, dv_acc, bias_ref, p_ref, ds_ref,
):
    take_tasks(meta_hbm, list_ref, task_ref, meta_ref, meta_sem)
    fill_bias(bias_ref)
    dq_acc[...] = jnp.zeros_like(dq_acc)
    dk_acc[...] = jnp.zeros_like(dk_acc)
    dv_acc[...] = jnp.zeros_like(dv_acc)

    def group(n, _):
        tasks = [read_task(task_ref, GROUP * n + t) for t in range(GROUP)]
        for t, (i, j0, j1, kind0, kind1) in enumerate(tasks):
            keys = jnp.concatenate([keys_ref[j0, 0], keys_ref[j1, 0]], axis=0)
            values = jnp.concatenate([keys_ref[j0, 1], keys_ref[j1, 1]], axis=0)
            s = across(keys, rows_ref[i, 0].reshape(COLS, D)) * C2 - total_ref[i]
            s = jnp.concatenate([s[:B] + bias_ref[kind0], s[B:] + bias_ref[kind1]], axis=0)
            p = jnp.exp2(s)
            p_ref[t] = p.astype(BF)
            dp = across(values, rows_ref[i, 1].reshape(COLS, D))
            ds_ref[t] = (p * (dp - delta_ref[i])).astype(BF)
        for t, (i, j0, j1, _, _) in enumerate(tasks):
            keys = jnp.concatenate([keys_ref[j0, 0], keys_ref[j1, 0]], axis=0)
            ds = ds_ref[t]
            dv = jnp.dot(p_ref[t], rows_ref[i, 1].reshape(COLS, D), preferred_element_type=F32)
            dk = jnp.dot(ds, rows_ref[i, 0].reshape(COLS, D), preferred_element_type=F32)
            dq_acc[i] += jnp.dot(jnp.transpose(keys), ds, preferred_element_type=F32)
            dk_acc[j0] += dk[:B]
            dk_acc[j1] += dk[B:]
            dv_acc[j0] += dv[:B]
            dv_acc[j1] += dv[B:]
        return 0

    lax.fori_loop(0, task_ref[TASKS - 1], group, 0)

    def write(j, _):
        dkv_ref[j, 0] = (dk_acc[j] * SCALE).astype(BF)
        dkv_ref[j, 1] = dv_acc[j].astype(BF)
        return 0

    lax.fori_loop(0, LOCAL_KEYS, write, 0, unroll=8)

    def write_rows(i, _):
        for k in range(PART):
            dq_ref[i, k] = (dq_acc[i, :, k * B : (k + 1) * B] * SCALE).astype(BF)
        return 0

    lax.fori_loop(0, LOCAL_ROWS, write_rows, 0, unroll=8)


def grads(meta, lists, rows, keys, total, delta):
    return pl.pallas_call(
        grads_kernel,
        out_shape=(
            pltpu.VMEM((LOCAL_ROWS, PART, D, B), BF),
            pltpu.VMEM((LOCAL_KEYS, 2, B, D), BF),
        ),
        in_specs=[ANY, SMEM] + [VMEM] * 4,
        out_specs=(VMEM, VMEM),
        scratch_shapes=[
            pltpu.SMEM((TASKS,), jnp.int32),
            pltpu.SMEM((LOCAL_ROWS, 128), jnp.int32),
            pltpu.SemaphoreType.DMA,
            pltpu.VMEM((LOCAL_ROWS, D, COLS), F32),
            pltpu.VMEM((LOCAL_KEYS, B, D), F32),
            pltpu.VMEM((LOCAL_KEYS, B, D), F32),
            pltpu.VMEM((3, B, COLS), F32),
            pltpu.VMEM((GROUP, 2 * B, COLS), BF),
            pltpu.VMEM((GROUP, 2 * B, COLS), BF),
        ],
        compiler_params=pltpu.CompilerParams(vmem_limit_bytes=32 * 2**20),
        name="grads",
    )(meta, lists, rows, keys, total, delta)


class Scatter:
    def __init__(self, place, axis, part, near, far, mid, six, send, recv):
        self.me = getattr(place, axis)
        self.to = (place.along(axis, 1), place.along(axis, -1))
        self.part, self.near, self.far, self.mid, self.six = part, near, far, mid, six
        self.send, self.recv = send, recv

    def copy(self, src, dst, way, k):
        return pltpu.make_async_remote_copy(
            src_ref=src,
            dst_ref=dst,
            send_sem=self.send,
            recv_sem=self.recv.at[way * 3 + k],
            device_id=self.to[way],
            device_id_type=MESH,
        )

    def far_copy(self, way):
        return self.copy(self.part(ring_at(self.me, 2), way), self.far.at[way], way, 0)

    def plain_copy(self, way):
        step = 1 if way == 0 else -1
        return self.copy(
            self.part(ring_at(self.me, step), 1 - way), self.near.at[way, 1 - way], way, 1
        )

    def mid_copy(self, way):
        return self.copy(self.mid.at[way], self.near.at[way, way], way, 2)

    def start_far(self):
        for way in range(2):
            self.far_copy(way).start()

    def start_plain(self, way):
        self.plain_copy(way).start()

    def forward(self):
        for way in range(2):
            step = 1 if way == 0 else -1
            self.far_copy(way).wait_recv()
            own = self.part(ring_at(self.me, step), way)[...].astype(F32)
            self.mid[way] = (self.far[way].astype(F32) + own).astype(BF)
            self.mid_copy(way).start()

    def finish(self):
        for way in range(2):
            self.plain_copy(way).wait_recv()
        for way in range(2):
            self.mid_copy(way).wait_recv()

    def total(self, half, own=None):
        own = self.part(self.me, half)[...].astype(F32) if own is None else own
        return own + self.near[0, half].astype(F32) + self.near[1, half].astype(F32)

    def sent(self):
        self.copy(self.six, self.six, 0, 0).wait_send()


STEPS = (2, -1, 1, 0)
MEMBERS = (3, 2, 1, 0)
ORDER = (
    "c10P0", "c00F", "c01P1", "c10F", "r0F", "c12F", "r3P1", "r1P0", "c11F",
    "c01F", "r1P1", "r0P1", "r3F", "c00P0", "c11P0", "c10P1", "c00P1", "c03F",
    "c12P1", "c02F", "r0P0", "c00W", "c10W", "r3P0", "r2F", "c02P0", "c01P0",
    "c12P0", "c11P1", "c12W", "c13P1", "c11W", "r0W", "r2P0", "r1F", "r2P1",
    "c01W", "c10E", "l1F", "c13F", "r2W", "c02W", "c00E", "l0F", "c02P1",
    "c03W", "r0E", "c03P1", "r3W", "c01E", "l0P1", "c12E", "r1W", "l1P0",
    "c11E", "l1W", "c13W", "c13P0", "c02E", "l0P0", "c03P0", "l0W", "l1P1",
    "r1E", "r2E", "c13E", "l1E", "r3E", "c03E", "l0E",
)


def scatter_kernel(
    dq_ref, dkv_ref, qg_ref, kg_ref, vg_ref,
    zn, zf, zm, cn, cf, cm, ln, lf, lm, sums, own_sum, fin, qout,
    zs, zr, cs, cr, ls, lr, swap_send, swap_recv, q_send, q_recv, local,
):
    place = Place()
    h, x, y, z = place.h, place.x, place.y, place.z
    greet(place.around())

    def row_ring(k):
        number = place.quarter(MEMBERS[k])
        part = lambda at, half: dq_ref.at[at, number, half]
        return Scatter(place, "z", part, zn.at[k], zf.at[k], zm.at[k], dq_ref.at[0, 0:3], zs.at[k], zr.at[k])

    def cross(n, k):
        spot = ring_at((x, y)[n], STEPS[k])
        part = lambda at, half: dkv_ref.at[n, at, spot, half]
        return Scatter(
            place, "yx"[n], part, cn.at[n, k], cf.at[n, k], cm.at[n, k], dkv_ref.at[n, 0, 0:3],
            cs.at[n, k], cr.at[n, k],
        )

    def line(n):
        part = lambda at, half: sums.at[n, at, half]
        return Scatter(place, "xy"[n], part, ln.at[n], lf.at[n], lm.at[n], sums.at[n, 0:3], ls.at[n], lr.at[n])

    rows = [row_ring(k) for k in range(RING)]
    crosses = [[cross(n, k) for k in range(RING)] for n in range(2)]
    lines = [line(n) for n in range(2)]
    part_cols = pl.ds(pl.multiple_of(place.quarter(0) * COLS, COLS), COLS)

    def q_copy(k):
        r = MEMBERS[k]
        return pltpu.make_async_remote_copy(
            src_ref=qout.at[k],
            dst_ref=qg_ref.at[:, part_cols],
            send_sem=q_send.at[r],
            recv_sem=q_recv.at[r],
            device_id=place.square(r),
            device_id_type=MESH,
        )

    q_own = pltpu.make_async_copy(qout.at[RING - 1], qg_ref.at[:, part_cols], local.at[0])
    ours = pl.ds(pl.multiple_of(h * D, D), D)
    theirs = pl.ds(pl.multiple_of((1 - h) * D, D), D)
    swaps = [
        pltpu.make_async_remote_copy(
            src_ref=fin.at[1, n],
            dst_ref=target.at[:, ours],
            send_sem=swap_send.at[n],
            recv_sem=swap_recv.at[n],
            device_id=place.partner(),
            device_id_type=MESH,
        )
        for n, target in enumerate((kg_ref, vg_ref))
    ]
    outs = [
        pltpu.make_async_copy(fin.at[0, n], target.at[:, ours], local.at[1 + n])
        for n, target in enumerate((kg_ref, vg_ref))
    ]
    def end_rows(k):
        rows[k].finish()
        for half in range(PART):
            qout[k, :, half * D : (half + 1) * D] = jnp.transpose(rows[k].total(half)).astype(BF)
        if MEMBERS[k]:
            q_copy(k).start()
        else:
            q_own.start()

    def end_cross(n, k):
        ring = crosses[n][k]
        ring.finish()
        for half in range(2):
            total = ring.total(half)
            if STEPS[k] == 0:
                own_sum[n, half] = total
            else:
                sums[n, ring_at((x, y)[n], STEPS[k]), half] = total.astype(BF)

    def end_line(n):
        lines[n].finish()
        for half in range(2):
            fin[n, half] = lines[n].total(half, own_sum[n, half]).astype(BF)
        for copy in (outs, swaps)[n]:
            copy.start()

    for step in ORDER:
        at = [int(c) for c in step if c.isdigit()]
        kind, action = step[0], next(c for c in step if c in "FPWE")
        ring = {"r": lambda: rows[at[0]], "c": lambda: crosses[at[0]][at[1]], "l": lambda: lines[at[0]]}[kind]()
        if action == "F":
            ring.start_far()
        elif action == "P":
            ring.start_plain(at[-1])
        elif action == "W":
            ring.forward()
        else:
            {"r": end_rows, "c": end_cross, "l": end_line}[kind](*at)
    for copy in outs:
        copy.wait()
    q_own.wait()
    for n, target in enumerate((kg_ref, vg_ref)):
        swaps[n].wait_send()
        ref = target.at[:, theirs]
        pltpu.make_async_remote_copy(
            src_ref=ref,
            dst_ref=ref,
            send_sem=swap_send.at[n],
            recv_sem=swap_recv.at[n],
            device_id=place.partner(),
            device_id_type=MESH,
        ).wait_recv()
    for k in range(RING - 1):
        q_copy(k).wait_send()
        r = MEMBERS[k]
        ref = qg_ref.at[:, pl.ds(pl.multiple_of(place.quarter(r) * COLS, COLS), COLS)]
        pltpu.make_async_remote_copy(
            src_ref=ref,
            dst_ref=ref,
            send_sem=q_send.at[r],
            recv_sem=q_recv.at[r],
            device_id=place.square(r),
            device_id_type=MESH,
        ).wait_recv()
    for ring in rows + crosses[0] + crosses[1] + lines:
        ring.sent()


def scatter(dq, dkv):
    def ring_scratch(*rings):
        return [
            pltpu.VMEM(rings + (2, 2, B, D), BF),
            pltpu.VMEM(rings + (2, B, D), BF),
            pltpu.VMEM(rings + (2, B, D), BF),
        ]

    def ring_semaphores(*rings):
        return [pltpu.SemaphoreType.DMA(rings), pltpu.SemaphoreType.DMA(rings + (6,))]

    return pl.pallas_call(
        scatter_kernel,
        out_shape=(
            pltpu.VMEM((B, HEADS * D), BF),
            pltpu.VMEM((B, 2 * D), BF),
            pltpu.VMEM((B, 2 * D), BF),
        ),
        in_specs=[VMEM, VMEM],
        out_specs=(VMEM, VMEM, VMEM),
        scratch_shapes=ring_scratch(RING)
        + ring_scratch(2, RING)
        + ring_scratch(2)
        + [
            pltpu.VMEM((2, RING, 2, B, D), BF),
            pltpu.VMEM((2, 2, B, D), F32),
            pltpu.VMEM((2, 2, B, D), BF),
            pltpu.VMEM((QUARTERS, B, COLS), BF),
        ]
        + ring_semaphores(RING)
        + ring_semaphores(2, RING)
        + ring_semaphores(2)
        + [
            pltpu.SemaphoreType.DMA((2,)),
            pltpu.SemaphoreType.DMA((2,)),
            pltpu.SemaphoreType.DMA((QUARTERS,)),
            pltpu.SemaphoreType.DMA((QUARTERS,)),
            pltpu.SemaphoreType.DMA((3,)),
        ],
        compiler_params=pltpu.CompilerParams(
            collective_id=2, has_side_effects=True, vmem_limit_bytes=24 * 2**20
        ),
        name="scatter",
    )(dq.reshape(RING, QUARTERS, PART, D, B), dkv.reshape(2, RING, RING, 2, B, D))


def store_kernel(q_ref, k_ref, v_ref, qg_ref, kg_ref, vg_ref, sems):
    copies = [
        pltpu.make_async_copy(src, dst, sems.at[n])
        for n, (src, dst) in enumerate(((q_ref, qg_ref), (k_ref, kg_ref), (v_ref, vg_ref)))
    ]
    for copy in copies:
        copy.start()
    for copy in copies:
        copy.wait()


def store(*results):
    return pl.pallas_call(
        store_kernel,
        out_shape=tuple(pltpu.HBM(r.shape, r.dtype) for r in results),
        in_specs=[VMEM] * 3,
        out_specs=(HBM,) * 3,
        scratch_shapes=[pltpu.SemaphoreType.DMA((3,))],
        compiler_params=pltpu.CompilerParams(vmem_limit_bytes=4 * 2**20),
        name="store",
    )(*results)


def body(q, k, v, o, g, query_blocks, key_blocks, kept_blocks):
    rows, keys, delta, meta, lists = gather(query_blocks, key_blocks, kept_blocks, q, k, v, o, g)
    rows = rows.reshape(LOCAL_ROWS, 2, PART, B, D)
    keys = keys.reshape(LOCAL_KEYS, 2, B, D)
    total = exchange(statistics(meta, lists, rows, keys))
    dq, dkv = grads(meta, lists, rows, keys, total, delta.reshape(LOCAL_ROWS, 1, COLS))
    return store(*scatter(dq, dkv))


def solution(mesh):
    rows, stored = P(("inner", "outer"), "head"), P(("head", "inner", "outer"), None)
    return jax.shard_map(
        body,
        mesh=mesh,
        in_specs=(rows, stored, stored, rows, rows, P(), P(), P()),
        out_specs=(rows, stored, stored),
        check_vma=False,
    )
```

```python
import math

import jax
import jax.numpy as jnp
from jax import lax
from jax.experimental import pallas as pl
from jax.experimental.pallas import tpu as pltpu
from jax.sharding import PartitionSpec as P

HEADS = 8
D = 128
B = 128
RING = 4
QUARTERS = 4
PART = 2
COLS = PART * B
LOCAL_ROWS = 16
LOCAL_KEYS = 32
ENTRIES = 64
GROUP = 8
TASKS = 272
EARLY = 64
FIRST_KEY = 64
SCALE = 1.0 / math.sqrt(D)
LOG2E = math.log2(math.e)
C2 = SCALE * LOG2E
NEG = -1e30
MASKED = -2e30
MESH = pl.DeviceIdType.MESH
ANY = pl.BlockSpec(memory_space=pl.ANY)
HBM = pl.BlockSpec(memory_space=pltpu.HBM)
VMEM = pl.BlockSpec(memory_space=pltpu.VMEM)
SMEM = pl.BlockSpec(memory_space=pltpu.SMEM)
BF = jnp.bfloat16
F32 = jnp.float32


class Place:
    def __init__(self):
        self.h = lax.axis_index("head")
        inner, outer = lax.axis_index("inner"), lax.axis_index("outer")
        self.x, self.z = lax.rem(outer, 4), lax.rem(inner, 4)
        self.y = (inner // 4) * 2 + outer // 4

    def device(self, x=None, y=None, z=None, h=None):
        x, y, z, h = (
            own if new is None else new
            for own, new in ((self.x, x), (self.y, y), (self.z, z), (self.h, h))
        )
        return (h, (y // 2) * 4 + z, lax.rem(y, 2) * 4 + x)

    def along(self, axis, step):
        at = lax.rem(getattr(self, axis) + step + RING, RING)
        return self.device(**{axis: at})

    def partner(self):
        return self.device(h=1 - self.h)

    def quarter(self, r):
        b, a = lax.rem(self.y, 2), lax.rem(self.x, 2)
        b, a = (1 - b if r & 2 else b), (1 - a if r & 1 else a)
        return 2 * b + a

    def square(self, r):
        b, a = lax.rem(self.y, 2), lax.rem(self.x, 2)
        y = self.y + 1 - 2 * b if r & 2 else self.y
        x = self.x + 1 - 2 * a if r & 1 else self.x
        return self.device(x=x, y=y)

    def around(self):
        near = [self.along(a, s) for a in ("x", "y", "z") for s in (1, -1)]
        return near + [self.partner(), self.square(3)]


def ring_at(me, step):
    return lax.rem(me + step + RING, RING)


def greet(devices):
    barrier = pltpu.get_barrier_semaphore()
    for device in devices:
        pl.semaphore_signal(barrier, inc=1, device_id=device, device_id_type=MESH)
    pl.semaphore_wait(barrier, len(devices))


class Gather:
    def __init__(self, place, axis, part, own, six, send, recv):
        self.me = getattr(place, axis)
        self.to = (place.along(axis, 1), place.along(axis, -1))
        self.part, self.own, self.six, self.send, self.recv = part, own, six, send, recv

    def copy(self, src, dst, way, k):
        return pltpu.make_async_remote_copy(
            src_ref=src,
            dst_ref=dst,
            send_sem=self.send,
            recv_sem=self.recv.at[way * 3 + k],
            device_id=self.to[way],
            device_id_type=MESH,
        )

    def start(self):
        for k in range(2):
            for way in range(2):
                for src, dst in self.own(k ^ way):
                    self.copy(src, dst, way, k).start()

    def whole(self, at, half, way, k):
        ref = self.part(at, half)
        return self.copy(ref, ref, way, k)

    def arrived(self, way, k):
        step = (-1 if way == 0 else 1) * (2 if k == 2 else 1)
        half = way if k == 2 else k ^ way
        self.whole(ring_at(self.me, step), half, way, k).wait_recv()

    def forward(self):
        for way in range(2):
            self.arrived(way, 0)
            step = -1 if way == 0 else 1
            self.whole(ring_at(self.me, step), way, way, 2).start()

    def finish(self):
        for way in range(2):
            self.arrived(way, 1)
        for way in range(2):
            self.arrived(way, 2)

    def sent(self):
        self.copy(self.six, self.six, 0, 0).wait_send()


def key_slot(place, j):
    n, a, b = j // 16, lax.rem(j // 4, 4), lax.rem(j, 4)
    owner = jnp.where(n == 0, place.h, 1 - place.h)
    yy, xx = jnp.where(n == 0, a, b), jnp.where(n == 0, b, a)
    return owner * 64 + (yy // 2) * 32 + place.z * 8 + lax.rem(yy, 2) * 4 + xx


def row_slot(place, i):
    zz, b, a = i // 4, lax.rem(i // 2, 2), lax.rem(i, 2)
    return (place.y // 2) * 32 + zz * 8 + b * 4 + (place.x // 2) * 2 + a


def tile_lists(place, qb_ref, kb_ref, kept):
    lanes = lax.broadcasted_iota(jnp.int32, (1, 128), 1)
    subs = lax.broadcasted_iota(jnp.int32, (LOCAL_ROWS, 1), 0)

    def key_step(j, row):
        return jnp.where(lanes == j, kb_ref[key_slot(place, j)], row)

    def row_step(i, column):
        return jnp.where(subs == i, qb_ref[row_slot(place, i)], column)

    key_pos = lax.fori_loop(0, LOCAL_KEYS, key_step, jnp.full((1, 128), -7, jnp.int32))
    row_pos = lax.fori_loop(0, LOCAL_ROWS, row_step, jnp.zeros((LOCAL_ROWS, 1), jnp.int32))
    wide = lax.broadcasted_iota(jnp.int32, (64, 128), 1)
    listed = jnp.zeros((64, 128), F32)
    for e in range(ENTRIES):
        listed = jnp.where(kept[:, e : e + 1] == wide, 1.0, listed)
    rows_of = (row_pos == lax.broadcasted_iota(jnp.int32, (LOCAL_ROWS, 64), 1)).astype(F32)
    keys_of = (key_pos == lax.broadcasted_iota(jnp.int32, (128, 128), 0)).astype(F32)
    mine = jnp.dot(
        jnp.dot(rows_of.astype(BF), listed.astype(BF), preferred_element_type=F32).astype(BF),
        keys_of.astype(BF),
        preferred_element_type=F32,
    )
    lane16 = lax.broadcasted_iota(jnp.int32, (LOCAL_ROWS, 128), 1)
    weight = lax.shift_left(jnp.ones_like(lane16), lax.rem(lane16, 16)).astype(F32)
    low = jnp.sum(jnp.where(lane16 < 16, mine * weight, 0.0), axis=1, keepdims=True)
    high = jnp.sum(
        jnp.where((lane16 >= 16) & (lane16 < 32), mine * weight, 0.0), axis=1, keepdims=True
    )
    bits = low.astype(jnp.int32) + lax.shift_left(
        high.astype(jnp.int32), jnp.full((LOCAL_ROWS, 1), 16, jnp.int32)
    )
    on = (key_pos == row_pos + FIRST_KEY).astype(F32)
    diagonal = jnp.sum(on * (lane16 - 99).astype(F32), axis=1, keepdims=True) + 99.0
    meta = jnp.where(lane16 == 0, bits, diagonal.astype(jnp.int32))
    return meta, mine, diagonal


def halves_up(count):
    return lax.shift_right_logical(
        count.astype(jnp.int32) + 1, jnp.ones(count.shape, jnp.int32)
    ).astype(F32)


def exact(a, b, dims=(((1,), (0,)), ((), ()))):
    return lax.dot_general(a.astype(BF), b.astype(BF), dims, preferred_element_type=F32)


def early_tasks(mine, diagonal):
    sub = lax.broadcasted_iota(jnp.int32, (LOCAL_ROWS, 128), 0)
    lane = lax.broadcasted_iota(jnp.int32, (LOCAL_ROWS, 128), 1)
    count = jnp.broadcast_to(jnp.sum(mine, axis=1, keepdims=True), (LOCAL_ROWS, 128))
    tasks = halves_up(count)
    before = (
        lax.broadcasted_iota(jnp.int32, (LOCAL_ROWS, LOCAL_ROWS), 1)
        < lax.broadcasted_iota(jnp.int32, (LOCAL_ROWS, LOCAL_ROWS), 0)
    ).astype(F32)
    start = exact(before, tasks)
    at = lane.astype(F32)
    chosen = ((start <= at) & (at < start + tasks)).astype(F32)

    def of_row(column):
        return jnp.sum(chosen * column, axis=0, keepdims=True)

    row, first, diag = of_row(sub.astype(F32)), of_row(start), of_row(diagonal)
    lower = (
        lax.broadcasted_iota(jnp.int32, (128, 128), 0)
        < lax.broadcasted_iota(jnp.int32, (128, 128), 1)
    ).astype(F32)
    rank = exact(mine, lower)
    down = (((0,), (0,)), ((), ()))
    mine_t, rank_t = exact(mine, chosen, down), exact(rank, chosen, down)
    block = lax.broadcasted_iota(jnp.int32, (128, 128), 0).astype(F32)
    code = row
    for k in range(2):
        here = mine_t * (rank_t == 2.0 * (at[:1] - first) + k).astype(F32)
        j = jnp.sum(here * block, axis=0, keepdims=True)
        valid = jnp.sum(here, axis=0, keepdims=True)
        kind = valid * jnp.where(j == diag, 1.0, 2.0)
        code = code + j * (16.0, 512.0)[k] + kind * (16384.0, 65536.0)[k]
    return code, jnp.sum(tasks, axis=0, keepdims=True)


def gather_kernel(
    qb_hbm, kb_hbm, kept_hbm, q_ref, k_ref, v_ref, o_ref, g_ref,
    rows_out, keys_out, delta_ref, meta_ref, list_ref,
    qb, kb, kept, o_vmem, g_vmem, parts,
    load, local, swap_send, swap_recv, s_send, s_recv, d_send, d_recv, dz_send, dz_recv, zs, zr, cs, cr,
):
    place = Place()
    h, x, y, z = place.h, place.x, place.y, place.z
    pairs = ((o_ref, o_vmem), (g_ref, g_vmem), (kept_hbm, kept), (qb_hbm, qb), (kb_hbm, kb))
    loads = [pltpu.make_async_copy(src, dst, load.at[n]) for n, (src, dst) in enumerate(pairs)]
    for copy in loads:
        copy.start()
    greet(place.around() + [place.along("z", 2)])
    ours = pl.ds(pl.multiple_of(h * D, D), D)
    theirs = pl.ds(pl.multiple_of((1 - h) * D, D), D)

    swaps = [
        pltpu.make_async_remote_copy(
            src_ref=source.at[:, theirs],
            dst_ref=keys_out.at[1, x, y, n],
            send_sem=swap_send.at[n],
            recv_sem=swap_recv.at[n],
            device_id=place.partner(),
            device_id_type=MESH,
        )
        for n, source in enumerate((k_ref, v_ref))
    ]
    for copy in swaps:
        copy.start()

    def head(half, quarter, k):
        source = (q_ref, g_ref)[half]
        return source.at[:, pl.ds(pl.multiple_of((quarter * PART + k) * D, D), D)]

    def rows_copies(half):
        mine = place.quarter(0)
        return [(head(half, mine, k), rows_out.at[z, mine, half, k]) for k in range(PART)]

    def row_ring(r):
        part = lambda at, half: rows_out.at[at, place.quarter(r), half]
        own = rows_copies if r == 0 else lambda half: [(part(z, half),) * 2]
        return Gather(place, "z", part, own, rows_out.at[0, 0:3], zs.at[r], zr.at[r])

    gz = [row_ring(r) for r in range(QUARTERS)]

    def row_swaps(r):
        return [
            pltpu.make_async_remote_copy(
                src_ref=head(half, place.quarter(r), k),
                dst_ref=rows_out.at[z, place.quarter(0), half, k],
                send_sem=s_send.at[r],
                recv_sem=s_recv.at[r],
                device_id=place.square(r),
                device_id_type=MESH,
            )
            for half in range(2)
            for k in range(PART)
        ]

    def swapped(r):
        ref = rows_out.at[z, place.quarter(r)]
        return pltpu.make_async_remote_copy(
            src_ref=ref,
            dst_ref=ref,
            send_sem=s_send.at[r],
            recv_sem=s_recv.at[r],
            device_id=place.square(r),
            device_id_type=MESH,
        )

    def pass_rows(r):
        swapped(r).wait_recv()
        gz[r].start()

    def line(n):
        at_line = y if n == 0 else x
        part = lambda at, half: keys_out.at[n, at_line, at, half]
        if n == 0:
            own = lambda half: [((k_ref, v_ref)[half].at[:, ours], part(x, half))]
        else:
            own = lambda half: [(part(y, half),) * 2]
        return Gather(place, "xy"[n], part, own, keys_out.at[n, 0, 0:3], cs.at[n, 0], cr.at[n, 0])

    def cross(n, step):
        at_line, spot = (y, x) if n == 0 else (x, y)
        spot = ring_at(spot, step)
        part = lambda at, half: keys_out.at[n, at, spot, half]
        if n == 0 and step == 0:
            own = lambda half: [((k_ref, v_ref)[half].at[:, ours], part(y, half))]
        else:
            own = lambda half: [(part(at_line, half),) * 2]
        k = 1 + step % RING
        return Gather(place, "yx"[n], part, own, keys_out.at[n, 0, 0:3], cs.at[n, k], cr.at[n, k])

    lines = [line(n) for n in range(2)]
    crosses = [[cross(n, step) for step in (0, -1, 1, 2)] for n in range(2)]

    def send_rows(r):
        for copy in row_swaps(r):
            copy.start()

    def start_cross(n, way):
        lines[n].arrived(way, 1)
        crosses[n][1 + way].start()

    def start_far(n):
        for way in range(2):
            lines[n].arrived(way, 2)
        crosses[n][3].start()

    def start_keys(n):
        lines[n].start()
        crosses[n][0].start()

    gz[0].start()
    send_rows(2)
    send_rows(1)
    start_keys(0)
    send_rows(3)
    for src, dst in rows_copies(0) + rows_copies(1):
        pltpu.make_async_copy(src, dst, local.at[0]).start()
    for n, source in enumerate((k_ref, v_ref)):
        pltpu.make_async_copy(source.at[:, ours], keys_out.at[0, y, x, n], local.at[1]).start()
    for copy in swaps:
        copy.wait_recv()
    start_keys(1)

    for copy in loads:
        copy.wait()
    for quarter in range(QUARTERS):
        for k in range(PART):
            cols = slice((quarter * PART + k) * D, (quarter * PART + k + 1) * D)
            product = g_vmem[:, cols].astype(F32) * o_vmem[:, cols].astype(F32)
            parts[quarter, :, k * B : (k + 1) * B] = jnp.sum(
                jnp.transpose(product), axis=0, keepdims=True
            )

    def delta_copy(r):
        return pltpu.make_async_remote_copy(
            src_ref=parts.at[place.quarter(r)],
            dst_ref=delta_ref.at[z, place.quarter(0)],
            send_sem=d_send.at[r],
            recv_sem=d_recv.at[r],
            device_id=place.square(r),
            device_id_type=MESH,
        )

    def swapped_delta(r):
        ref = delta_ref.at[z, place.quarter(r)]
        return pltpu.make_async_remote_copy(
            src_ref=ref,
            dst_ref=ref,
            send_sem=d_send.at[r],
            recv_sem=d_recv.at[r],
            device_id=place.square(r),
            device_id_type=MESH,
        )

    def delta_line(step, at):
        return pltpu.make_async_remote_copy(
            src_ref=delta_ref.at[at],
            dst_ref=delta_ref.at[at],
            send_sem=dz_send.at[step - 1],
            recv_sem=dz_recv.at[step - 1],
            device_id=place.along("z", step),
            device_id_type=MESH,
        )

    for r in (1, 2, 3):
        delta_copy(r).start()
    delta_ref[z, place.quarter(0)] = parts[place.quarter(0)]
    pass_rows(2)
    pass_rows(1)
    gz[0].forward()
    lines[0].forward()
    start_cross(0, 0)
    start_cross(0, 1)

    meta, mine, diagonal = tile_lists(place, qb, kb, kept)
    meta_ref[...] = meta
    code, count = early_tasks(mine, diagonal)
    sub = lax.broadcasted_iota(jnp.int32, (8, 128), 0)
    list_ref[...] = jnp.where(sub == 0, code, count).astype(jnp.int32)

    lines[1].forward()
    start_cross(1, 0)
    start_cross(1, 1)
    pass_rows(3)
    for n in range(2):
        crosses[n][0].forward()
    for n in range(2):
        start_far(n)
    gz[2].forward()
    gz[1].forward()
    for n in range(2):
        crosses[n][1].forward()
        crosses[n][2].forward()
    gz[3].forward()
    for n in range(2):
        crosses[n][3].forward()
    for r in (1, 2, 3):
        swapped_delta(r).wait_recv()
    for step in (1, 2, 3):
        delta_line(step, z).start()

    for n in range(2):
        for ring in crosses[n]:
            ring.finish()
    for ring in gz:
        ring.finish()
    for n, ref in enumerate((rows_out.at[z, place.quarter(0)], keys_out.at[0, y, x])):
        pltpu.make_async_copy(ref, ref, local.at[n]).wait()
    for copy in swaps:
        copy.wait_send()
    for r in (1, 2, 3):
        swapped(r).wait_send()
        swapped_delta(r).wait_send()
    for step in (1, 2, 3):
        delta_line(step, z).wait_send()
        delta_line(step, ring_at(z, -step)).wait_recv()
    for ring in gz + lines + crosses[0] + crosses[1]:
        ring.sent()


def in_hbm(*arrays):
    return [pltpu.with_memory_space_constraint(a, pltpu.HBM) for a in arrays]


def gather(qb, kb, kept, q, k, v, o, g):
    return pl.pallas_call(
        gather_kernel,
        out_shape=(
            pltpu.VMEM((RING, QUARTERS, 2, PART, B, D), BF),
            pltpu.VMEM((2, RING, RING, 2, B, D), BF),
            pltpu.VMEM((RING, QUARTERS, 1, COLS), F32),
            pltpu.VMEM((LOCAL_ROWS, 128), jnp.int32),
            pltpu.VMEM((8, 128), jnp.int32),
        ),
        in_specs=[HBM] * 8,
        out_specs=(ANY, ANY, VMEM, VMEM, VMEM),
        scratch_shapes=[
            pltpu.SMEM((64,), jnp.int32),
            pltpu.SMEM((128,), jnp.int32),
            pltpu.VMEM((64, 64), jnp.int32),
            pltpu.VMEM((B, HEADS * D), BF),
            pltpu.VMEM((B, HEADS * D), BF),
            pltpu.VMEM((QUARTERS, 1, COLS), F32),
            pltpu.SemaphoreType.DMA((5,)),
            pltpu.SemaphoreType.DMA((2,)),
            pltpu.SemaphoreType.DMA((2,)),
            pltpu.SemaphoreType.DMA((2,)),
            pltpu.SemaphoreType.DMA((QUARTERS,)),
            pltpu.SemaphoreType.DMA((QUARTERS,)),
            pltpu.SemaphoreType.DMA((QUARTERS,)),
            pltpu.SemaphoreType.DMA((QUARTERS,)),
            pltpu.SemaphoreType.DMA((3,)),
            pltpu.SemaphoreType.DMA((3,)),
            pltpu.SemaphoreType.DMA((QUARTERS,)),
            pltpu.SemaphoreType.DMA((QUARTERS, 6)),
            pltpu.SemaphoreType.DMA((2, 1 + RING)),
            pltpu.SemaphoreType.DMA((2, 1 + RING, 6)),
        ],
        compiler_params=pltpu.CompilerParams(
            collective_id=0, has_side_effects=True, vmem_limit_bytes=8 * 2**20
        ),
        name="gather",
    )(*in_hbm(qb, kb, kept, q, k, v, o, g))


def across(a, b):
    return lax.dot_general(a, b, (((1,), (1,)), ((), ())), preferred_element_type=F32)


def fill_bias(bias_ref):
    keys = lax.broadcasted_iota(jnp.int32, (B, COLS), 0)
    rows = lax.rem(lax.broadcasted_iota(jnp.int32, (B, COLS), 1), B)
    bias_ref[0] = jnp.full((B, COLS), MASKED, F32)
    bias_ref[1] = jnp.where(keys <= rows, 0.0, MASKED)
    bias_ref[2] = jnp.zeros((B, COLS), F32)


def pop(bits, diagonal):
    j = (31 - lax.clz(bits)) & 31
    kind = jnp.where(bits == 0, 0, jnp.where(j == diagonal, 1, 2))
    return j, bits & ~lax.shift_left(jnp.int32(1), j), kind


def list_tasks(meta_ref, task_ref):
    def row(i, count):
        diagonal = meta_ref[i, 1]

        def more(state):
            return state[0] != 0

        def step(state):
            bits, count = state
            j0, bits, kind0 = pop(bits, diagonal)
            j1, bits, kind1 = pop(bits, diagonal)
            task_ref[count] = i + j0 * 16 + j1 * 512 + kind0 * 16384 + kind1 * 65536
            return bits, count + 1

        return lax.while_loop(more, step, (meta_ref[i, 0], count))[1]

    count = lax.fori_loop(0, LOCAL_ROWS, row, jnp.int32(0))
    for n in range(GROUP - 1):
        task_ref[count + n] = 0
    task_ref[TASKS - 1] = count


def read_task(task_ref, n):
    e = task_ref[n]
    return (
        e & 15,
        (e // 16) & 31,
        (e // 512) & 31,
        (e // 16384) & 3,
        (e // 65536) & 3,
    )


def take_tasks(meta_hbm, list_ref, task_ref, meta_ref, meta_sem):
    count = list_ref[1, 0]

    @pl.when(count <= EARLY)
    def _():
        for n in range(EARLY):
            task_ref[n] = list_ref[0, n]
        task_ref[TASKS - 1] = count

    @pl.when(count > EARLY)
    def _():
        copy = pltpu.make_async_copy(meta_hbm, meta_ref, meta_sem)
        copy.start()
        copy.wait()
        list_tasks(meta_ref, task_ref)


def in_groups(task_ref, work):
    count = task_ref[TASKS - 1]
    rest = lax.rem(count, GROUP)
    whole = count // GROUP + (rest > GROUP // 2).astype(jnp.int32)

    def group(n, _):
        work(GROUP * n, GROUP)
        return 0

    lax.fori_loop(0, whole, group, 0)

    @pl.when((rest > 0) & (rest <= GROUP // 2))
    def _():
        work(GROUP * whole, GROUP // 2)


def stats_kernel(
    meta_hbm, list_ref, rows_ref, keys_ref, st_ref, task_ref, meta_ref, meta_sem, m_ref, l_ref, bias_ref
):
    take_tasks(meta_hbm, list_ref, task_ref, meta_ref, meta_sem)
    fill_bias(bias_ref)
    m_ref[...] = jnp.full_like(m_ref, NEG)
    l_ref[...] = jnp.zeros_like(l_ref)

    def work(first, size):
        results = []
        for t in range(size):
            i, j0, j1, kind0, kind1 = read_task(task_ref, first + t)
            queries = rows_ref[i, 0].reshape(COLS, D)
            keys = jnp.concatenate([keys_ref[j0, 0], keys_ref[j1, 0]], axis=0)
            s = across(keys, queries) * C2
            s = jnp.concatenate([s[:B] + bias_ref[kind0], s[B:] + bias_ref[kind1]], axis=0)
            s = s.reshape(2 * B // 8, 8, COLS)
            m = jnp.max(s, axis=0)
            results.append((i, m, jnp.sum(jnp.exp2(s - m[None]), axis=0)))
        for i, m, l in results:
            old = m_ref[i]
            new = jnp.maximum(old, m)
            m_ref[i] = new
            l_ref[i] = l_ref[i] * jnp.exp2(old - new) + l * jnp.exp2(m - new)

    in_groups(task_ref, work)
    m8 = m_ref[...]
    m = jnp.max(m8, axis=1, keepdims=True)
    l = jnp.sum(l_ref[...] * jnp.exp2(m8 - m), axis=1, keepdims=True)
    st_ref[...] = jnp.where(l > 0.0, m + jnp.log2(l), NEG)


def statistics(meta, lists, rows, keys):
    return pl.pallas_call(
        stats_kernel,
        out_shape=pltpu.VMEM((LOCAL_ROWS, 1, COLS), F32),
        in_specs=[ANY, SMEM, VMEM, VMEM],
        out_specs=VMEM,
        scratch_shapes=[
            pltpu.SMEM((TASKS,), jnp.int32),
            pltpu.SMEM((LOCAL_ROWS, 128), jnp.int32),
            pltpu.SemaphoreType.DMA,
            pltpu.VMEM((LOCAL_ROWS, 8, COLS), F32),
            pltpu.VMEM((LOCAL_ROWS, 8, COLS), F32),
            pltpu.VMEM((3, B, COLS), F32),
        ],
        compiler_params=pltpu.CompilerParams(vmem_limit_bytes=24 * 2**20),
        name="statistics",
    )(meta, lists, rows, keys)


def exchange_kernel(st_ref, total_ref, sts, st_send, st_recv):
    place = Place()
    greet([place.along("z", step) for step in (1, 2, 3)])
    copies = [
        pltpu.make_async_remote_copy(
            src_ref=st_ref,
            dst_ref=sts.at[step - 1],
            send_sem=st_send.at[step - 1],
            recv_sem=st_recv.at[step - 1],
            device_id=place.along("z", step),
            device_id_type=MESH,
        )
        for step in (1, 2, 3)
    ]
    for copy in copies:
        copy.start()
    for copy in copies:
        copy.wait()
    logs = [st_ref[...]] + [sts[n] for n in range(3)]
    top = jnp.maximum(jnp.maximum(logs[0], logs[1]), jnp.maximum(logs[2], logs[3]))
    total_ref[...] = top + jnp.log2(sum(jnp.exp2(log - top) for log in logs))


def exchange(st):
    return pl.pallas_call(
        exchange_kernel,
        out_shape=pltpu.VMEM((LOCAL_ROWS, 1, COLS), F32),
        in_specs=[VMEM],
        out_specs=VMEM,
        scratch_shapes=[
            pltpu.VMEM((3, LOCAL_ROWS, 1, COLS), F32),
            pltpu.SemaphoreType.DMA((3,)),
            pltpu.SemaphoreType.DMA((3,)),
        ],
        compiler_params=pltpu.CompilerParams(
            collective_id=1, has_side_effects=True, vmem_limit_bytes=8 * 2**20
        ),
        name="exchange",
    )(st)


def grads_kernel(
    meta_hbm, list_ref, rows_ref, keys_ref, total_ref, delta_ref, dq_ref, dkv_ref,
    task_ref, meta_ref, meta_sem, dq_acc, dk_acc, dv_acc, bias_ref, p_ref, ds_ref,
):
    take_tasks(meta_hbm, list_ref, task_ref, meta_ref, meta_sem)
    fill_bias(bias_ref)
    dq_acc[...] = jnp.zeros_like(dq_acc)
    dk_acc[...] = jnp.zeros_like(dk_acc)
    dv_acc[...] = jnp.zeros_like(dv_acc)

    def work(first, size):
        tasks = [read_task(task_ref, first + t) for t in range(size)]
        for t, (i, j0, j1, kind0, kind1) in enumerate(tasks):
            keys = jnp.concatenate([keys_ref[j0, 0], keys_ref[j1, 0]], axis=0)
            values = jnp.concatenate([keys_ref[j0, 1], keys_ref[j1, 1]], axis=0)
            s = across(keys, rows_ref[i, 0].reshape(COLS, D)) * C2 - total_ref[i]
            s = jnp.concatenate([s[:B] + bias_ref[kind0], s[B:] + bias_ref[kind1]], axis=0)
            p = jnp.exp2(s)
            p_ref[t] = p.astype(BF)
            dp = across(values, rows_ref[i, 1].reshape(COLS, D))
            ds_ref[t] = (p * (dp - delta_ref[i])).astype(BF)
        for t, (i, j0, j1, _, _) in enumerate(tasks):
            keys = jnp.concatenate([keys_ref[j0, 0], keys_ref[j1, 0]], axis=0)
            ds = ds_ref[t]
            dv = jnp.dot(p_ref[t], rows_ref[i, 1].reshape(COLS, D), preferred_element_type=F32)
            dk = jnp.dot(ds, rows_ref[i, 0].reshape(COLS, D), preferred_element_type=F32)
            dq_acc[i] += jnp.dot(jnp.transpose(keys), ds, preferred_element_type=F32)
            dk_acc[j0] += dk[:B]
            dk_acc[j1] += dk[B:]
            dv_acc[j0] += dv[:B]
            dv_acc[j1] += dv[B:]

    in_groups(task_ref, work)

    def write(j, _):
        dkv_ref[j, 0] = (dk_acc[j] * SCALE).astype(BF)
        dkv_ref[j, 1] = dv_acc[j].astype(BF)
        return 0

    lax.fori_loop(0, LOCAL_KEYS, write, 0, unroll=8)

    def write_rows(i, _):
        for k in range(PART):
            dq_ref[i, k] = (dq_acc[i, :, k * B : (k + 1) * B] * SCALE).astype(BF)
        return 0

    lax.fori_loop(0, LOCAL_ROWS, write_rows, 0, unroll=8)


def grads(meta, lists, rows, keys, total, delta):
    return pl.pallas_call(
        grads_kernel,
        out_shape=(
            pltpu.VMEM((LOCAL_ROWS, PART, D, B), BF),
            pltpu.VMEM((LOCAL_KEYS, 2, B, D), BF),
        ),
        in_specs=[ANY, SMEM] + [VMEM] * 4,
        out_specs=(VMEM, VMEM),
        scratch_shapes=[
            pltpu.SMEM((TASKS,), jnp.int32),
            pltpu.SMEM((LOCAL_ROWS, 128), jnp.int32),
            pltpu.SemaphoreType.DMA,
            pltpu.VMEM((LOCAL_ROWS, D, COLS), F32),
            pltpu.VMEM((LOCAL_KEYS, B, D), F32),
            pltpu.VMEM((LOCAL_KEYS, B, D), F32),
            pltpu.VMEM((3, B, COLS), F32),
            pltpu.VMEM((GROUP, 2 * B, COLS), BF),
            pltpu.VMEM((GROUP, 2 * B, COLS), BF),
        ],
        compiler_params=pltpu.CompilerParams(vmem_limit_bytes=32 * 2**20),
        name="grads",
    )(meta, lists, rows, keys, total, delta)


class Scatter:
    def __init__(self, place, axis, part, near, far, mid, six, send, recv):
        self.me = getattr(place, axis)
        self.to = (place.along(axis, 1), place.along(axis, -1))
        self.part, self.near, self.far, self.mid, self.six = part, near, far, mid, six
        self.send, self.recv = send, recv

    def copy(self, src, dst, way, k):
        return pltpu.make_async_remote_copy(
            src_ref=src,
            dst_ref=dst,
            send_sem=self.send,
            recv_sem=self.recv.at[way * 3 + k],
            device_id=self.to[way],
            device_id_type=MESH,
        )

    def far_copy(self, way):
        return self.copy(self.part(ring_at(self.me, 2), way), self.far.at[way], way, 0)

    def plain_copy(self, way):
        step = 1 if way == 0 else -1
        return self.copy(
            self.part(ring_at(self.me, step), 1 - way), self.near.at[way, 1 - way], way, 1
        )

    def mid_copy(self, way):
        return self.copy(self.mid.at[way], self.near.at[way, way], way, 2)

    def start_far(self):
        for way in range(2):
            self.far_copy(way).start()

    def start_plain(self, way):
        self.plain_copy(way).start()

    def forward(self):
        for way in range(2):
            step = 1 if way == 0 else -1
            self.far_copy(way).wait_recv()
            own = self.part(ring_at(self.me, step), way)[...].astype(F32)
            self.mid[way] = (self.far[way].astype(F32) + own).astype(BF)
            self.mid_copy(way).start()

    def finish(self):
        for way in range(2):
            self.plain_copy(way).wait_recv()
        for way in range(2):
            self.mid_copy(way).wait_recv()

    def total(self, half, own=None):
        own = self.part(self.me, half)[...].astype(F32) if own is None else own
        return own + self.near[0, half].astype(F32) + self.near[1, half].astype(F32)

    def sent(self):
        self.copy(self.six, self.six, 0, 0).wait_send()


STEPS = (2, -1, 1, 0)
MEMBERS = (3, 2, 1, 0)
ORDER = (
    "c10P0", "c00F", "c01P1", "c10F", "r0F", "c12F", "r3P1", "r1P0", "c11F",
    "c01F", "r1P1", "r0P1", "r3F", "c00P0", "c11P0", "c10P1", "c00P1", "c03F",
    "c12P1", "c02F", "r0P0", "c00W", "c10W", "r3P0", "r2F", "c02P0", "c01P0",
    "c12P0", "c11P1", "c12W", "c13P1", "c11W", "r0W", "r2P0", "r1F", "r2P1",
    "c01W", "c10E", "l1F", "c13F", "r2W", "c02W", "c00E", "l0F", "c02P1",
    "c03W", "r0E", "c03P1", "r3W", "c01E", "l0P1", "c12E", "r1W", "l1P0",
    "c11E", "l1W", "c13W", "c13P0", "c02E", "l0P0", "c03P0", "l0W", "l1P1",
    "r1E", "r2E", "c13E", "l1E", "r3E", "c03E", "l0E",
)


def scatter_kernel(
    dq_ref, dkv_ref, qg_ref, kg_ref, vg_ref,
    zn, zf, zm, cn, cf, cm, ln, lf, lm, sums, own_sum, fin, qout,
    zs, zr, cs, cr, ls, lr, swap_send, swap_recv, q_send, q_recv, local,
):
    place = Place()
    h, x, y, z = place.h, place.x, place.y, place.z
    greet(place.around())

    def row_ring(k):
        number = place.quarter(MEMBERS[k])
        part = lambda at, half: dq_ref.at[at, number, half]
        return Scatter(place, "z", part, zn.at[k], zf.at[k], zm.at[k], dq_ref.at[0, 0:3], zs.at[k], zr.at[k])

    def cross(n, k):
        spot = ring_at((x, y)[n], STEPS[k])
        part = lambda at, half: dkv_ref.at[n, at, spot, half]
        return Scatter(
            place, "yx"[n], part, cn.at[n, k], cf.at[n, k], cm.at[n, k], dkv_ref.at[n, 0, 0:3],
            cs.at[n, k], cr.at[n, k],
        )

    def line(n):
        part = lambda at, half: sums.at[n, at, half]
        return Scatter(place, "xy"[n], part, ln.at[n], lf.at[n], lm.at[n], sums.at[n, 0:3], ls.at[n], lr.at[n])

    rows = [row_ring(k) for k in range(RING)]
    crosses = [[cross(n, k) for k in range(RING)] for n in range(2)]
    lines = [line(n) for n in range(2)]
    part_cols = pl.ds(pl.multiple_of(place.quarter(0) * COLS, COLS), COLS)

    def q_copy(k):
        r = MEMBERS[k]
        return pltpu.make_async_remote_copy(
            src_ref=qout.at[k],
            dst_ref=qg_ref.at[:, part_cols],
            send_sem=q_send.at[r],
            recv_sem=q_recv.at[r],
            device_id=place.square(r),
            device_id_type=MESH,
        )

    q_own = pltpu.make_async_copy(qout.at[RING - 1], qg_ref.at[:, part_cols], local.at[0])
    ours = pl.ds(pl.multiple_of(h * D, D), D)
    theirs = pl.ds(pl.multiple_of((1 - h) * D, D), D)
    swaps = [
        pltpu.make_async_remote_copy(
            src_ref=fin.at[1, n],
            dst_ref=target.at[:, ours],
            send_sem=swap_send.at[n],
            recv_sem=swap_recv.at[n],
            device_id=place.partner(),
            device_id_type=MESH,
        )
        for n, target in enumerate((kg_ref, vg_ref))
    ]
    outs = [
        pltpu.make_async_copy(fin.at[0, n], target.at[:, ours], local.at[1 + n])
        for n, target in enumerate((kg_ref, vg_ref))
    ]
    def end_rows(k):
        rows[k].finish()
        for half in range(PART):
            qout[k, :, half * D : (half + 1) * D] = jnp.transpose(rows[k].total(half)).astype(BF)
        if MEMBERS[k]:
            q_copy(k).start()
        else:
            q_own.start()

    def end_cross(n, k):
        ring = crosses[n][k]
        ring.finish()
        for half in range(2):
            total = ring.total(half)
            if STEPS[k] == 0:
                own_sum[n, half] = total
            else:
                sums[n, ring_at((x, y)[n], STEPS[k]), half] = total.astype(BF)

    def end_line(n):
        lines[n].finish()
        for half in range(2):
            fin[n, half] = lines[n].total(half, own_sum[n, half]).astype(BF)
        for copy in (outs, swaps)[n]:
            copy.start()

    for step in ORDER:
        at = [int(c) for c in step if c.isdigit()]
        kind, action = step[0], next(c for c in step if c in "FPWE")
        ring = {"r": lambda: rows[at[0]], "c": lambda: crosses[at[0]][at[1]], "l": lambda: lines[at[0]]}[kind]()
        if action == "F":
            ring.start_far()
        elif action == "P":
            ring.start_plain(at[-1])
        elif action == "W":
            ring.forward()
        else:
            {"r": end_rows, "c": end_cross, "l": end_line}[kind](*at)
    for copy in outs:
        copy.wait()
    q_own.wait()
    for n, target in enumerate((kg_ref, vg_ref)):
        swaps[n].wait_send()
        ref = target.at[:, theirs]
        pltpu.make_async_remote_copy(
            src_ref=ref,
            dst_ref=ref,
            send_sem=swap_send.at[n],
            recv_sem=swap_recv.at[n],
            device_id=place.partner(),
            device_id_type=MESH,
        ).wait_recv()
    for k in range(RING - 1):
        q_copy(k).wait_send()
        r = MEMBERS[k]
        ref = qg_ref.at[:, pl.ds(pl.multiple_of(place.quarter(r) * COLS, COLS), COLS)]
        pltpu.make_async_remote_copy(
            src_ref=ref,
            dst_ref=ref,
            send_sem=q_send.at[r],
            recv_sem=q_recv.at[r],
            device_id=place.square(r),
            device_id_type=MESH,
        ).wait_recv()
    for ring in rows + crosses[0] + crosses[1] + lines:
        ring.sent()


def scatter(dq, dkv):
    def ring_scratch(*rings):
        return [
            pltpu.VMEM(rings + (2, 2, B, D), BF),
            pltpu.VMEM(rings + (2, B, D), BF),
            pltpu.VMEM(rings + (2, B, D), BF),
        ]

    def ring_semaphores(*rings):
        return [pltpu.SemaphoreType.DMA(rings), pltpu.SemaphoreType.DMA(rings + (6,))]

    return pl.pallas_call(
        scatter_kernel,
        out_shape=(
            pltpu.VMEM((B, HEADS * D), BF),
            pltpu.VMEM((B, 2 * D), BF),
            pltpu.VMEM((B, 2 * D), BF),
        ),
        in_specs=[VMEM, VMEM],
        out_specs=(VMEM, VMEM, VMEM),
        scratch_shapes=ring_scratch(RING)
        + ring_scratch(2, RING)
        + ring_scratch(2)
        + [
            pltpu.VMEM((2, RING, 2, B, D), BF),
            pltpu.VMEM((2, 2, B, D), F32),
            pltpu.VMEM((2, 2, B, D), BF),
            pltpu.VMEM((QUARTERS, B, COLS), BF),
        ]
        + ring_semaphores(RING)
        + ring_semaphores(2, RING)
        + ring_semaphores(2)
        + [
            pltpu.SemaphoreType.DMA((2,)),
            pltpu.SemaphoreType.DMA((2,)),
            pltpu.SemaphoreType.DMA((QUARTERS,)),
            pltpu.SemaphoreType.DMA((QUARTERS,)),
            pltpu.SemaphoreType.DMA((3,)),
        ],
        compiler_params=pltpu.CompilerParams(
            collective_id=2, has_side_effects=True, vmem_limit_bytes=24 * 2**20
        ),
        name="scatter",
    )(dq.reshape(RING, QUARTERS, PART, D, B), dkv.reshape(2, RING, RING, 2, B, D))


def store_kernel(q_ref, k_ref, v_ref, qg_ref, kg_ref, vg_ref, sems):
    copies = [
        pltpu.make_async_copy(src, dst, sems.at[n])
        for n, (src, dst) in enumerate(((q_ref, qg_ref), (k_ref, kg_ref), (v_ref, vg_ref)))
    ]
    for copy in copies:
        copy.start()
    for copy in copies:
        copy.wait()


def store(*results):
    return pl.pallas_call(
        store_kernel,
        out_shape=tuple(pltpu.HBM(r.shape, r.dtype) for r in results),
        in_specs=[VMEM] * 3,
        out_specs=(HBM,) * 3,
        scratch_shapes=[pltpu.SemaphoreType.DMA((3,))],
        compiler_params=pltpu.CompilerParams(vmem_limit_bytes=4 * 2**20),
        name="store",
    )(*results)


def body(q, k, v, o, g, query_blocks, key_blocks, kept_blocks):
    rows, keys, delta, meta, lists = gather(query_blocks, key_blocks, kept_blocks, q, k, v, o, g)
    rows = rows.reshape(LOCAL_ROWS, 2, PART, B, D)
    keys = keys.reshape(LOCAL_KEYS, 2, B, D)
    total = exchange(statistics(meta, lists, rows, keys))
    dq, dkv = grads(meta, lists, rows, keys, total, delta.reshape(LOCAL_ROWS, 1, COLS))
    return store(*scatter(dq, dkv))


def solution(mesh):
    rows, stored = P(("inner", "outer"), "head"), P(("head", "inner", "outer"), None)
    return jax.shard_map(
        body,
        mesh=mesh,
        in_specs=(rows, stored, stored, rows, rows, P(), P(), P()),
        out_specs=(rows, stored, stored),
        check_vma=False,
    )
```

```python
import math

import jax
import jax.numpy as jnp
from jax import lax
from jax.experimental import pallas as pl
from jax.experimental.pallas import tpu as pltpu
from jax.sharding import PartitionSpec as P

HEADS = 8
D = 128
B = 128
RING = 4
QUARTERS = 4
PART = 2
COLS = PART * B
LOCAL_ROWS = 16
LOCAL_KEYS = 32
ENTRIES = 64
GROUP = 8
TASKS = 272
EARLY = 64
FIRST_KEY = 64
SCALE = 1.0 / math.sqrt(D)
LOG2E = math.log2(math.e)
C2 = SCALE * LOG2E
NEG = -1e30
MASKED = -2e30
MESH = pl.DeviceIdType.MESH
ANY = pl.BlockSpec(memory_space=pl.ANY)
HBM = pl.BlockSpec(memory_space=pltpu.HBM)
VMEM = pl.BlockSpec(memory_space=pltpu.VMEM)
SMEM = pl.BlockSpec(memory_space=pltpu.SMEM)
BF = jnp.bfloat16
F32 = jnp.float32


class Place:
    def __init__(self):
        self.h = lax.axis_index("head")
        inner, outer = lax.axis_index("inner"), lax.axis_index("outer")
        self.x, self.z = lax.rem(outer, 4), lax.rem(inner, 4)
        self.y = (inner // 4) * 2 + outer // 4

    def device(self, x=None, y=None, z=None, h=None):
        x, y, z, h = (
            own if new is None else new
            for own, new in ((self.x, x), (self.y, y), (self.z, z), (self.h, h))
        )
        return (h, (y // 2) * 4 + z, lax.rem(y, 2) * 4 + x)

    def along(self, axis, step):
        at = lax.rem(getattr(self, axis) + step + RING, RING)
        return self.device(**{axis: at})

    def partner(self):
        return self.device(h=1 - self.h)

    def quarter(self, r):
        b, a = lax.rem(self.y, 2), lax.rem(self.x, 2)
        b, a = (1 - b if r & 2 else b), (1 - a if r & 1 else a)
        return 2 * b + a

    def square(self, r):
        b, a = lax.rem(self.y, 2), lax.rem(self.x, 2)
        y = self.y + 1 - 2 * b if r & 2 else self.y
        x = self.x + 1 - 2 * a if r & 1 else self.x
        return self.device(x=x, y=y)

    def around(self):
        near = [self.along(a, s) for a in ("x", "y", "z") for s in (1, -1)]
        return near + [self.partner(), self.square(3)]


def ring_at(me, step):
    return lax.rem(me + step + RING, RING)


def greet(devices):
    barrier = pltpu.get_barrier_semaphore()
    for device in devices:
        pl.semaphore_signal(barrier, inc=1, device_id=device, device_id_type=MESH)
    pl.semaphore_wait(barrier, len(devices))


class Gather:
    def __init__(self, place, axis, part, own, six, send, recv):
        self.me = getattr(place, axis)
        self.to = (place.along(axis, 1), place.along(axis, -1))
        self.part, self.own, self.six, self.send, self.recv = part, own, six, send, recv

    def copy(self, src, dst, way, k):
        return pltpu.make_async_remote_copy(
            src_ref=src,
            dst_ref=dst,
            send_sem=self.send,
            recv_sem=self.recv.at[way * 3 + k],
            device_id=self.to[way],
            device_id_type=MESH,
        )

    def start(self):
        for k in range(2):
            for way in range(2):
                for src, dst in self.own(k ^ way):
                    self.copy(src, dst, way, k).start()

    def whole(self, at, half, way, k):
        ref = self.part(at, half)
        return self.copy(ref, ref, way, k)

    def arrived(self, way, k):
        step = (-1 if way == 0 else 1) * (2 if k == 2 else 1)
        half = way if k == 2 else k ^ way
        self.whole(ring_at(self.me, step), half, way, k).wait_recv()

    def forward(self):
        for way in range(2):
            self.arrived(way, 0)
            step = -1 if way == 0 else 1
            self.whole(ring_at(self.me, step), way, way, 2).start()

    def finish(self):
        for way in range(2):
            self.arrived(way, 1)
        for way in range(2):
            self.arrived(way, 2)

    def sent(self):
        self.copy(self.six, self.six, 0, 0).wait_send()


def key_slot(place, j):
    n, a, b = j // 16, lax.rem(j // 4, 4), lax.rem(j, 4)
    owner = jnp.where(n == 0, place.h, 1 - place.h)
    yy, xx = jnp.where(n == 0, a, b), jnp.where(n == 0, b, a)
    return owner * 64 + (yy // 2) * 32 + place.z * 8 + lax.rem(yy, 2) * 4 + xx


def row_slot(place, i):
    zz, b, a = i // 4, lax.rem(i // 2, 2), lax.rem(i, 2)
    return (place.y // 2) * 32 + zz * 8 + b * 4 + (place.x // 2) * 2 + a


def tile_lists(place, qb_ref, kb_ref, kept):
    lanes = lax.broadcasted_iota(jnp.int32, (1, 128), 1)
    subs = lax.broadcasted_iota(jnp.int32, (LOCAL_ROWS, 1), 0)

    def key_step(j, row):
        return jnp.where(lanes == j, kb_ref[key_slot(place, j)], row)

    def row_step(i, column):
        return jnp.where(subs == i, qb_ref[row_slot(place, i)], column)

    key_pos = lax.fori_loop(0, LOCAL_KEYS, key_step, jnp.full((1, 128), -7, jnp.int32))
    row_pos = lax.fori_loop(0, LOCAL_ROWS, row_step, jnp.zeros((LOCAL_ROWS, 1), jnp.int32))
    wide = lax.broadcasted_iota(jnp.int32, (64, 128), 1)
    listed = jnp.zeros((64, 128), F32)
    for e in range(ENTRIES):
        listed = jnp.where(kept[:, e : e + 1] == wide, 1.0, listed)
    rows_of = (row_pos == lax.broadcasted_iota(jnp.int32, (LOCAL_ROWS, 64), 1)).astype(F32)
    keys_of = (key_pos == lax.broadcasted_iota(jnp.int32, (128, 128), 0)).astype(F32)
    mine = jnp.dot(
        jnp.dot(rows_of.astype(BF), listed.astype(BF), preferred_element_type=F32).astype(BF),
        keys_of.astype(BF),
        preferred_element_type=F32,
    )
    lane16 = lax.broadcasted_iota(jnp.int32, (LOCAL_ROWS, 128), 1)
    weight = lax.shift_left(jnp.ones_like(lane16), lax.rem(lane16, 16)).astype(F32)
    low = jnp.sum(jnp.where(lane16 < 16, mine * weight, 0.0), axis=1, keepdims=True)
    high = jnp.sum(
        jnp.where((lane16 >= 16) & (lane16 < 32), mine * weight, 0.0), axis=1, keepdims=True
    )
    bits = low.astype(jnp.int32) + lax.shift_left(
        high.astype(jnp.int32), jnp.full((LOCAL_ROWS, 1), 16, jnp.int32)
    )
    on = (key_pos == row_pos + FIRST_KEY).astype(F32)
    diagonal = jnp.sum(on * (lane16 - 99).astype(F32), axis=1, keepdims=True) + 99.0
    meta = jnp.where(lane16 == 0, bits, diagonal.astype(jnp.int32))
    return meta, mine, diagonal


def halves_up(count):
    return lax.shift_right_logical(
        count.astype(jnp.int32) + 1, jnp.ones(count.shape, jnp.int32)
    ).astype(F32)


def exact(a, b, dims=(((1,), (0,)), ((), ()))):
    return lax.dot_general(a.astype(BF), b.astype(BF), dims, preferred_element_type=F32)


def early_tasks(mine, diagonal):
    sub = lax.broadcasted_iota(jnp.int32, (LOCAL_ROWS, 128), 0)
    lane = lax.broadcasted_iota(jnp.int32, (LOCAL_ROWS, 128), 1)
    count = jnp.broadcast_to(jnp.sum(mine, axis=1, keepdims=True), (LOCAL_ROWS, 128))
    tasks = halves_up(count)
    before = (
        lax.broadcasted_iota(jnp.int32, (LOCAL_ROWS, LOCAL_ROWS), 1)
        < lax.broadcasted_iota(jnp.int32, (LOCAL_ROWS, LOCAL_ROWS), 0)
    ).astype(F32)
    start = exact(before, tasks)
    at = lane.astype(F32)
    chosen = ((start <= at) & (at < start + tasks)).astype(F32)

    def of_row(column):
        return jnp.sum(chosen * column, axis=0, keepdims=True)

    row, first, diag = of_row(sub.astype(F32)), of_row(start), of_row(diagonal)
    lower = (
        lax.broadcasted_iota(jnp.int32, (128, 128), 0)
        < lax.broadcasted_iota(jnp.int32, (128, 128), 1)
    ).astype(F32)
    rank = exact(mine, lower)
    down = (((0,), (0,)), ((), ()))
    mine_t, rank_t = exact(mine, chosen, down), exact(rank, chosen, down)
    block = lax.broadcasted_iota(jnp.int32, (128, 128), 0).astype(F32)
    code = row
    for k in range(2):
        here = mine_t * (rank_t == 2.0 * (at[:1] - first) + k).astype(F32)
        j = jnp.sum(here * block, axis=0, keepdims=True)
        valid = jnp.sum(here, axis=0, keepdims=True)
        kind = valid * jnp.where(j == diag, 1.0, 2.0)
        code = code + j * (16.0, 512.0)[k] + kind * (16384.0, 65536.0)[k]
    return code, jnp.sum(tasks, axis=0, keepdims=True)


def gather_kernel(
    qb_hbm, kb_hbm, kept_hbm, q_ref, k_ref, v_ref, o_ref, g_ref,
    rows_out, keys_out, delta_ref, meta_ref, list_ref,
    qb, kb, kept, o_vmem, g_vmem, parts,
    load, local, swap_send, swap_recv, s_send, s_recv, d_send, d_recv, dz_send, dz_recv, zs, zr, cs, cr,
):
    place = Place()
    h, x, y, z = place.h, place.x, place.y, place.z
    pairs = ((o_ref, o_vmem), (g_ref, g_vmem), (kept_hbm, kept), (qb_hbm, qb), (kb_hbm, kb))
    loads = [pltpu.make_async_copy(src, dst, load.at[n]) for n, (src, dst) in enumerate(pairs)]
    for copy in loads:
        copy.start()
    greet(place.around() + [place.along("z", 2)])
    ours = pl.ds(pl.multiple_of(h * D, D), D)
    theirs = pl.ds(pl.multiple_of((1 - h) * D, D), D)

    swaps = [
        pltpu.make_async_remote_copy(
            src_ref=source.at[:, theirs],
            dst_ref=keys_out.at[1, x, y, n],
            send_sem=swap_send.at[n],
            recv_sem=swap_recv.at[n],
            device_id=place.partner(),
            device_id_type=MESH,
        )
        for n, source in enumerate((k_ref, v_ref))
    ]
    for copy in swaps:
        copy.start()

    def head(half, quarter, k):
        source = (q_ref, g_ref)[half]
        return source.at[:, pl.ds(pl.multiple_of((quarter * PART + k) * D, D), D)]

    def rows_copies(half):
        mine = place.quarter(0)
        return [(head(half, mine, k), rows_out.at[z, mine, half, k]) for k in range(PART)]

    def row_ring(r):
        part = lambda at, half: rows_out.at[at, place.quarter(r), half]
        own = rows_copies if r == 0 else lambda half: [(part(z, half),) * 2]
        return Gather(place, "z", part, own, rows_out.at[0, 0:3], zs.at[r], zr.at[r])

    gz = [row_ring(r) for r in range(QUARTERS)]

    def row_swaps(r):
        return [
            pltpu.make_async_remote_copy(
                src_ref=head(half, place.quarter(r), k),
                dst_ref=rows_out.at[z, place.quarter(0), half, k],
                send_sem=s_send.at[r],
                recv_sem=s_recv.at[r],
                device_id=place.square(r),
                device_id_type=MESH,
            )
            for half in range(2)
            for k in range(PART)
        ]

    def swapped(r):
        ref = rows_out.at[z, place.quarter(r)]
        return pltpu.make_async_remote_copy(
            src_ref=ref,
            dst_ref=ref,
            send_sem=s_send.at[r],
            recv_sem=s_recv.at[r],
            device_id=place.square(r),
            device_id_type=MESH,
        )

    def pass_rows(r):
        swapped(r).wait_recv()
        gz[r].start()

    def line(n):
        at_line = y if n == 0 else x
        part = lambda at, half: keys_out.at[n, at_line, at, half]
        if n == 0:
            own = lambda half: [((k_ref, v_ref)[half].at[:, ours], part(x, half))]
        else:
            own = lambda half: [(part(y, half),) * 2]
        return Gather(place, "xy"[n], part, own, keys_out.at[n, 0, 0:3], cs.at[n, 0], cr.at[n, 0])

    def cross(n, step):
        at_line, spot = (y, x) if n == 0 else (x, y)
        spot = ring_at(spot, step)
        part = lambda at, half: keys_out.at[n, at, spot, half]
        if n == 0 and step == 0:
            own = lambda half: [((k_ref, v_ref)[half].at[:, ours], part(y, half))]
        else:
            own = lambda half: [(part(at_line, half),) * 2]
        k = 1 + step % RING
        return Gather(place, "yx"[n], part, own, keys_out.at[n, 0, 0:3], cs.at[n, k], cr.at[n, k])

    lines = [line(n) for n in range(2)]
    crosses = [[cross(n, step) for step in (0, -1, 1, 2)] for n in range(2)]

    def send_rows(r):
        for copy in row_swaps(r):
            copy.start()

    def start_cross(n, way):
        lines[n].arrived(way, 1)
        crosses[n][1 + way].start()

    def start_far(n):
        for way in range(2):
            lines[n].arrived(way, 2)
        crosses[n][3].start()

    def start_keys(n):
        lines[n].start()
        crosses[n][0].start()

    gz[0].start()
    send_rows(2)
    send_rows(1)
    start_keys(0)
    send_rows(3)
    for src, dst in rows_copies(0) + rows_copies(1):
        pltpu.make_async_copy(src, dst, local.at[0]).start()
    for n, source in enumerate((k_ref, v_ref)):
        pltpu.make_async_copy(source.at[:, ours], keys_out.at[0, y, x, n], local.at[1]).start()
    for copy in swaps:
        copy.wait_recv()
    start_keys(1)

    for copy in loads:
        copy.wait()
    for quarter in range(QUARTERS):
        for k in range(PART):
            cols = slice((quarter * PART + k) * D, (quarter * PART + k + 1) * D)
            product = g_vmem[:, cols].astype(F32) * o_vmem[:, cols].astype(F32)
            parts[quarter, :, k * B : (k + 1) * B] = jnp.sum(
                jnp.transpose(product), axis=0, keepdims=True
            )

    def delta_copy(r):
        return pltpu.make_async_remote_copy(
            src_ref=parts.at[place.quarter(r)],
            dst_ref=delta_ref.at[z, place.quarter(0)],
            send_sem=d_send.at[r],
            recv_sem=d_recv.at[r],
            device_id=place.square(r),
            device_id_type=MESH,
        )

    def swapped_delta(r):
        ref = delta_ref.at[z, place.quarter(r)]
        return pltpu.make_async_remote_copy(
            src_ref=ref,
            dst_ref=ref,
            send_sem=d_send.at[r],
            recv_sem=d_recv.at[r],
            device_id=place.square(r),
            device_id_type=MESH,
        )

    def delta_line(step, at):
        return pltpu.make_async_remote_copy(
            src_ref=delta_ref.at[at],
            dst_ref=delta_ref.at[at],
            send_sem=dz_send.at[step - 1],
            recv_sem=dz_recv.at[step - 1],
            device_id=place.along("z", step),
            device_id_type=MESH,
        )

    for r in (1, 2, 3):
        delta_copy(r).start()
    delta_ref[z, place.quarter(0)] = parts[place.quarter(0)]
    pass_rows(2)
    pass_rows(1)
    gz[0].forward()
    lines[0].forward()
    start_cross(0, 0)
    start_cross(0, 1)

    meta, mine, diagonal = tile_lists(place, qb, kb, kept)
    meta_ref[...] = meta
    code, count = early_tasks(mine, diagonal)
    sub = lax.broadcasted_iota(jnp.int32, (8, 128), 0)
    list_ref[...] = jnp.where(sub == 0, code, count).astype(jnp.int32)

    lines[1].forward()
    start_cross(1, 0)
    start_cross(1, 1)
    pass_rows(3)
    for n in range(2):
        crosses[n][0].forward()
    for n in range(2):
        start_far(n)
    gz[2].forward()
    gz[1].forward()
    for n in range(2):
        crosses[n][1].forward()
        crosses[n][2].forward()
    gz[3].forward()
    for n in range(2):
        crosses[n][3].forward()
    for r in (1, 2, 3):
        swapped_delta(r).wait_recv()
    for step in (1, 2, 3):
        delta_line(step, z).start()

    for n in range(2):
        for ring in crosses[n]:
            ring.finish()
    for ring in gz:
        ring.finish()
    for n, ref in enumerate((rows_out.at[z, place.quarter(0)], keys_out.at[0, y, x])):
        pltpu.make_async_copy(ref, ref, local.at[n]).wait()
    for copy in swaps:
        copy.wait_send()
    for r in (1, 2, 3):
        swapped(r).wait_send()
        swapped_delta(r).wait_send()
    for step in (1, 2, 3):
        delta_line(step, z).wait_send()
        delta_line(step, ring_at(z, -step)).wait_recv()
    for ring in gz + lines + crosses[0] + crosses[1]:
        ring.sent()


def in_hbm(*arrays):
    return [pltpu.with_memory_space_constraint(a, pltpu.HBM) for a in arrays]


def gather(qb, kb, kept, q, k, v, o, g):
    return pl.pallas_call(
        gather_kernel,
        out_shape=(
            pltpu.VMEM((RING, QUARTERS, 2, PART, B, D), BF),
            pltpu.VMEM((2, RING, RING, 2, B, D), BF),
            pltpu.VMEM((RING, QUARTERS, 1, COLS), F32),
            pltpu.VMEM((LOCAL_ROWS, 128), jnp.int32),
            pltpu.VMEM((8, 128), jnp.int32),
        ),
        in_specs=[HBM] * 8,
        out_specs=(ANY, ANY, VMEM, VMEM, VMEM),
        scratch_shapes=[
            pltpu.SMEM((64,), jnp.int32),
            pltpu.SMEM((128,), jnp.int32),
            pltpu.VMEM((64, 64), jnp.int32),
            pltpu.VMEM((B, HEADS * D), BF),
            pltpu.VMEM((B, HEADS * D), BF),
            pltpu.VMEM((QUARTERS, 1, COLS), F32),
            pltpu.SemaphoreType.DMA((5,)),
            pltpu.SemaphoreType.DMA((2,)),
            pltpu.SemaphoreType.DMA((2,)),
            pltpu.SemaphoreType.DMA((2,)),
            pltpu.SemaphoreType.DMA((QUARTERS,)),
            pltpu.SemaphoreType.DMA((QUARTERS,)),
            pltpu.SemaphoreType.DMA((QUARTERS,)),
            pltpu.SemaphoreType.DMA((QUARTERS,)),
            pltpu.SemaphoreType.DMA((3,)),
            pltpu.SemaphoreType.DMA((3,)),
            pltpu.SemaphoreType.DMA((QUARTERS,)),
            pltpu.SemaphoreType.DMA((QUARTERS, 6)),
            pltpu.SemaphoreType.DMA((2, 1 + RING)),
            pltpu.SemaphoreType.DMA((2, 1 + RING, 6)),
        ],
        compiler_params=pltpu.CompilerParams(
            collective_id=0, has_side_effects=True, vmem_limit_bytes=8 * 2**20
        ),
        name="gather",
    )(*in_hbm(qb, kb, kept, q, k, v, o, g))


def across(a, b):
    return lax.dot_general(a, b, (((1,), (1,)), ((), ())), preferred_element_type=F32)


def fill_bias(bias_ref):
    keys = lax.broadcasted_iota(jnp.int32, (B, COLS), 0)
    rows = lax.rem(lax.broadcasted_iota(jnp.int32, (B, COLS), 1), B)
    bias_ref[0] = jnp.full((B, COLS), MASKED, F32)
    bias_ref[1] = jnp.where(keys <= rows, 0.0, MASKED)
    bias_ref[2] = jnp.zeros((B, COLS), F32)


def pop(bits, diagonal):
    j = (31 - lax.clz(bits)) & 31
    kind = jnp.where(bits == 0, 0, jnp.where(j == diagonal, 1, 2))
    return j, bits & ~lax.shift_left(jnp.int32(1), j), kind


def list_tasks(meta_ref, task_ref):
    def row(i, count):
        diagonal = meta_ref[i, 1]

        def more(state):
            return state[0] != 0

        def step(state):
            bits, count = state
            j0, bits, kind0 = pop(bits, diagonal)
            j1, bits, kind1 = pop(bits, diagonal)
            task_ref[count] = i + j0 * 16 + j1 * 512 + kind0 * 16384 + kind1 * 65536
            return bits, count + 1

        return lax.while_loop(more, step, (meta_ref[i, 0], count))[1]

    count = lax.fori_loop(0, LOCAL_ROWS, row, jnp.int32(0))
    for n in range(GROUP - 1):
        task_ref[count + n] = 0
    task_ref[TASKS - 1] = (count + GROUP - 1) // GROUP


def read_task(task_ref, n):
    e = task_ref[n]
    return (
        e & 15,
        (e // 16) & 31,
        (e // 512) & 31,
        (e // 16384) & 3,
        (e // 65536) & 3,
    )


def take_tasks(meta_hbm, list_ref, task_ref, meta_ref, meta_sem):
    count = list_ref[1, 0]

    @pl.when(count <= EARLY)
    def _():
        for n in range(EARLY):
            task_ref[n] = list_ref[0, n]
        task_ref[TASKS - 1] = (count + GROUP - 1) // GROUP

    @pl.when(count > EARLY)
    def _():
        copy = pltpu.make_async_copy(meta_hbm, meta_ref, meta_sem)
        copy.start()
        copy.wait()
        list_tasks(meta_ref, task_ref)


def stats_kernel(
    meta_hbm, list_ref, rows_ref, keys_ref, st_ref, task_ref, meta_ref, meta_sem, m_ref, l_ref, bias_ref
):
    take_tasks(meta_hbm, list_ref, task_ref, meta_ref, meta_sem)
    fill_bias(bias_ref)
    m_ref[...] = jnp.full_like(m_ref, NEG)
    l_ref[...] = jnp.zeros_like(l_ref)

    def group(n, _):
        results = []
        for t in range(GROUP):
            i, j0, j1, kind0, kind1 = read_task(task_ref, GROUP * n + t)
            queries = rows_ref[i, 0].reshape(COLS, D)
            keys = jnp.concatenate([keys_ref[j0, 0], keys_ref[j1, 0]], axis=0)
            s = across(keys, queries) * C2
            s = jnp.concatenate([s[:B] + bias_ref[kind0], s[B:] + bias_ref[kind1]], axis=0)
            s = s.reshape(2 * B // 8, 8, COLS)
            m = jnp.max(s, axis=0)
            results.append((i, m, jnp.sum(jnp.exp2(s - m[None]), axis=0)))
        for i, m, l in results:
            old = m_ref[i]
            new = jnp.maximum(old, m)
            m_ref[i] = new
            l_ref[i] = l_ref[i] * jnp.exp2(old - new) + l * jnp.exp2(m - new)
        return 0

    lax.fori_loop(0, task_ref[TASKS - 1], group, 0)
    m8 = m_ref[...]
    m = jnp.max(m8, axis=1, keepdims=True)
    l = jnp.sum(l_ref[...] * jnp.exp2(m8 - m), axis=1, keepdims=True)
    st_ref[...] = jnp.where(l > 0.0, m + jnp.log2(l), NEG)


def statistics(meta, lists, rows, keys):
    return pl.pallas_call(
        stats_kernel,
        out_shape=pltpu.VMEM((LOCAL_ROWS, 1, COLS), F32),
        in_specs=[ANY, SMEM, VMEM, VMEM],
        out_specs=VMEM,
        scratch_shapes=[
            pltpu.SMEM((TASKS,), jnp.int32),
            pltpu.SMEM((LOCAL_ROWS, 128), jnp.int32),
            pltpu.SemaphoreType.DMA,
            pltpu.VMEM((LOCAL_ROWS, 8, COLS), F32),
            pltpu.VMEM((LOCAL_ROWS, 8, COLS), F32),
            pltpu.VMEM((3, B, COLS), F32),
        ],
        compiler_params=pltpu.CompilerParams(vmem_limit_bytes=24 * 2**20),
        name="statistics",
    )(meta, lists, rows, keys)


def exchange_kernel(st_ref, total_ref, sts, st_send, st_recv):
    place = Place()
    greet([place.along("z", step) for step in (1, 2, 3)])
    copies = [
        pltpu.make_async_remote_copy(
            src_ref=st_ref,
            dst_ref=sts.at[step - 1],
            send_sem=st_send.at[step - 1],
            recv_sem=st_recv.at[step - 1],
            device_id=place.along("z", step),
            device_id_type=MESH,
        )
        for step in (1, 2, 3)
    ]
    for copy in copies:
        copy.start()
    for copy in copies:
        copy.wait()
    logs = [st_ref[...]] + [sts[n] for n in range(3)]
    top = jnp.maximum(jnp.maximum(logs[0], logs[1]), jnp.maximum(logs[2], logs[3]))
    total_ref[...] = top + jnp.log2(sum(jnp.exp2(log - top) for log in logs))


def exchange(st):
    return pl.pallas_call(
        exchange_kernel,
        out_shape=pltpu.VMEM((LOCAL_ROWS, 1, COLS), F32),
        in_specs=[VMEM],
        out_specs=VMEM,
        scratch_shapes=[
            pltpu.VMEM((3, LOCAL_ROWS, 1, COLS), F32),
            pltpu.SemaphoreType.DMA((3,)),
            pltpu.SemaphoreType.DMA((3,)),
        ],
        compiler_params=pltpu.CompilerParams(
            collective_id=1, has_side_effects=True, vmem_limit_bytes=8 * 2**20
        ),
        name="exchange",
    )(st)


def grads_kernel(
    meta_hbm, list_ref, rows_ref, keys_ref, total_ref, delta_ref, dq_ref, dkv_ref,
    task_ref, meta_ref, meta_sem, dq_acc, dk_acc, dv_acc, bias_ref, p_ref, ds_ref,
):
    take_tasks(meta_hbm, list_ref, task_ref, meta_ref, meta_sem)
    fill_bias(bias_ref)
    dq_acc[...] = jnp.zeros_like(dq_acc)
    dk_acc[...] = jnp.zeros_like(dk_acc)
    dv_acc[...] = jnp.zeros_like(dv_acc)

    def group(n, _):
        tasks = [read_task(task_ref, GROUP * n + t) for t in range(GROUP)]
        for t, (i, j0, j1, kind0, kind1) in enumerate(tasks):
            keys = jnp.concatenate([keys_ref[j0, 0], keys_ref[j1, 0]], axis=0)
            values = jnp.concatenate([keys_ref[j0, 1], keys_ref[j1, 1]], axis=0)
            s = across(keys, rows_ref[i, 0].reshape(COLS, D)) * C2 - total_ref[i]
            s = jnp.concatenate([s[:B] + bias_ref[kind0], s[B:] + bias_ref[kind1]], axis=0)
            p = jnp.exp2(s)
            p_ref[t] = p.astype(BF)
            dp = across(values, rows_ref[i, 1].reshape(COLS, D))
            ds_ref[t] = (p * (dp - delta_ref[i])).astype(BF)
        for t, (i, j0, j1, _, _) in enumerate(tasks):
            keys = jnp.concatenate([keys_ref[j0, 0], keys_ref[j1, 0]], axis=0)
            ds = ds_ref[t]
            dv = jnp.dot(p_ref[t], rows_ref[i, 1].reshape(COLS, D), preferred_element_type=F32)
            dk = jnp.dot(ds, rows_ref[i, 0].reshape(COLS, D), preferred_element_type=F32)
            dq_acc[i] += jnp.dot(jnp.transpose(keys), ds, preferred_element_type=F32)
            dk_acc[j0] += dk[:B]
            dk_acc[j1] += dk[B:]
            dv_acc[j0] += dv[:B]
            dv_acc[j1] += dv[B:]
        return 0

    lax.fori_loop(0, task_ref[TASKS - 1], group, 0)

    def write(j, _):
        dkv_ref[j, 0] = (dk_acc[j] * SCALE).astype(BF)
        dkv_ref[j, 1] = dv_acc[j].astype(BF)
        return 0

    lax.fori_loop(0, LOCAL_KEYS, write, 0, unroll=8)

    def write_rows(i, _):
        for k in range(PART):
            dq_ref[i, k] = (dq_acc[i, :, k * B : (k + 1) * B] * SCALE).astype(BF)
        return 0

    lax.fori_loop(0, LOCAL_ROWS, write_rows, 0, unroll=8)


def grads(meta, lists, rows, keys, total, delta):
    return pl.pallas_call(
        grads_kernel,
        out_shape=(
            pltpu.VMEM((LOCAL_ROWS, PART, D, B), BF),
            pltpu.VMEM((LOCAL_KEYS, 2, B, D), BF),
        ),
        in_specs=[ANY, SMEM] + [VMEM] * 4,
        out_specs=(VMEM, VMEM),
        scratch_shapes=[
            pltpu.SMEM((TASKS,), jnp.int32),
            pltpu.SMEM((LOCAL_ROWS, 128), jnp.int32),
            pltpu.SemaphoreType.DMA,
            pltpu.VMEM((LOCAL_ROWS, D, COLS), F32),
            pltpu.VMEM((LOCAL_KEYS, B, D), F32),
            pltpu.VMEM((LOCAL_KEYS, B, D), F32),
            pltpu.VMEM((3, B, COLS), F32),
            pltpu.VMEM((GROUP, 2 * B, COLS), BF),
            pltpu.VMEM((GROUP, 2 * B, COLS), BF),
        ],
        compiler_params=pltpu.CompilerParams(vmem_limit_bytes=32 * 2**20),
        name="grads",
    )(meta, lists, rows, keys, total, delta)


class Scatter:
    def __init__(self, place, axis, part, near, far, mid, six, send, recv):
        self.me = getattr(place, axis)
        self.to = (place.along(axis, 1), place.along(axis, -1))
        self.part, self.near, self.far, self.mid, self.six = part, near, far, mid, six
        self.send, self.recv = send, recv

    def copy(self, src, dst, way, k):
        return pltpu.make_async_remote_copy(
            src_ref=src,
            dst_ref=dst,
            send_sem=self.send,
            recv_sem=self.recv.at[2 * way + min(k, 1)],
            device_id=self.to[way],
            device_id_type=MESH,
        )

    def far_copy(self, way):
        return self.copy(self.part(ring_at(self.me, 2), way), self.far.at[way], way, 0)

    def plain_copy(self, way):
        step = 1 if way == 0 else -1
        return self.copy(
            self.part(ring_at(self.me, step), 1 - way), self.near.at[way, 1 - way], way, 1
        )

    def mid_copy(self, way):
        return self.copy(self.mid.at[way], self.near.at[way, way], way, 2)

    def start_far(self):
        for way in range(2):
            self.far_copy(way).start()

    def start_plain(self, way):
        self.plain_copy(way).start()

    def forward(self):
        for way in range(2):
            step = 1 if way == 0 else -1
            self.far_copy(way).wait_recv()
            own = self.part(ring_at(self.me, step), way)[...].astype(F32)
            self.mid[way] = (self.far[way].astype(F32) + own).astype(BF)
            self.mid_copy(way).start()

    def finish(self):
        for way in range(2):
            near = self.near.at[way]
            self.copy(near, near, way, 1).wait_recv()

    def total(self, half, own=None):
        own = self.part(self.me, half)[...].astype(F32) if own is None else own
        return own + self.near[0, half].astype(F32) + self.near[1, half].astype(F32)

    def sent(self):
        self.copy(self.six, self.six, 0, 0).wait_send()


STEPS = (2, -1, 1, 0)
MEMBERS = (3, 2, 1, 0)
ORDER = (
    "c10P0", "c00F", "c01P1", "c10F", "r0F", "c12F", "r3P1", "r1P0", "c11F",
    "c01F", "r1P1", "r0P1", "r3F", "c00P0", "c11P0", "c10P1", "c00P1", "c03F",
    "c12P1", "c02F", "r0P0", "c00W", "c10W", "r3P0", "r2F", "c02P0", "c01P0",
    "c12P0", "c11P1", "c12W", "c13P1", "c11W", "r0W", "r2P0", "r1F", "r2P1",
    "c01W", "c10E", "l1F", "c13F", "r2W", "c02W", "c00E", "l0F", "c02P1",
    "c03W", "r0E", "c03P1", "r3W", "c01E", "l0P1", "c12E", "r1W", "l1P0",
    "c11E", "l1W", "c13W", "c13P0", "c02E", "l0P0", "c03P0", "l0W", "l1P1",
    "r1E", "r2E", "c13E", "l1E", "r3E", "c03E", "l0E",
)


def scatter_kernel(
    dq_ref, dkv_ref, qg_ref, kg_ref, vg_ref,
    zn, zf, zm, cn, cf, cm, ln, lf, lm, sums, own_sum, fin, qout,
    zs, zr, cs, cr, ls, lr, swap_send, swap_recv, q_send, q_recv, local,
):
    place = Place()
    h, x, y, z = place.h, place.x, place.y, place.z
    greet(place.around())

    def row_ring(k):
        number = place.quarter(MEMBERS[k])
        part = lambda at, half: dq_ref.at[at, number, half]
        return Scatter(place, "z", part, zn.at[k], zf.at[k], zm.at[k], dq_ref.at[0, 0:3], zs.at[k], zr.at[k])

    def cross(n, k):
        spot = ring_at((x, y)[n], STEPS[k])
        part = lambda at, half: dkv_ref.at[n, at, spot, half]
        return Scatter(
            place, "yx"[n], part, cn.at[n, k], cf.at[n, k], cm.at[n, k], dkv_ref.at[n, 0, 0:3],
            cs.at[n, k], cr.at[n, k],
        )

    def line(n):
        part = lambda at, half: sums.at[n, at, half]
        return Scatter(place, "xy"[n], part, ln.at[n], lf.at[n], lm.at[n], sums.at[n, 0:3], ls.at[n], lr.at[n])

    rows = [row_ring(k) for k in range(RING)]
    crosses = [[cross(n, k) for k in range(RING)] for n in range(2)]
    lines = [line(n) for n in range(2)]
    part_cols = pl.ds(pl.multiple_of(place.quarter(0) * COLS, COLS), COLS)

    def q_copy(k):
        r = MEMBERS[k]
        return pltpu.make_async_remote_copy(
            src_ref=qout.at[k],
            dst_ref=qg_ref.at[:, part_cols],
            send_sem=q_send.at[r],
            recv_sem=q_recv.at[r],
            device_id=place.square(r),
            device_id_type=MESH,
        )

    q_own = pltpu.make_async_copy(qout.at[RING - 1], qg_ref.at[:, part_cols], local.at[0])
    ours = pl.ds(pl.multiple_of(h * D, D), D)
    theirs = pl.ds(pl.multiple_of((1 - h) * D, D), D)
    swaps = [
        pltpu.make_async_remote_copy(
            src_ref=fin.at[1, n],
            dst_ref=target.at[:, ours],
            send_sem=swap_send.at[n],
            recv_sem=swap_recv.at[n],
            device_id=place.partner(),
            device_id_type=MESH,
        )
        for n, target in enumerate((kg_ref, vg_ref))
    ]
    outs = [
        pltpu.make_async_copy(fin.at[0, n], target.at[:, ours], local.at[1 + n])
        for n, target in enumerate((kg_ref, vg_ref))
    ]
    def end_rows(k):
        rows[k].finish()
        for half in range(PART):
            qout[k, :, half * D : (half + 1) * D] = jnp.transpose(rows[k].total(half)).astype(BF)
        if MEMBERS[k]:
            q_copy(k).start()
        else:
            q_own.start()

    def end_cross(n, k):
        ring = crosses[n][k]
        ring.finish()
        for half in range(2):
            total = ring.total(half)
            if STEPS[k] == 0:
                own_sum[n, half] = total
            else:
                sums[n, ring_at((x, y)[n], STEPS[k]), half] = total.astype(BF)

    def end_line(n):
        lines[n].finish()
        for half in range(2):
            fin[n, half] = lines[n].total(half, own_sum[n, half]).astype(BF)
        for copy in (outs, swaps)[n]:
            copy.start()

    for step in ORDER:
        at = [int(c) for c in step if c.isdigit()]
        kind, action = step[0], next(c for c in step if c in "FPWE")
        ring = {"r": lambda: rows[at[0]], "c": lambda: crosses[at[0]][at[1]], "l": lambda: lines[at[0]]}[kind]()
        if action == "F":
            ring.start_far()
        elif action == "P":
            ring.start_plain(at[-1])
        elif action == "W":
            ring.forward()
        else:
            {"r": end_rows, "c": end_cross, "l": end_line}[kind](*at)
    for copy in outs:
        copy.wait()
    q_own.wait()
    for n, target in enumerate((kg_ref, vg_ref)):
        swaps[n].wait_send()
        ref = target.at[:, theirs]
        pltpu.make_async_remote_copy(
            src_ref=ref,
            dst_ref=ref,
            send_sem=swap_send.at[n],
            recv_sem=swap_recv.at[n],
            device_id=place.partner(),
            device_id_type=MESH,
        ).wait_recv()
    for k in range(RING - 1):
        q_copy(k).wait_send()
        r = MEMBERS[k]
        ref = qg_ref.at[:, pl.ds(pl.multiple_of(place.quarter(r) * COLS, COLS), COLS)]
        pltpu.make_async_remote_copy(
            src_ref=ref,
            dst_ref=ref,
            send_sem=q_send.at[r],
            recv_sem=q_recv.at[r],
            device_id=place.square(r),
            device_id_type=MESH,
        ).wait_recv()
    for ring in rows + crosses[0] + crosses[1] + lines:
        ring.sent()


def scatter(dq, dkv):
    def ring_scratch(*rings):
        return [
            pltpu.VMEM(rings + (2, 2, B, D), BF),
            pltpu.VMEM(rings + (2, B, D), BF),
            pltpu.VMEM(rings + (2, B, D), BF),
        ]

    def ring_semaphores(*rings):
        return [pltpu.SemaphoreType.DMA(rings), pltpu.SemaphoreType.DMA(rings + (4,))]

    return pl.pallas_call(
        scatter_kernel,
        out_shape=(
            pltpu.VMEM((B, HEADS * D), BF),
            pltpu.VMEM((B, 2 * D), BF),
            pltpu.VMEM((B, 2 * D), BF),
        ),
        in_specs=[VMEM, VMEM],
        out_specs=(VMEM, VMEM, VMEM),
        scratch_shapes=ring_scratch(RING)
        + ring_scratch(2, RING)
        + ring_scratch(2)
        + [
            pltpu.VMEM((2, RING, 2, B, D), BF),
            pltpu.VMEM((2, 2, B, D), F32),
            pltpu.VMEM((2, 2, B, D), BF),
            pltpu.VMEM((QUARTERS, B, COLS), BF),
        ]
        + ring_semaphores(RING)
        + ring_semaphores(2, RING)
        + ring_semaphores(2)
        + [
            pltpu.SemaphoreType.DMA((2,)),
            pltpu.SemaphoreType.DMA((2,)),
            pltpu.SemaphoreType.DMA((QUARTERS,)),
            pltpu.SemaphoreType.DMA((QUARTERS,)),
            pltpu.SemaphoreType.DMA((3,)),
        ],
        compiler_params=pltpu.CompilerParams(
            collective_id=2, has_side_effects=True, vmem_limit_bytes=24 * 2**20
        ),
        name="scatter",
    )(dq.reshape(RING, QUARTERS, PART, D, B), dkv.reshape(2, RING, RING, 2, B, D))


def store_kernel(q_ref, k_ref, v_ref, qg_ref, kg_ref, vg_ref, sems):
    copies = [
        pltpu.make_async_copy(src, dst, sems.at[n])
        for n, (src, dst) in enumerate(((q_ref, qg_ref), (k_ref, kg_ref), (v_ref, vg_ref)))
    ]
    for copy in copies:
        copy.start()
    for copy in copies:
        copy.wait()


def store(*results):
    return pl.pallas_call(
        store_kernel,
        out_shape=tuple(pltpu.HBM(r.shape, r.dtype) for r in results),
        in_specs=[VMEM] * 3,
        out_specs=(HBM,) * 3,
        scratch_shapes=[pltpu.SemaphoreType.DMA((3,))],
        compiler_params=pltpu.CompilerParams(vmem_limit_bytes=4 * 2**20),
        name="store",
    )(*results)


def body(q, k, v, o, g, query_blocks, key_blocks, kept_blocks):
    rows, keys, delta, meta, lists = gather(query_blocks, key_blocks, kept_blocks, q, k, v, o, g)
    rows = rows.reshape(LOCAL_ROWS, 2, PART, B, D)
    keys = keys.reshape(LOCAL_KEYS, 2, B, D)
    total = exchange(statistics(meta, lists, rows, keys))
    dq, dkv = grads(meta, lists, rows, keys, total, delta.reshape(LOCAL_ROWS, 1, COLS))
    return store(*scatter(dq, dkv))


def solution(mesh):
    rows, stored = P(("inner", "outer"), "head"), P(("head", "inner", "outer"), None)
    return jax.shard_map(
        body,
        mesh=mesh,
        in_specs=(rows, stored, stored, rows, rows, P(), P(), P()),
        out_specs=(rows, stored, stored),
        check_vma=False,
    )
```
